256 devices in a mesh: seq: 32 (over y, z), res: 8 (over x, core).
Axes of the slice: x: 4, y: 4, z: 8, core: 2. Of those that a mesh axis runs over, the one named last changes fastest.
Arguments:
- homolog_features: float32 [4096, 16384], P('seq', 'res')
- homolog_loss_slope: float32 [4096, 16384], P('seq', 'res'), may hold values from -6 to 6
- pair_update_gradient: float32 [256, 256, 128], P('res'), may hold values from -384 to 384
- alignment_mask: int32 [4096, 256], P('seq', 'res'), may hold values from 0 to 1, as said below
- asking_matrix: float32 [64, 64], replicated, may hold values from -0.75 to 0.75
- key_weight: float32 [64, 8], replicated
- content_matrix: float32 [64, 8], replicated, may hold values from -0.75 to 0.75
- sigmoid_filter_matrix: float32 [64, 64], replicated, may hold values from -0.75 to 0.75
- final_mixing_matrix: float32 [64, 64], replicated, may hold values from -0.75 to 0.75
- first_factor_matrix: float32 [64, 32], replicated, may hold values from -0.75 to 0.75
- second_factor_matrix: float32 [64, 32], replicated, may hold values from -0.75 to 0.75
- pair_weight: float32 [1024, 128], replicated, may hold values from -0.1875 to 0.1875
Outputs:
- input_grad_out: float32 [4096, 16384], P('seq', 'res')
The draws below stay inside these ranges and needn't reach their ends.
Inputs may be any that keep to these rules, and one draw needn't show every extreme that they name: `alignment_mask`: 1 marks a sequence present at a residue; sequence 0 is present at every residue.
All inputs are finite; a program needn't handle non-finite values.
Results may differ from the reference program's by a relative error of at most 0.0003.
Values sent between devices are 32-bit elements; how exact they have to be, the bound alone decides.
No kernel may reach another device: no remote copies, remote signals or barrier semaphores. Data moves between devices by JAX's collectives and lax.ppermute only.
A program may use at most 128 MiB of HBM per device.

```python
import jax
import jax.numpy as jnp
from jax import lax

FEATURE_DEPTH = 64
CZ = 128
HEAD_COUNT = 8
HEAD_SIZE = 8
FACTOR_WIDTH = 32
R_DEV = 32
HOMOLOG_COUNT = 4096
AMINO_COUNT = 256


def draw_homolog_features(key, part):
    key = jax.random.fold_in(key, 11)
    random_seed_perturb = jax.random.fold_in(key, 0)
    starting_point = jax.random.normal(random_seed_perturb, (HOMOLOG_COUNT, AMINO_COUNT * FEATURE_DEPTH), jnp.float32)
    return starting_point


def draw_key_weight(key, part):
    key = jax.random.fold_in(key, 12)
    starting_point = jax.random.normal(key, (FEATURE_DEPTH, HEAD_SIZE), jnp.float32) * FEATURE_DEPTH ** (-0.5)
    return starting_point


def draw_alignment_mask(key, part):
    key = jax.random.fold_in(key, 13)
    draws = jax.random.randint(key, (HOMOLOG_COUNT, AMINO_COUNT), 0, 1000, dtype=jnp.int32)
    seq_index = jnp.arange(HOMOLOG_COUNT, dtype=jnp.int32)
    limit = 900 - 600 * seq_index // HOMOLOG_COUNT
    present_mask = (draws < limit[:, None]).astype(jnp.int32)
    first_row = (seq_index == 0)[:, None]
    return jnp.where(first_row, 1, present_mask).astype(jnp.int32)


def shard_levels(own_key, dims, shards, low, high):
    factor_of, own = 1.0, jax.random.fold_in(own_key, 6)
    for position, blocks in shards:
        steps = jnp.exp(jax.random.uniform(jax.random.fold_in(own, position), (blocks,), jnp.float32, low / len(shards), high / len(shards)))
        factor_of = factor_of * jnp.repeat(steps, dims[position] // blocks).reshape([-1 if axis == position else 1 for axis in range(len(dims))])
    return factor_of


def bell_draw(stream_key, extent, width, reach, shards=(), kind=jnp.bfloat16):
    factor_of = shard_levels(stream_key, extent, shards, -0.22, 0.18) if shards else 1.0
    entries = jax.random.normal(stream_key, extent, jnp.float32) * width * factor_of
    return jnp.minimum(jnp.maximum(entries, -reach), reach).astype(kind)


def setup_inputs(seed: int = 0) -> dict:
    keys = jax.random.split(jax.random.key(seed), 13)
    homolog_features = draw_homolog_features(jax.random.fold_in(keys[12], 71), 0)
    homolog_loss_slope = bell_draw(keys[1], (HOMOLOG_COUNT, AMINO_COUNT * FEATURE_DEPTH), 1.0, 6.0, ((0, 32), (1, 8)), jnp.float32)
    pair_update_gradient = bell_draw(keys[2], (AMINO_COUNT, AMINO_COUNT, CZ), (HOMOLOG_COUNT // 64), 384.0, ((0, 8),), jnp.float32)
    alignment_mask = draw_alignment_mask(jax.random.fold_in(keys[12], 71), 0)
    asking_matrix = bell_draw(keys[4], (FEATURE_DEPTH, HEAD_COUNT * HEAD_SIZE), FEATURE_DEPTH ** -0.5, 0.75, (), jnp.float32)
    key_weight = draw_key_weight(jax.random.fold_in(keys[12], 71), 0)
    content_matrix = bell_draw(keys[6], (FEATURE_DEPTH, HEAD_SIZE), FEATURE_DEPTH ** -0.5, 0.75, (), jnp.float32)
    sigmoid_filter_matrix = bell_draw(keys[7], (FEATURE_DEPTH, HEAD_COUNT * HEAD_SIZE), FEATURE_DEPTH ** -0.5, 0.75, (), jnp.float32)
    final_mixing_matrix = bell_draw(keys[8], (HEAD_COUNT * HEAD_SIZE, FEATURE_DEPTH), (HEAD_COUNT * HEAD_SIZE) ** -0.5, 0.75, (), jnp.float32)
    first_factor_matrix = bell_draw(keys[9], (FEATURE_DEPTH, FACTOR_WIDTH), FEATURE_DEPTH ** -0.5, 0.75, (), jnp.float32)
    second_factor_matrix = bell_draw(keys[10], (FEATURE_DEPTH, FACTOR_WIDTH), FEATURE_DEPTH ** -0.5, 0.75, (), jnp.float32)
    pair_weight = bell_draw(keys[11], (FACTOR_WIDTH * FACTOR_WIDTH, CZ), (FACTOR_WIDTH * FACTOR_WIDTH) ** -0.5, 0.1875, (), jnp.float32)
    return {"homolog_features": homolog_features, "homolog_loss_slope": homolog_loss_slope, "pair_update_gradient": pair_update_gradient, "alignment_mask": alignment_mask, "asking_matrix": asking_matrix, "key_weight": key_weight, "content_matrix": content_matrix, "sigmoid_filter_matrix": sigmoid_filter_matrix, "final_mixing_matrix": final_mixing_matrix, "first_factor_matrix": first_factor_matrix, "second_factor_matrix": second_factor_matrix, "pair_weight": pair_weight}


EPSILON = 1e-05
MASK_FILL = -1000000000.0
PRECISE = lax.Precision.HIGHEST

def layer_normalize(values):
    center = values - lax.optimization_barrier(jnp.mean(values, axis=-1, keepdims=True))
    inverse_norm = lax.rsqrt(lax.optimization_barrier(jnp.mean(center * center, axis=-1, keepdims=True)) + EPSILON)
    return (center * inverse_norm, inverse_norm)

def norm_back(normed_input, inverse_norm, incoming_loss_slope):
    return inverse_norm * (incoming_loss_slope - lax.optimization_barrier(jnp.mean(incoming_loss_slope, axis=-1, keepdims=True)) - normed_input * lax.optimization_barrier(jnp.mean(incoming_loss_slope * normed_input, axis=-1, keepdims=True)))

def linear_project(values, weight):
    return jnp.einsum('...c,cd->...d', values, weight, precision=PRECISE)

def reference(homolog_features, homolog_loss_slope, pair_update_gradient, alignment_mask, asking_matrix, key_weight, content_matrix, sigmoid_filter_matrix, final_mixing_matrix, first_factor_matrix, second_factor_matrix, pair_weight):
    homolog_offset = homolog_features.reshape(HOMOLOG_COUNT, AMINO_COUNT, FEATURE_DEPTH)
    incoming_loss_slope = homolog_loss_slope.reshape(HOMOLOG_COUNT, AMINO_COUNT, FEATURE_DEPTH)
    present_mask = alignment_mask.astype(jnp.float32)
    normed_input, inverse_norm = layer_normalize(homolog_offset)
    col_count = lax.optimization_barrier(jnp.sum(present_mask, axis=0))
    query_mean = lax.optimization_barrier(jnp.sum(present_mask[:, :, None] * normed_input, axis=0)) / col_count[:, None]
    queries = (linear_project(query_mean, asking_matrix) * HEAD_SIZE ** (-0.5)).reshape(AMINO_COUNT, HEAD_COUNT, HEAD_SIZE)
    key_vecs = linear_project(normed_input, key_weight)
    values = linear_project(normed_input, content_matrix)
    scores = jnp.einsum('rhd,srd->srh', queries, key_vecs, precision=PRECISE)
    scores = jnp.where(present_mask[:, :, None] > 0, scores, MASK_FILL)
    score_top = lax.optimization_barrier(jnp.max(scores, axis=0))
    raw_weights = jnp.exp(scores - score_top[None])
    totals = lax.optimization_barrier(jnp.sum(raw_weights, axis=0))
    attn_probs = raw_weights / totals[None]
    attended_heads = jnp.einsum('srh,srd->rhd', attn_probs, values, precision=PRECISE)
    attended_output = attended_heads.reshape(AMINO_COUNT, HEAD_COUNT * HEAD_SIZE)
    gate_activation = jax.nn.sigmoid(linear_project(normed_input, sigmoid_filter_matrix))
    middle_output = homolog_offset + linear_project(gate_activation * attended_output[None], final_mixing_matrix)
    normed_mid, inverse_mid = layer_normalize(middle_output)
    left_act = present_mask[:, :, None] * linear_project(normed_mid, first_factor_matrix)
    right_act = present_mask[:, :, None] * linear_project(normed_mid, second_factor_matrix)
    pair_count = jnp.dot(present_mask.T, present_mask, precision=PRECISE)

    def opm_step(running, block_index):
        row_begin = (block_index * R_DEV).astype(jnp.int32)
        grad_rows = lax.dynamic_slice_in_dim(pair_update_gradient, row_begin, R_DEV, 0)
        count_rows = lax.dynamic_slice_in_dim(pair_count, row_begin, R_DEV, 0)
        left_rows = lax.dynamic_slice_in_dim(left_act, row_begin, R_DEV, 1)
        outer_grad = jnp.einsum('ijk,mk->ijm', grad_rows, pair_weight, precision=PRECISE) / count_rows[:, :, None]
        outer_grad = outer_grad.reshape(R_DEV, AMINO_COUNT, FACTOR_WIDTH, FACTOR_WIDTH)
        left_part = jnp.einsum('ijcf,sjf->sic', outer_grad, right_act, precision=PRECISE)
        running = running + jnp.einsum('ijcf,sic->sjf', outer_grad, left_rows, precision=PRECISE)
        return (running, left_part)
    right_grad, left_parts = lax.scan(opm_step, jnp.zeros((HOMOLOG_COUNT, AMINO_COUNT, FACTOR_WIDTH), jnp.float32), jnp.arange(AMINO_COUNT // R_DEV, dtype=jnp.int32))
    left_grad = jnp.transpose(left_parts, (1, 0, 2, 3)).reshape(HOMOLOG_COUNT, AMINO_COUNT, FACTOR_WIDTH)
    mid_in = linear_project(present_mask[:, :, None] * left_grad, first_factor_matrix.T) + linear_project(present_mask[:, :, None] * right_grad, second_factor_matrix.T)
    mid_grad = incoming_loss_slope + norm_back(normed_mid, inverse_mid, mid_in)
    out_grad = linear_project(mid_grad, final_mixing_matrix.T)
    gate_pre = out_grad * attended_output[None] * gate_activation * (1.0 - gate_activation)
    att_grad = lax.optimization_barrier(jnp.sum(out_grad * gate_activation, axis=0)).reshape(AMINO_COUNT, HEAD_COUNT, HEAD_SIZE)
    along = lax.optimization_barrier(jnp.sum(att_grad * attended_heads, axis=-1))
    score_grad = attn_probs * (jnp.einsum('rhd,srd->srh', att_grad, values, precision=PRECISE) - along[None])
    query_grad = jnp.einsum('srh,srd->rhd', score_grad, key_vecs, precision=PRECISE)
    key_grad = jnp.einsum('srh,rhd->srd', score_grad, queries, precision=PRECISE)
    value_grad = jnp.einsum('srh,rhd->srd', attn_probs, att_grad, precision=PRECISE)
    mean_grad = linear_project(query_grad.reshape(AMINO_COUNT, HEAD_COUNT * HEAD_SIZE) * HEAD_SIZE ** (-0.5), asking_matrix.T)
    x_grad = linear_project(gate_pre, sigmoid_filter_matrix.T) + linear_project(key_grad, key_weight.T) + linear_project(value_grad, content_matrix.T)
    x_grad = x_grad + present_mask[:, :, None] * mean_grad[None] / col_count[None, :, None]
    returned_tuple = mid_grad + norm_back(normed_input, inverse_norm, x_grad)
    return returned_tuple.reshape(HOMOLOG_COUNT, AMINO_COUNT * FEATURE_DEPTH)
```

```python
import math

import jax
import jax.numpy as jnp
from jax import lax
from jax.sharding import PartitionSpec as P

FEATURE_DEPTH = 64
HEAD_COUNT = 8
HEAD_SIZE = 8
FACTOR_WIDTH = 32


EPSILON = 1e-05
MASK_FILL = -1000000000.0
PRECISE = lax.Precision.HIGHEST


def layer_normalize(values):
    center = values - jnp.mean(values, axis=-1, keepdims=True)
    inverse_norm = lax.rsqrt(jnp.mean(center * center, axis=-1, keepdims=True) + EPSILON)
    return (center * inverse_norm, inverse_norm)


def norm_back(normed_input, inverse_norm, incoming_loss_slope):
    return inverse_norm * (
        incoming_loss_slope
        - jnp.mean(incoming_loss_slope, axis=-1, keepdims=True)
        - normed_input * jnp.mean(incoming_loss_slope * normed_input, axis=-1, keepdims=True)
    )


def linear_project(values, weight):
    return jnp.einsum("...c,cd->...d", values, weight, precision=PRECISE)


def weigh(weights, vectors):
    return jnp.einsum("srh,srd->rhd", weights, vectors, precision=PRECISE)


def share_all(values):
    devices = lax.axis_size("seq")
    copies = jnp.broadcast_to(values[None], (devices,) + values.shape)
    return lax.all_to_all(copies, "seq", 0, 0, tiled=True)


def sum_all(values):
    return jnp.sum(share_all(values), axis=0)


def body(
    homolog_features,
    homolog_loss_slope,
    pair_update_gradient,
    alignment_mask,
    asking_matrix,
    key_weight,
    content_matrix,
    sigmoid_filter_matrix,
    final_mixing_matrix,
    first_factor_matrix,
    second_factor_matrix,
    pair_weight,
):
    homolog_entries, amino_positions = alignment_mask.shape
    homolog_offset = homolog_features.reshape(homolog_entries, amino_positions, FEATURE_DEPTH)
    incoming_loss_slope = homolog_loss_slope.reshape(
        homolog_entries, amino_positions, FEATURE_DEPTH
    )
    present_mask = alignment_mask.astype(jnp.float32)
    normed_input, inverse_norm = layer_normalize(homolog_offset)
    sums = jnp.concatenate(
        [jnp.sum(present_mask[:, :, None] * normed_input, axis=0), jnp.sum(present_mask, axis=0)[:, None]],
        axis=1,
    )
    sums = sum_all(sums)
    query_sum, col_count = sums[:, :FEATURE_DEPTH], sums[:, FEATURE_DEPTH]
    queries = (
        linear_project(query_sum / col_count[:, None], asking_matrix) * HEAD_SIZE ** (-0.5)
    ).reshape(amino_positions, HEAD_COUNT, HEAD_SIZE)
    key_vecs = linear_project(normed_input, key_weight)
    values = linear_project(normed_input, content_matrix)
    scores = jnp.einsum("rhd,srd->srh", queries, key_vecs, precision=PRECISE)
    scores = jnp.where(present_mask[:, :, None] > 0, scores, MASK_FILL)
    local_top = jnp.max(scores, axis=0)
    raw_weights = jnp.exp(scores - local_top[None])
    packed = jnp.concatenate(
        [local_top[..., None], jnp.sum(raw_weights, axis=0)[..., None], weigh(raw_weights, values)], axis=-1
    )
    packed = share_all(packed.reshape(amino_positions, HEAD_COUNT * (HEAD_SIZE + 2)))
    packed = packed.reshape(-1, amino_positions, HEAD_COUNT, HEAD_SIZE + 2)
    score_top = jnp.max(packed[..., 0], axis=0)
    rescale = jnp.exp(packed[..., 0] - score_top[None])
    totals = jnp.sum(rescale * packed[..., 1], axis=0)
    weighted = jnp.sum(rescale[..., None] * packed[..., 2:], axis=0)
    attn_probs = raw_weights * (jnp.exp(local_top - score_top) / totals)[None]
    attended_heads = weighted / totals[..., None]
    attended_output = attended_heads.reshape(amino_positions, HEAD_COUNT * HEAD_SIZE)
    gate_activation = jax.nn.sigmoid(linear_project(normed_input, sigmoid_filter_matrix))
    middle_output = homolog_offset + linear_project(
        gate_activation * attended_output[None], final_mixing_matrix
    )
    normed_mid, inverse_mid = layer_normalize(middle_output)
    left_act = present_mask[:, :, None] * linear_project(normed_mid, first_factor_matrix)
    right_act = present_mask[:, :, None] * linear_project(normed_mid, second_factor_matrix)
    right_all, mask_all = (
        lax.all_gather(right_act, "res", axis=1, tiled=True),
        lax.all_gather(alignment_mask, "res", axis=1, tiled=True),
    )
    pair_part = jnp.dot(present_mask.T, mask_all.astype(jnp.float32), precision=PRECISE)
    devices = lax.axis_size("seq")
    pair_slices = lax.all_to_all(pair_part.reshape(devices, -1), "seq", 0, 0, tiled=True)
    pair_count = share_all(jnp.sum(pair_slices, axis=0)).reshape(pair_part.shape)
    full_cols = right_all.shape[1]
    block_rows = math.gcd(amino_positions, 8)
    blocks = amino_positions // block_rows

    def opm_step(running, block_index):
        row_begin = block_index * block_rows
        grad_rows = lax.dynamic_slice_in_dim(pair_update_gradient, row_begin, block_rows, 0)
        count_rows = lax.dynamic_slice_in_dim(pair_count, row_begin, block_rows, 0)
        left_rows = lax.dynamic_slice_in_dim(left_act, row_begin, block_rows, 1)
        outer_grad = (
            jnp.einsum("ijk,mk->ijm", grad_rows, pair_weight, precision=PRECISE)
            / count_rows[:, :, None]
        )
        outer_grad = outer_grad.reshape(block_rows, full_cols, FACTOR_WIDTH, FACTOR_WIDTH)
        left_part = jnp.einsum("ijcf,sjf->sic", outer_grad, right_all, precision=PRECISE)
        running = running + jnp.einsum("ijcf,sic->sjf", outer_grad, left_rows, precision=PRECISE)
        return (running, left_part)

    right_terms, left_parts = lax.scan(
        opm_step,
        jnp.zeros((homolog_entries, full_cols, FACTOR_WIDTH), jnp.float32),
        jnp.arange(blocks, dtype=jnp.int32),
    )
    left_grad = jnp.transpose(left_parts, (1, 0, 2, 3)).reshape(
        homolog_entries, amino_positions, FACTOR_WIDTH
    )
    right_grad = lax.psum_scatter(right_terms, "res", scatter_dimension=1, tiled=True)
    mid_in = linear_project(
        present_mask[:, :, None] * left_grad, first_factor_matrix.T
    ) + linear_project(present_mask[:, :, None] * right_grad, second_factor_matrix.T)
    mid_grad = incoming_loss_slope + norm_back(normed_mid, inverse_mid, mid_in)
    out_grad = linear_project(mid_grad, final_mixing_matrix.T)
    gate_pre = out_grad * attended_output[None] * gate_activation * (1.0 - gate_activation)
    att_grad = sum_all(jnp.sum(out_grad * gate_activation, axis=0)).reshape(
        amino_positions, HEAD_COUNT, HEAD_SIZE
    )
    along = jnp.sum(att_grad * attended_heads, axis=-1)
    score_grad = attn_probs * (
        jnp.einsum("rhd,srd->srh", att_grad, values, precision=PRECISE) - along[None]
    )
    query_grad = sum_all(
        jnp.einsum("srh,srd->rhd", score_grad, key_vecs, precision=PRECISE).reshape(
            amino_positions, HEAD_COUNT * HEAD_SIZE
        )
    )
    key_grad = jnp.einsum("srh,rhd->srd", score_grad, queries, precision=PRECISE)
    value_grad = jnp.einsum("srh,rhd->srd", attn_probs, att_grad, precision=PRECISE)
    mean_grad = linear_project(
        query_grad.reshape(amino_positions, HEAD_COUNT * HEAD_SIZE) * HEAD_SIZE ** (-0.5),
        asking_matrix.T,
    )
    x_grad = (
        linear_project(gate_pre, sigmoid_filter_matrix.T)
        + linear_project(key_grad, key_weight.T)
        + linear_project(value_grad, content_matrix.T)
    )
    x_grad = x_grad + present_mask[:, :, None] * mean_grad[None] / col_count[None, :, None]
    returned_tuple = mid_grad + norm_back(normed_input, inverse_norm, x_grad)
    return returned_tuple.reshape(homolog_entries, amino_positions * FEATURE_DEPTH)


def solution(mesh):
    in_specs = (
        P("seq", "res"),
        P("seq", "res"),
        P("res", None, None),
        P("seq", "res"),
        P(),
        P(),
        P(),
        P(),
        P(),
        P(),
        P(),
        P(),
    )
    out_specs = P("seq", "res")
    return jax.shard_map(body, mesh=mesh, in_specs=in_specs, out_specs=out_specs, check_vma=False)
```

```python
import jax
import jax.numpy as jnp
from jax import lax
from jax.experimental import pallas as pl
from jax.experimental.pallas import tpu as pltpu
from jax.sharding import Mesh
from jax.sharding import PartitionSpec as P

FEATURE_DEPTH = 64
HEAD_COUNT = 8
HEAD_SIZE = 8
FACTOR_WIDTH = 32
RES = 32
SEQ = 128

EPSILON = 1e-05
MASK_FILL = -1000000000.0
PRECISE = lax.Precision.HIGHEST
F32 = jnp.float32


def split(values):
    high = values.astype(jnp.bfloat16)
    low = (values - high.astype(jnp.float32)).astype(jnp.bfloat16)
    return high, low


def dot_nn(a, b):
    return lax.dot_general(a, b, (((1,), (0,)), ((), ())), preferred_element_type=jnp.float32)


def dot_nt(a, b):
    return lax.dot_general(a, b, (((1,), (1,)), ((), ())), preferred_element_type=jnp.float32)


def exact_nn(a, b):
    return lax.dot_general(a, b, (((1,), (0,)), ((), ())), preferred_element_type=F32, precision=PRECISE)


def exact_nt(a, b):
    return lax.dot_general(a, b, (((1,), (1,)), ((), ())), preferred_element_type=F32, precision=PRECISE)


def lhs_parts(weight):
    high, low = split(weight)
    return jnp.concatenate([high, high, low], axis=1)


def project(parts, values):
    high, low = split(values)
    return dot_nn(parts, jnp.concatenate([high, low, high], axis=0))


def row_lane(shape):
    return lax.broadcasted_iota(jnp.int32, shape, 0), lax.broadcasted_iota(jnp.int32, shape, 1)


def sum_lanes_01(ones, values):
    high, rest = values.astype(jnp.bfloat16), values
    rest = rest - high.astype(F32)
    mid = rest.astype(jnp.bfloat16)
    low = (rest - mid.astype(F32)).astype(jnp.bfloat16)
    return dot_nt(ones, high) + dot_nt(ones, mid) + dot_nt(ones, low)


def own_blocks(values):
    rows, _ = row_lane((RES, 128))
    total = jnp.zeros((RES, 128), F32)
    for pair in range(RES // 2):
        total = jnp.where(rows // 2 == pair, values[:, 128 * pair : 128 * pair + 128], total)
    return jnp.where(rows[:, :64] % 2 == 0, total[:, :64], total[:, 64:])


def pack(values):
    return jnp.concatenate([values[:16], values[16:]], axis=1)


def unpack(values):
    return jnp.concatenate([values[:, :64], values[:, 64:]], axis=0)


def over_heads(values):
    return jnp.broadcast_to(values[:, None, :], (RES, 8, values.shape[1])).reshape(RES * 8, values.shape[1])


def head_column(values):
    rows, lanes = row_lane((RES * 8, values.shape[1]))
    return jnp.sum(jnp.where(rows % 8 == lanes, over_heads(values), 0.0), axis=1, keepdims=True)


def head_blocks(values):
    rows, lanes = row_lane((RES * 8, 64))
    picked = jnp.where(rows % 8 == lanes // 8, over_heads(values), 0.0)
    r, c = row_lane((64, RES * 8))
    spread = exact_nn(picked, (r % 8 == c % 8).astype(F32))
    rows, lanes = row_lane((RES * 8, RES * 8))
    return jnp.where(rows // 8 == lanes // 8, spread, 0.0)


def fold_blocks(values):
    rows, lanes = row_lane((RES * 8, RES * 8))
    r, c = row_lane((RES * 8, 128))
    fold = jnp.where((r % 8 == c % 8) & (c < 64), 1.0, 0.0)
    return exact_nn(jnp.where(rows // 8 == lanes // 8, values, 0.0), fold)


def sum_heads(values):
    return jnp.sum(values.reshape(RES, 8, values.shape[1]), axis=1)


def send_all(send, rows, values):
    send[:, rows, :] = jnp.broadcast_to(values[None], (send.shape[0],) + values.shape)


def norm_kernel(m0, mask, m0t, x0t, inverse, present, send):
    shown = mask[...].astype(F32).T
    present[...] = shown
    for pair in range(RES // 2):
        block = m0[:, 128 * pair : 128 * pair + 128].T
        m0t[128 * pair : 128 * pair + 128] = block
        for k in range(2):
            part = block[64 * k : 64 * k + 64]
            center = part - jnp.mean(part, axis=0, keepdims=True)
            scale = lax.rsqrt(jnp.mean(center * center, axis=0, keepdims=True) + EPSILON)
            row = 2 * pair + k
            inverse[row : row + 1] = scale
            x0t[64 * row : 64 * row + 64] = center * scale
    ones = shown.astype(jnp.bfloat16)
    sums = own_blocks(sum_lanes_01(ones, x0t[...]))
    counts = dot_nt(jnp.ones((16, SEQ), jnp.bfloat16), ones)
    send[...] = jnp.zeros_like(send)
    send_all(send, slice(0, 16), pack(sums))
    send_all(send, slice(16, 17), jnp.concatenate([counts[0:1], jnp.zeros((1, 96), F32)], axis=1))


def pair_kernel(sent, mask, mask_core, mask_1, mask_2, mask_3, send):
    send[...] = sent[...]
    own = mask[...].astype(F32).T.astype(jnp.bfloat16)
    rows = jnp.concatenate([own, mask_core[...].astype(F32).T.astype(jnp.bfloat16)], axis=0)
    columns = jnp.concatenate(
        [own] + [part[...].astype(F32).T.astype(jnp.bfloat16) for part in (mask_1, mask_2, mask_3)], axis=0
    )
    count = dot_nt(rows, columns)
    share = 64 // send.shape[0]
    for peer in range(send.shape[0]):
        send[peer, 17 : 17 + share, :] = count[share * peer : share * peer + share]


def project_kernel(x0t, slope, key, value_gate, keys, values, gate, slope_t):
    parts = lhs_parts(value_gate[...])
    for pair in range(RES // 2):
        slope_t[128 * pair : 128 * pair + 128] = slope[:, 128 * pair : 128 * pair + 128].T
        row = 128 * pair
        both = jnp.concatenate([x0t[row : row + 64], x0t[row + 64 : row + 128]], axis=1)
        found = project(parts, both)
        key_rows = exact_nn(key[...], both)
        gates = jax.nn.sigmoid(found[8:72])
        for k in range(2):
            lanes = slice(SEQ * k, SEQ * k + SEQ)
            head = 8 * (2 * pair + k)
            keys[head : head + 8] = key_rows[:, lanes]
            values[head : head + 8] = found[0:8, lanes]
            gate[row + 64 * k : row + 64 * k + 64] = gates[:, lanes]


def score_kernel(got, keys, values, present, asking, weights, local, counts, query_blocks, send):
    sums = jnp.sum(got[...], axis=0)
    r, c = row_lane((RES, RES))
    count = jnp.sum(jnp.where(r == c, jnp.broadcast_to(sums[16:17, :RES], (RES, RES)), 0.0), axis=1, keepdims=True)
    counts[...] = jnp.broadcast_to(count, (RES, 128))
    queries = exact_nn(unpack(sums[:16]) / count, asking[...]) * HEAD_SIZE ** (-0.5)
    blocks = head_blocks(queries)
    query_blocks[...] = blocks
    scores = exact_nn(blocks, keys[...])
    scores = jnp.where(over_heads(present[...]) > 0, scores, MASK_FILL)
    top = jnp.max(scores, axis=1, keepdims=True)
    raw = jnp.exp(scores - top)
    weights[...] = raw
    total = jnp.sum(raw, axis=1, keepdims=True)
    folded = fold_blocks(exact_nt(raw, values[...]))
    rows, lanes = row_lane((RES * 8, 128))
    head = rows % 8
    packed = jnp.where(lanes < 64, jnp.where(lanes // 8 == head, folded, 0.0), 0.0)
    packed = jnp.where(lanes == 64 + head, top, packed)
    packed = jnp.where(lanes == 72 + head, total, packed)
    packed = sum_heads(packed)
    local[...] = packed
    send_all(send, slice(0, 32), packed)
    share = 64 // send.shape[0]
    send[:, 32:, :] = jnp.zeros((send.shape[0], send.shape[1] - 32, 128), F32)
    send_all(send, slice(32, 32 + share), sums[17 : 17 + share])


def attend_kernel(
    got, local, raw, m0t, gate, present, mixing, factors,
    probs, attended, mixed, x1t, inverse_mid, left, right, inverse_count, scratch,
):
    peers = got.shape[0]
    share = 64 // peers
    for peer in range(peers):
        inverse_count[share * peer : share * peer + share] = 1.0 / got[peer, 32 : 32 + share, :]
    parts = got[:, 0:32, :]
    top = jnp.max(parts, axis=0)
    lane = lax.broadcasted_iota(jnp.int32, (peers, RES, 128), 2)
    factor = jnp.where((lane >= 64) & (lane < 72), jnp.exp(parts - top[None]), 0.0)
    r, c = row_lane((128, 128))
    expand = ((c < 64) & (r == 64 + c // 8)) | ((c >= 72) & (c < 80) & (r == c - 8))
    expand = jnp.where(expand, 1.0, 0.0).astype(jnp.bfloat16)
    high, low = split(factor.reshape(peers * RES, 128))
    factor = (dot_nn(high, expand) + dot_nn(low, expand)).reshape(peers, RES, 128)
    total = jnp.sum(factor * parts, axis=0)
    share = jnp.exp(local[:, 64:72] - top[:, 64:72]) / total[:, 72:80]
    probs[...] = raw[...] * head_column(share)
    spread = jnp.where((c < 64) & (r == 72 + c // 8), 1.0, 0.0)
    heads = total[:, :64] / exact_nn(total, spread)[:, :64]
    attended[...] = heads
    heads_t = heads.T
    mixing_parts = lhs_parts(mixing[...])
    factor_parts = lhs_parts(factors[...])
    for pair in range(RES // 2):
        shown, used, base = [], [], []
        for k in range(2):
            i = 2 * pair + k
            rows = slice(64 * i, 64 * i + 64)
            use = gate[rows] * heads_t[:, i : i + 1]
            mixed[rows] = use
            used.append(use)
            base.append(m0t[rows])
            shown.append(present[i : i + 1])
        middle = jnp.concatenate(base, axis=1) + project(mixing_parts, jnp.concatenate(used, axis=1))
        center = middle - jnp.mean(middle, axis=0, keepdims=True)
        scale = lax.rsqrt(jnp.mean(center * center, axis=0, keepdims=True) + EPSILON)
        normed = center * scale
        found = project(factor_parts, normed) * jnp.concatenate(shown, axis=1)
        for k in range(2):
            i = 2 * pair + k
            lanes = slice(SEQ * k, SEQ * k + SEQ)
            x1t[64 * i : 64 * i + 64] = normed[:, lanes]
            inverse_mid[i : i + 1] = scale[:, lanes]
            left[32 * i : 32 * i + 32] = found[:32, lanes]
            scratch[32 * i : 32 * i + 32] = found[32:, lanes]
    for f in range(FACTOR_WIDTH):
        right[f] = scratch[pl.ds(f, RES, stride=FACTOR_WIDTH), :]


def middle_kernel(
    left_own, left_far, right_own, right_1, right_2, right_3, x1t, inverse_mid, present, slope_t, gate,
    factors_back, mixing_back, mid, out_grad, send, scratch,
):
    for f in range(FACTOR_WIDTH):
        scratch[32 * f : 32 * f + 32] = (right_own[f] + right_1[f]) + (right_2[f] + right_3[f])
    parts = lhs_parts(factors_back[...])
    mixing_parts = lhs_parts(mixing_back[...])
    ones = jnp.ones((16, SEQ), jnp.bfloat16)
    sums = []
    for pair in range(RES // 2):
        grads = []
        for k in range(2):
            i = 2 * pair + k
            rows = slice(32 * i, 32 * i + 32)
            both = jnp.concatenate(
                [left_own[rows] + left_far[rows], scratch[pl.ds(i, FACTOR_WIDTH, stride=RES), :]], axis=0
            )
            grads.append(both * present[i : i + 1])
        mid_in = project(parts, jnp.concatenate(grads, axis=1))
        rows = slice(128 * pair, 128 * pair + 128)
        normed = jnp.concatenate([x1t[128 * pair : 128 * pair + 64], x1t[128 * pair + 64 : 128 * pair + 128]], axis=1)
        scale = jnp.concatenate([inverse_mid[2 * pair : 2 * pair + 1], inverse_mid[2 * pair + 1 : 2 * pair + 2]], axis=1)
        back = scale * (
            mid_in
            - jnp.mean(mid_in, axis=0, keepdims=True)
            - normed * jnp.mean(mid_in * normed, axis=0, keepdims=True)
        )
        back = back + jnp.concatenate(
            [slope_t[128 * pair : 128 * pair + 64], slope_t[128 * pair + 64 : 128 * pair + 128]], axis=1
        )
        grad = project(mixing_parts, back)
        gated = []
        for k in range(2):
            lanes = slice(SEQ * k, SEQ * k + SEQ)
            rows = slice(128 * pair + 64 * k, 128 * pair + 64 * k + 64)
            mid[rows] = back[:, lanes]
            out_grad[rows] = grad[:, lanes]
            gated.append(grad[:, lanes] * gate[rows])
        sums.append(sum_lanes_01(ones, jnp.concatenate(gated, axis=0)))
    sums = [jnp.concatenate([part, part], axis=0) for part in sums]
    send_all(send, slice(0, 16), pack(own_blocks(jnp.concatenate(sums, axis=1))))


def gate_back_kernel(out_grad, mixed, gate, filter_weight, x_grad):
    parts = lhs_parts(filter_weight[...])
    for pair in range(RES // 2):
        both = []
        for k in range(2):
            rows = slice(128 * pair + 64 * k, 128 * pair + 64 * k + 64)
            both.append(out_grad[rows] * mixed[rows] * (1.0 - gate[rows]))
        found = project(parts, jnp.concatenate(both, axis=1))
        for k in range(2):
            x_grad[128 * pair + 64 * k : 128 * pair + 64 * k + 64] = found[:, SEQ * k : SEQ * k + SEQ]


def score_back_kernel(got, attended, probs, keys, values, score_grad, grad_blocks, send):
    att_grad = unpack(jnp.sum(got[...], axis=0))
    blocks = head_blocks(att_grad)
    grad_blocks[...] = blocks
    rows, lanes = row_lane((RES * 8, 64))
    along = jnp.sum(
        jnp.where(rows % 8 == lanes // 8, over_heads(att_grad * attended[...]), 0.0), axis=1, keepdims=True
    )
    grad = probs[...] * (exact_nn(blocks, values[...]) - along)
    score_grad[...] = grad
    folded = fold_blocks(exact_nt(grad, keys[...]))[:, :64]
    send_all(send, slice(0, 16), pack(sum_heads(jnp.where(rows % 8 == lanes // 8, folded, 0.0))))


def key_back_kernel(score_grad, grad_blocks, query_blocks, probs, partial, key_value, x_grad):
    key_grad = exact_nn(query_blocks[...].T, score_grad[...])
    value_grad = exact_nn(grad_blocks[...].T, probs[...])
    parts = lhs_parts(key_value[...])
    for pair in range(RES // 2):
        both = []
        for k in range(2):
            rows = slice(16 * pair + 8 * k, 16 * pair + 8 * k + 8)
            both.append(jnp.concatenate([key_grad[rows], value_grad[rows]], axis=0))
        found = project(parts, jnp.concatenate(both, axis=1))
        for k in range(2):
            rows = slice(128 * pair + 64 * k, 128 * pair + 64 * k + 64)
            x_grad[rows] = partial[rows] + found[:, SEQ * k : SEQ * k + SEQ]


def final_kernel(got, counts, asking, present, x0t, inverse, x_grad, mid, out):
    query_grad = unpack(jnp.sum(got[...], axis=0)) * HEAD_SIZE ** (-0.5)
    mean_grad = (exact_nt(query_grad, asking[...]) / counts[:, :64]).T
    for pair in range(RES // 2):
        done = []
        for k in range(2):
            i = 2 * pair + k
            rows = slice(64 * i, 64 * i + 64)
            grad = x_grad[rows] + mean_grad[:, i : i + 1] * present[i : i + 1]
            normed = x0t[rows]
            back = inverse[i : i + 1] * (
                grad - jnp.mean(grad, axis=0, keepdims=True) - normed * jnp.mean(grad * normed, axis=0, keepdims=True)
            )
            done.append(mid[rows] + back)
        out[:, 128 * pair : 128 * pair + 128] = jnp.concatenate(done, axis=0).T


def call(kernel, shapes, *operands, scratch=(), flops=100_000_000, vmem=24):
    shapes = [jax.ShapeDtypeStruct(shape, F32) for shape in shapes]
    size = sum(4 * array.size for array in shapes) + sum(array.size * array.dtype.itemsize for array in operands)
    return pl.pallas_call(
        kernel,
        out_shape=shapes,
        scratch_shapes=list(scratch),
        compiler_params=pltpu.CompilerParams(vmem_limit_bytes=vmem * 2**20),
        cost_estimate=pl.CostEstimate(flops=flops, bytes_accessed=int(size), transcendentals=0),
        name=kernel.__name__,
    )(*operands)


ROWS = 8


def right_kernel(place, own_g, far_g, inverse_count, weight, left, high, low, out, weights, total):
    step = pl.program_id(0)
    x = place[0]

    @pl.when(step == 0)
    def _():
        w_high, w_low = split(weight[...])
        weights[:, 0:128] = w_high
        weights[:, 128:256] = w_low
        weights[:, 256:384] = w_high
        total[...] = jnp.zeros_like(total)

    near = step < pl.num_programs(0) // 2
    for pair in range(ROWS // 2):
        blocks = []
        for row in (2 * pair, 2 * pair + 1):
            for d in range(4):
                chip = lax.rem(x + d, 4)
                blocks.append(jnp.where(near, own_g[row, chip, 0], far_g[row, chip]))
        g_high, g_low = split(jnp.concatenate(blocks, axis=0))
        grads = dot_nt(weights[...], jnp.concatenate([g_high, g_high, g_low], axis=1))
        grads = grads * jnp.concatenate(
            [inverse_count[2 * pair : 2 * pair + 1], inverse_count[2 * pair + 1 : 2 * pair + 2]], axis=1
        )
        grads_high, grads_low = split(grads)
        for k in range(2):
            row = (2 * pair + k) * FACTOR_WIDTH
            rows, lanes = slice(row, row + FACTOR_WIDTH), slice(128 * k, 128 * k + 128)
            high[:, rows, :] = grads_high[:, lanes].reshape(FACTOR_WIDTH, FACTOR_WIDTH, 128)
            low[:, rows, :] = grads_low[:, lanes].reshape(FACTOR_WIDTH, FACTOR_WIDTH, 128)
    l_high, l_low = split(left[...].T)
    stacked = jnp.concatenate([l_high, l_low], axis=0)
    for f in range(0, FACTOR_WIDTH, 2):
        first = dot_nn(stacked, jnp.concatenate([high[f], high[f + 1]], axis=1))
        second = dot_nn(l_high, jnp.concatenate([low[f], low[f + 1]], axis=1))
        total[:, 128 * f : 128 * f + 256] += first[:128] + first[128:] + second

    @pl.when(step == pl.num_programs(0) - 1)
    def _():
        for f in range(FACTOR_WIDTH):
            block = total[:, 128 * f : 128 * f + 128].T
            for d in range(4):
                out[d, f] = block[32 * d : 32 * d + 32]


def right_products(place, pair_grad, far_grad, inverse_count, weight, left):
    block = ROWS * FACTOR_WIDTH
    steps = 64 // ROWS
    half = steps // 2
    grid_spec = pltpu.PrefetchScalarGridSpec(
        num_scalar_prefetch=1,
        grid=(steps,),
        in_specs=[
            pl.BlockSpec((ROWS, 4, 1, 32, 128), lambda t, s: (jnp.minimum(t, half - 1), 0, s[1], 0, 0)),
            pl.BlockSpec((ROWS, 4, 32, 128), lambda t, s: (jnp.maximum(t - half, 0), 0, 0, 0)),
            pl.BlockSpec((ROWS, 128), lambda t, s: (t, 0)),
            pl.BlockSpec((1024, 128), lambda t, s: (0, 0)),
            pl.BlockSpec((block, 128), lambda t, s: (t, 0)),
        ],
        out_specs=[
            pl.BlockSpec((FACTOR_WIDTH, block, 128), lambda t, s: (0, t, 0)),
            pl.BlockSpec((FACTOR_WIDTH, block, 128), lambda t, s: (0, t, 0)),
            pl.BlockSpec((4, FACTOR_WIDTH, 32, 128), lambda t, s: (0, 0, 0, 0)),
        ],
        scratch_shapes=[
            pltpu.VMEM((1024, 384), jnp.bfloat16),
            pltpu.VMEM((128, 4096), jnp.float32),
        ],
    )
    return pl.pallas_call(
        right_kernel,
        grid_spec=grid_spec,
        out_shape=[
            jax.ShapeDtypeStruct((FACTOR_WIDTH, 64 * FACTOR_WIDTH, 128), jnp.bfloat16),
            jax.ShapeDtypeStruct((FACTOR_WIDTH, 64 * FACTOR_WIDTH, 128), jnp.bfloat16),
            jax.ShapeDtypeStruct((4, FACTOR_WIDTH, 32, 128), jnp.float32),
        ],
        compiler_params=pltpu.CompilerParams(vmem_limit_bytes=48 * 2**20),
        cost_estimate=pl.CostEstimate(flops=16_000_000_000, bytes_accessed=42_000_000, transcendentals=0),
        name="right_products",
    )(place, pair_grad, far_grad, inverse_count, weight, left)


def left_kernel(high, low, right_0, right_1, right_2, right_3, out, weights):
    @pl.when(pl.program_id(0) == 0)
    def _():
        for f in range(FACTOR_WIDTH):
            for d, right in enumerate((right_0, right_1, right_2, right_3)):
                r_high, r_low = split(right[f])
                row = (f % 2) * 128 + d * 32
                weights[f // 2, row : row + 32, 0:128] = r_high
                weights[f // 2, row : row + 32, 128:256] = r_low

    first = jnp.zeros((ROWS * FACTOR_WIDTH, 256), jnp.float32)
    second = jnp.zeros((ROWS * FACTOR_WIDTH, 128), jnp.float32)
    for f in range(0, FACTOR_WIDTH, 2):
        first += dot_nn(jnp.concatenate([high[f], high[f + 1]], axis=1), weights[f // 2])
        second += dot_nn(jnp.concatenate([low[f], low[f + 1]], axis=1), weights[f // 2, :, 0:128])
    out[...] = first[:, :128] + first[:, 128:] + second


def left_products(high, low, rights):
    block = ROWS * FACTOR_WIDTH
    whole = pl.BlockSpec((FACTOR_WIDTH, 32, 128), lambda t: (0, 0, 0))
    return pl.pallas_call(
        left_kernel,
        grid=(64 // ROWS,),
        in_specs=[
            pl.BlockSpec((FACTOR_WIDTH, block, 128), lambda t: (0, t, 0)),
            pl.BlockSpec((FACTOR_WIDTH, block, 128), lambda t: (0, t, 0)),
            whole,
            whole,
            whole,
            whole,
        ],
        out_specs=pl.BlockSpec((block, 128), lambda t: (t, 0)),
        out_shape=jax.ShapeDtypeStruct((64 * FACTOR_WIDTH, 128), jnp.float32),
        scratch_shapes=[pltpu.VMEM((FACTOR_WIDTH // 2, 256, 256), jnp.bfloat16)],
        compiler_params=pltpu.CompilerParams(vmem_limit_bytes=40 * 2**20),
        cost_estimate=pl.CostEstimate(flops=9_000_000_000, bytes_accessed=37_000_000, transcendentals=0),
        name="left_products",
    )(high, low, *rights)


def swap_core(values):
    return lax.ppermute(values, "core", [(0, 1), (1, 0)])


def fetch_chip(values, distance):
    return lax.ppermute(values, "x", [((i + distance) % 4, i) for i in range(4)])


def send_chip(values, distance):
    return lax.ppermute(values, "x", [(i, (i + distance) % 4) for i in range(4)])


def exchange(send):
    return lax.all_to_all(send, "seq", 0, 0, tiled=True)


def body(
    homolog_features,
    homolog_loss_slope,
    pair_update_gradient,
    alignment_mask,
    asking_matrix,
    key_weight,
    content_matrix,
    sigmoid_filter_matrix,
    final_mixing_matrix,
    first_factor_matrix,
    second_factor_matrix,
    pair_weight,
):
    peers = lax.axis_size("seq")
    share = 64 // peers
    counted, shared = -(-(17 + share) // 8) * 8, -(-(32 + share) // 8) * 8
    x, core = lax.axis_index("x"), lax.axis_index("core")
    place = jnp.stack([x, core]).astype(jnp.int32)
    mask_core = swap_core(alignment_mask)
    mask_chips = [fetch_chip(alignment_mask, d) for d in (1, 2, 3)]
    pair_grad = pair_update_gradient.reshape(32, 4, 2, 32, 128)
    far_grad = swap_core(lax.dynamic_index_in_dim(pair_grad, 1 - core, 2, keepdims=False))
    weight = pair_weight.reshape(FACTOR_WIDTH, FACTOR_WIDTH, 128).swapaxes(0, 1).reshape(1024, 128)
    value_gate = jnp.concatenate([content_matrix, sigmoid_filter_matrix], axis=1).T
    key_value = jnp.concatenate([key_weight, content_matrix], axis=1)
    factors = jnp.concatenate([first_factor_matrix, second_factor_matrix], axis=1)

    flat, heads, stat = (RES * 64, SEQ), (RES * 8, SEQ), (RES, SEQ)
    m0t, x0t, inverse, present, send = call(
        norm_kernel, [flat, flat, stat, stat, (peers, counted, 128)], homolog_features, alignment_mask
    )
    (send,) = call(pair_kernel, [(peers, counted, 128)], send, alignment_mask, mask_core, *mask_chips)
    got = exchange(send)
    keys, values, gate, slope_t = call(
        project_kernel, [heads, heads, flat, flat], x0t, homolog_loss_slope, key_weight.T, value_gate
    )
    raw, local, counts, query_blocks, send = call(
        score_kernel, [heads, stat, stat, (RES * 8, RES * 8), (peers, shared, 128)], got, keys, values, present, asking_matrix
    )
    got = exchange(send)
    probs, attended, mixed, x1t, inverse_mid, left, right, inverse_count = call(
        attend_kernel,
        [heads, (RES, 64), flat, flat, stat, (RES * 32, SEQ), (FACTOR_WIDTH, RES, SEQ), (64, 128)],
        got, local, raw, m0t, gate, present, final_mixing_matrix.T, factors.T,
        scratch=[pltpu.VMEM((RES * 32, SEQ), F32)],
    )
    left_rows = jnp.concatenate([left, swap_core(left)], axis=0)
    rights = [right] + [fetch_chip(right, d) for d in (1, 2, 3)]
    high, low, right_parts = right_products(place, pair_grad, far_grad, inverse_count, weight, left_rows)
    right_sent = [send_chip(right_parts[d], d) for d in (1, 2, 3)]
    left_parts = left_products(high, low, rights)
    half = RES * FACTOR_WIDTH
    mid, out_grad, send = call(
        middle_kernel, [flat, flat, (peers, 16, 128)],
        left_parts[:half], swap_core(left_parts[half:]), right_parts[0], *right_sent,
        x1t, inverse_mid, present, slope_t, gate, factors, final_mixing_matrix,
        scratch=[pltpu.VMEM((RES * 32, SEQ), F32)],
    )
    got = exchange(send)
    (gate_grad,) = call(gate_back_kernel, [flat], out_grad, mixed, gate, sigmoid_filter_matrix)
    score_grad, grad_blocks, send = call(
        score_back_kernel, [heads, (RES * 8, RES * 8), (peers, 16, 128)], got, attended, probs, keys, values
    )
    got = exchange(send)
    (x_grad,) = call(key_back_kernel, [flat], score_grad, grad_blocks, query_blocks, probs, gate_grad, key_value)
    (out,) = call(final_kernel, [(SEQ, RES * 64)], got, counts, asking_matrix, present, x0t, inverse, x_grad, mid)
    return out


def solution(mesh):
    grid = Mesh(mesh.devices.reshape(mesh.devices.shape[0], 4, 2), ("seq", "x", "core"))
    res = ("x", "core")
    in_specs = (
        P("seq", res),
        P("seq", res),
        P(res, None, None),
        P("seq", res),
        P(),
        P(),
        P(),
        P(),
        P(),
        P(),
        P(),
        P(),
    )
    return jax.shard_map(body, mesh=grid, in_specs=in_specs, out_specs=P("seq", res), check_vma=False)
```

```python
import functools

import jax
import jax.numpy as jnp
from jax import lax
from jax.experimental import pallas as pl
from jax.experimental.pallas import tpu as pltpu
from jax.sharding import Mesh
from jax.sharding import PartitionSpec as P

FEATURE_DEPTH = 64
HEAD_COUNT = 8
HEAD_SIZE = 8
FACTOR_WIDTH = 32
RES = 32
SEQ = 128

EPSILON = 1e-05
MASK_FILL = -1000000000.0
PRECISE = lax.Precision.HIGHEST
F32 = jnp.float32


def split(values):
    high = values.astype(jnp.bfloat16)
    low = (values - high.astype(jnp.float32)).astype(jnp.bfloat16)
    return high, low


def dot_nn(a, b):
    return lax.dot_general(a, b, (((1,), (0,)), ((), ())), preferred_element_type=jnp.float32)


def dot_nt(a, b):
    return lax.dot_general(a, b, (((1,), (1,)), ((), ())), preferred_element_type=jnp.float32)


def exact_nn(a, b):
    return lax.dot_general(a, b, (((1,), (0,)), ((), ())), preferred_element_type=F32, precision=PRECISE)


def exact_nt(a, b):
    return lax.dot_general(a, b, (((1,), (1,)), ((), ())), preferred_element_type=F32, precision=PRECISE)


def lhs_parts(weight):
    high, low = split(weight)
    return jnp.concatenate([high, high, low], axis=1)


def project(parts, values):
    high, low = split(values)
    return dot_nn(parts, jnp.concatenate([high, low, high], axis=0))


def row_lane(shape):
    return lax.broadcasted_iota(jnp.int32, shape, 0), lax.broadcasted_iota(jnp.int32, shape, 1)


def sum_lanes_01(ones, values):
    high, rest = values.astype(jnp.bfloat16), values
    rest = rest - high.astype(F32)
    mid = rest.astype(jnp.bfloat16)
    low = (rest - mid.astype(F32)).astype(jnp.bfloat16)
    return dot_nt(ones, high) + dot_nt(ones, mid) + dot_nt(ones, low)


def own_blocks(values):
    rows, _ = row_lane((RES, 128))
    total = jnp.zeros((RES, 128), F32)
    for pair in range(RES // 2):
        total = jnp.where(rows // 2 == pair, values[:, 128 * pair : 128 * pair + 128], total)
    return jnp.where(rows[:, :64] % 2 == 0, total[:, :64], total[:, 64:])


def pack(values):
    return jnp.concatenate([values[:16], values[16:]], axis=1)


def unpack(values):
    return jnp.concatenate([values[:, :64], values[:, 64:]], axis=0)


def over_heads(values):
    return jnp.broadcast_to(values[:, None, :], (RES, 8, values.shape[1])).reshape(RES * 8, values.shape[1])


def head_column(values):
    rows, lanes = row_lane((RES * 8, values.shape[1]))
    return jnp.sum(jnp.where(rows % 8 == lanes, over_heads(values), 0.0), axis=1, keepdims=True)


def head_blocks(values):
    rows, lanes = row_lane((RES * 8, 64))
    picked = jnp.where(rows % 8 == lanes // 8, over_heads(values), 0.0)
    r, c = row_lane((64, RES * 8))
    spread = exact_nn(picked, (r % 8 == c % 8).astype(F32))
    rows, lanes = row_lane((RES * 8, RES * 8))
    return jnp.where(rows // 8 == lanes // 8, spread, 0.0)


def fold_blocks(values):
    rows, lanes = row_lane((RES * 8, RES * 8))
    r, c = row_lane((RES * 8, 128))
    fold = jnp.where((r % 8 == c % 8) & (c < 64), 1.0, 0.0)
    return exact_nn(jnp.where(rows // 8 == lanes // 8, values, 0.0), fold)


def sum_heads(values):
    return jnp.sum(values.reshape(RES, 8, values.shape[1]), axis=1)


def send_all(send, rows, values):
    send[:, rows, :] = jnp.broadcast_to(values[None], (send.shape[0],) + values.shape)


def norm_kernel(m0, mask, x0t, inverse, present, send):
    shown = mask[...].astype(F32).T
    present[...] = shown
    for pair in range(RES // 2):
        block = m0[:, 128 * pair : 128 * pair + 128].T
        for k in range(2):
            part = block[64 * k : 64 * k + 64]
            center = part - jnp.mean(part, axis=0, keepdims=True)
            scale = lax.rsqrt(jnp.mean(center * center, axis=0, keepdims=True) + EPSILON)
            row = 2 * pair + k
            inverse[row : row + 1] = scale
            x0t[64 * row : 64 * row + 64] = center * scale
    ones = shown.astype(jnp.bfloat16)
    sums = own_blocks(sum_lanes_01(ones, x0t[...]))
    counts = dot_nt(jnp.ones((16, SEQ), jnp.bfloat16), ones)
    send[...] = jnp.zeros_like(send)
    send_all(send, slice(0, 16), pack(sums))
    send_all(send, slice(16, 17), jnp.concatenate([counts[0:1], jnp.zeros((1, 96), F32)], axis=1))


def pair_kernel(sent, mask, mask_core, mask_1, mask_2, mask_3, send):
    send[...] = sent[...]
    own = mask[...].astype(F32).T.astype(jnp.bfloat16)
    rows = jnp.concatenate([own, mask_core[...].astype(F32).T.astype(jnp.bfloat16)], axis=0)
    columns = jnp.concatenate(
        [own] + [part[...].astype(F32).T.astype(jnp.bfloat16) for part in (mask_1, mask_2, mask_3)], axis=0
    )
    count = dot_nt(rows, columns)
    share = 64 // send.shape[0]
    for peer in range(send.shape[0]):
        send[peer, 17 : 17 + share, :] = count[share * peer : share * peer + share]


def project_kernel(x0t, m0, slope, key, value_gate, keys, values, gate, m0t, slope_t):
    parts = lhs_parts(value_gate[...])
    for pair in range(RES // 2):
        m0t[128 * pair : 128 * pair + 128] = m0[:, 128 * pair : 128 * pair + 128].T
        slope_t[128 * pair : 128 * pair + 128] = slope[:, 128 * pair : 128 * pair + 128].T
        row = 128 * pair
        both = jnp.concatenate([x0t[row : row + 64], x0t[row + 64 : row + 128]], axis=1)
        found = project(parts, both)
        key_rows = exact_nn(key[...], both)
        gates = jax.nn.sigmoid(found[8:72])
        for k in range(2):
            lanes = slice(SEQ * k, SEQ * k + SEQ)
            head = 8 * (2 * pair + k)
            keys[head : head + 8] = key_rows[:, lanes]
            values[head : head + 8] = found[0:8, lanes]
            gate[row + 64 * k : row + 64 * k + 64] = gates[:, lanes]


def score_kernel(got, keys, values, present, asking, weights, local, counts, query_blocks, send):
    sums = jnp.sum(got[...], axis=0)
    r, c = row_lane((RES, RES))
    count = jnp.sum(jnp.where(r == c, jnp.broadcast_to(sums[16:17, :RES], (RES, RES)), 0.0), axis=1, keepdims=True)
    counts[...] = jnp.broadcast_to(count, (RES, 128))
    queries = exact_nn(unpack(sums[:16]) / count, asking[...]) * HEAD_SIZE ** (-0.5)
    blocks = head_blocks(queries)
    query_blocks[...] = blocks
    scores = exact_nn(blocks, keys[...])
    scores = jnp.where(over_heads(present[...]) > 0, scores, MASK_FILL)
    top = jnp.max(scores, axis=1, keepdims=True)
    raw = jnp.exp(scores - top)
    weights[...] = raw
    total = jnp.sum(raw, axis=1, keepdims=True)
    rows, lanes = row_lane((RES * 8, 64))
    own_head = rows % 8 == lanes // 8
    weighted = sum_heads(jnp.where(own_head, fold_blocks(exact_nt(raw, values[...]))[:, :64], 0.0))
    send_all(send, slice(0, 16), pack(weighted))
    rows, lanes = row_lane((RES * 8, 16))
    stats = jnp.where(lanes == rows % 8, top, jnp.where(lanes == 8 + rows % 8, total, 0.0))
    stats = sum_heads(stats)
    local[...] = stats
    share = 64 // send.shape[0]
    pairs = sums[17 : 17 + share]
    stats = jnp.concatenate([stats[8 * k : 8 * k + 8] for k in range(4)], axis=1)
    if share == 2:
        right = jnp.concatenate([pairs[:, :64], pairs[:, 64:], jnp.zeros((4, 64), F32)], axis=0)
    else:
        right = jnp.zeros((8, 64), F32)
        send_all(send, slice(send.shape[1] - share, send.shape[1]), pairs)
    send_all(send, slice(16, 24), jnp.concatenate([stats, right], axis=1))
    products = raw.reshape(RES, 8, 1, SEQ) * values[...].reshape(RES, 1, 8, SEQ)
    products = products.reshape(RES * 64, SEQ)
    half = RES // 2
    rows, lanes = row_lane((half * 64, 128))
    same = rows // 64 == lanes // 8
    r, c = row_lane((128, 64))
    fold = jnp.where(r % 8 == c % 8, 1.0, 0.0).astype(jnp.bfloat16)
    moments = []
    for k in range(2):
        a_high, a_low = split(products[half * 64 * k : half * 64 * (k + 1)])
        b_high, b_low = split(keys[128 * k : 128 * k + 128])
        found = dot_nt(
            jnp.concatenate([a_high, a_high, a_low], axis=1), jnp.concatenate([b_high, b_low, b_high], axis=1)
        )
        f_high, f_low = split(jnp.where(same, found, 0.0))
        spread = dot_nn(f_high, fold) + dot_nn(f_low, fold)
        spread = jnp.where(rows[:, :64] % 8 == lanes[:, :64] // 8, spread, 0.0)
        moments.append(jnp.sum(spread.reshape(half * 8, 8, 64), axis=1))
    moments = jnp.concatenate(moments, axis=0)
    firsts = fold_blocks(exact_nt(raw, keys[...]))
    rows, lanes = row_lane((RES * 8, 64))
    rest = jnp.where(lanes < 8, firsts[:, :64], jnp.where(lanes == 8, top, jnp.where(lanes == 9, total, 0.0)))
    block = jnp.concatenate([moments, rest], axis=1)
    size = RES * 8 // send.shape[0]
    send[:, 24 : 24 + size, :] = block.reshape(send.shape[0], size, 128)


def attend_kernel(
    got, local, raw, m0t, gate, present, mixing, factors,
    probs, attended, mixed, x1t, inverse_mid, left, right, inverse_count, moments, scratch, arrive,
):
    peers = got.shape[0]
    share = 64 // peers
    for peer in range(peers):
        if share == 2:
            pairs = jnp.concatenate([got[peer, 16:18, 64:], got[peer, 18:20, 64:]], axis=1)
        else:
            pairs = got[peer, got.shape[1] - share :, :]
        inverse_count[share * peer : share * peer + share] = 1.0 / pairs
    weighted = jnp.concatenate([got[:, 0:16, 0:64], got[:, 0:16, 64:128]], axis=1)
    stats = jnp.concatenate([got[:, 16:24, 16 * k : 16 * k + 16] for k in range(4)], axis=1)
    tops = stats[:, :, 0:8]
    top = jnp.max(tops, axis=0)
    factor = jnp.exp(tops - top[None])
    total = jnp.sum(factor * stats[:, :, 8:16], axis=0)
    r, c = row_lane((8, 64))
    expand = jnp.where(r == c // 8, 1.0, 0.0)
    high, low = split(factor.reshape(peers * RES, 8))
    wide = expand.astype(jnp.bfloat16)
    factor = (dot_nn(high, wide) + dot_nn(low, wide)).reshape(peers, RES, 64)
    heads = jnp.sum(factor * weighted, axis=0) / exact_nn(total, expand)
    probs[...] = raw[...] * head_column(jnp.exp(local[:, 0:8] - top) / total)
    attended[...] = heads
    size = RES * 8 // peers
    block = got[:, 24 : 24 + size, :]
    tops = block[:, :, 72:73]
    block = jnp.sum(jnp.exp(tops - jnp.max(tops, axis=0)[None]) * block, axis=0)
    lanes = lax.broadcasted_iota(jnp.int32, block.shape, 1)
    moments[...] = jnp.where(lanes < 72, block / block[:, 73:74], 0.0)
    heads_t = heads.T
    mixing_parts = lhs_parts(mixing[...])
    factor_parts = lhs_parts(factors[...])
    arrive()
    for pair in range(RES // 2):
        shown, used, base = [], [], []
        for k in range(2):
            i = 2 * pair + k
            rows = slice(64 * i, 64 * i + 64)
            use = gate[rows] * heads_t[:, i : i + 1]
            mixed[rows] = use
            used.append(use)
            base.append(m0t[rows])
            shown.append(present[i : i + 1])
        middle = jnp.concatenate(base, axis=1) + project(mixing_parts, jnp.concatenate(used, axis=1))
        center = middle - jnp.mean(middle, axis=0, keepdims=True)
        scale = lax.rsqrt(jnp.mean(center * center, axis=0, keepdims=True) + EPSILON)
        normed = center * scale
        found = project(factor_parts, normed) * jnp.concatenate(shown, axis=1)
        for k in range(2):
            i = 2 * pair + k
            lanes = slice(SEQ * k, SEQ * k + SEQ)
            x1t[64 * i : 64 * i + 64] = normed[:, lanes]
            inverse_mid[i : i + 1] = scale[:, lanes]
            left[32 * i : 32 * i + 32] = found[:32, lanes]
            scratch[32 * i : 32 * i + 32] = found[32:, lanes]
    for f in range(FACTOR_WIDTH):
        right[f] = scratch[pl.ds(f, RES, stride=FACTOR_WIDTH), :]


def middle_kernel(
    left_own, left_far_0, left_far_1, right_own, right_1, right_2, right_3, moments, x1t, inverse_mid, present, slope_t, gate,
    factors_back, mixing_back, mid, out_grad, send, scratch,
):
    for f in range(FACTOR_WIDTH):
        scratch[32 * f : 32 * f + 32] = (right_own[f] + right_1[f]) + (right_2[f] + right_3[f])
    parts = lhs_parts(factors_back[...])
    mixing_parts = lhs_parts(mixing_back[...])
    ones = jnp.ones((16, SEQ), jnp.bfloat16)
    sums = []
    for pair in range(RES // 2):
        grads = []
        for k in range(2):
            i = 2 * pair + k
            rows = slice(32 * i, 32 * i + 32)
            left_far = left_far_0 if i < RES // 2 else left_far_1
            near = slice(32 * (i % 16), 32 * (i % 16) + 32)
            both = jnp.concatenate(
                [left_own[rows] + left_far[near], scratch[pl.ds(i, FACTOR_WIDTH, stride=RES), :]], axis=0
            )
            grads.append(both * present[i : i + 1])
        mid_in = project(parts, jnp.concatenate(grads, axis=1))
        rows = slice(128 * pair, 128 * pair + 128)
        normed = jnp.concatenate([x1t[128 * pair : 128 * pair + 64], x1t[128 * pair + 64 : 128 * pair + 128]], axis=1)
        scale = jnp.concatenate([inverse_mid[2 * pair : 2 * pair + 1], inverse_mid[2 * pair + 1 : 2 * pair + 2]], axis=1)
        back = scale * (
            mid_in
            - jnp.mean(mid_in, axis=0, keepdims=True)
            - normed * jnp.mean(mid_in * normed, axis=0, keepdims=True)
        )
        back = back + jnp.concatenate(
            [slope_t[128 * pair : 128 * pair + 64], slope_t[128 * pair + 64 : 128 * pair + 128]], axis=1
        )
        grad = project(mixing_parts, back)
        gated = []
        for k in range(2):
            lanes = slice(SEQ * k, SEQ * k + SEQ)
            rows = slice(128 * pair + 64 * k, 128 * pair + 64 * k + 64)
            mid[rows] = back[:, lanes]
            out_grad[rows] = grad[:, lanes]
            gated.append(grad[:, lanes] * gate[rows])
        sums.append(sum_lanes_01(ones, jnp.concatenate(gated, axis=0)))
    sums = [jnp.concatenate([part, part], axis=0) for part in sums]
    send_all(send, slice(0, 16), pack(own_blocks(jnp.concatenate(sums, axis=1))))
    send_all(send, slice(16, 16 + moments.shape[0]), moments[...])


def gate_back_kernel(out_grad, mixed, gate, filter_weight, x_grad):
    parts = lhs_parts(filter_weight[...])
    for pair in range(RES // 2):
        both = []
        for k in range(2):
            rows = slice(128 * pair + 64 * k, 128 * pair + 64 * k + 64)
            both.append(out_grad[rows] * mixed[rows] * (1.0 - gate[rows]))
        found = project(parts, jnp.concatenate(both, axis=1))
        for k in range(2):
            x_grad[128 * pair + 64 * k : 128 * pair + 64 * k + 64] = found[:, SEQ * k : SEQ * k + SEQ]


def finish_kernel(
    got, attended, probs, keys, values, query_blocks, partial, key_value, counts, asking, present, x0t, inverse, mid, out, arrive
):
    att_grad = unpack(jnp.sum(got[:, 0:16, :], axis=0))
    moments = got[:, 16:, :].reshape(RES * 8, 128)
    rows, lanes = row_lane((RES * 8, 64))
    own_head = rows % 8 == lanes // 8
    along = jnp.sum(jnp.where(own_head, over_heads(att_grad * attended[...]), 0.0), axis=1, keepdims=True)
    r, c = row_lane((64, 64))
    spread = exact_nn(jnp.where(own_head, over_heads(att_grad), 0.0), (r % 8 == c // 8).astype(F32))
    both = jnp.concatenate([spread * moments[:, :64], -along * moments[:, 64:]], axis=1)
    r, c = row_lane((128, 64))
    query_grad = exact_nn(both, jnp.where((r < 72) & (r % 8 == c % 8), 1.0, 0.0))
    query_grad = sum_heads(jnp.where(own_head, query_grad, 0.0)) * HEAD_SIZE ** (-0.5)
    mean_grad = (exact_nt(query_grad, asking[...]) / counts[:, :64]).T

    blocks = head_blocks(att_grad)
    score_grad = probs[...] * (exact_nn(blocks, values[...]) - along)
    key_grad = exact_nn(query_blocks[...].T, score_grad)
    value_grad = exact_nn(blocks.T, probs[...])
    parts = lhs_parts(key_value[...])
    arrive()
    for pair in range(RES // 2):
        both = []
        for k in range(2):
            rows = slice(16 * pair + 8 * k, 16 * pair + 8 * k + 8)
            both.append(jnp.concatenate([key_grad[rows], value_grad[rows]], axis=0))
        found = project(parts, jnp.concatenate(both, axis=1))
        done = []
        for k in range(2):
            i = 2 * pair + k
            rows = slice(64 * i, 64 * i + 64)
            grad = partial[rows] + found[:, SEQ * k : SEQ * k + SEQ] + mean_grad[:, i : i + 1] * present[i : i + 1]
            normed = x0t[rows]
            back = inverse[i : i + 1] * (
                grad - jnp.mean(grad, axis=0, keepdims=True) - normed * jnp.mean(grad * normed, axis=0, keepdims=True)
            )
            done.append(mid[rows] + back)
        out[:, 128 * pair : 128 * pair + 128] = jnp.concatenate(done, axis=0).T


def whole(shape):
    return pl.BlockSpec(shape, lambda *_: (0,) * len(shape))


def staged(kernel, count, late, *refs):
    operands, rest = refs[: count[0]], refs[count[0] :]
    results, rest = rest[: count[1]], rest[count[1] :]
    total = count[0] + count[1]
    held, sems, scratch = rest[:total], rest[total], rest[total + 1 :]
    copies = [pltpu.make_async_copy(operands[k], held[k], sems.at[k]) for k in range(count[0])]
    for copy in copies:
        copy.start()

    def arrive():
        for k in late:
            copies[k].wait()

    for k in range(count[0]):
        if k not in late:
            copies[k].wait()
    kernel(*held, *scratch, *([arrive] if late else []))
    copies = [
        pltpu.make_async_copy(held[count[0] + k], results[k], sems.at[count[0] + k]) for k in range(count[1])
    ]
    for copy in copies:
        copy.start()
    for copy in copies:
        copy.wait()


def call(kernel, shapes, *operands, scratch=(), late=(), free=(), vmem=40):
    shapes = [jax.ShapeDtypeStruct(shape, F32) for shape in shapes]
    size = sum(4 * array.size for array in shapes) + sum(array.size * array.dtype.itemsize for array in operands)
    arrays = list(operands) + shapes
    return pl.pallas_call(
        functools.partial(staged, kernel, (len(operands), len(shapes)), late),
        in_specs=[
            pl.BlockSpec(memory_space=pl.ANY if k in free else pltpu.HBM) for k in range(len(operands))
        ],
        out_specs=[pl.BlockSpec(memory_space=pltpu.HBM)] * len(shapes),
        out_shape=[pltpu.HBM(array.shape, array.dtype) for array in shapes],
        scratch_shapes=[pltpu.VMEM(array.shape, array.dtype) for array in arrays]
        + [pltpu.SemaphoreType.DMA((len(arrays),))]
        + list(scratch),
        compiler_params=pltpu.CompilerParams(vmem_limit_bytes=vmem * 2**20),
        cost_estimate=pl.CostEstimate(flops=100_000_000, bytes_accessed=int(size), transcendentals=0),
        name=kernel.__name__,
    )(
        *[
            array if k in free else pltpu.with_memory_space_constraint(array, pltpu.HBM)
            for k, array in enumerate(operands)
        ]
    )


ROWS = 8
COST = 1000


def right_kernel(
    place, own_g, far_g, inverse_count, weight, left, left_far, high, low, out_0, out_1, out_2, out_3, weights, total
):
    step = pl.program_id(0)
    x = place[0]

    @pl.when(step == 0)
    def _():
        w_high, w_low = split(weight[...])
        weights[:, 0:128] = w_high
        weights[:, 128:256] = w_low
        weights[:, 256:384] = w_high
        total[...] = jnp.zeros_like(total)

    near = step < pl.num_programs(0) // 2
    for pair in range(ROWS // 2):
        blocks = []
        for row in (2 * pair, 2 * pair + 1):
            for d in range(4):
                chip = lax.rem(x + d, 4)
                blocks.append(jnp.where(near, own_g[row, chip, 0], far_g[row, chip]))
        g_high, g_low = split(jnp.concatenate(blocks, axis=0))
        grads = dot_nt(weights[...], jnp.concatenate([g_high, g_high, g_low], axis=1))
        grads = grads * jnp.concatenate(
            [inverse_count[2 * pair : 2 * pair + 1], inverse_count[2 * pair + 1 : 2 * pair + 2]], axis=1
        )
        grads_high, grads_low = split(grads)
        for k in range(2):
            row = (2 * pair + k) * FACTOR_WIDTH
            rows, lanes = slice(row, row + FACTOR_WIDTH), slice(128 * k, 128 * k + 128)
            high[:, rows, :] = grads_high[:, lanes].reshape(FACTOR_WIDTH, FACTOR_WIDTH, 128)
            low[:, rows, :] = grads_low[:, lanes].reshape(FACTOR_WIDTH, FACTOR_WIDTH, 128)
    l_high, l_low = split(jnp.where(near, left[...], left_far[...]).T)
    block = slice(None)
    stacked = jnp.concatenate([l_high, l_low], axis=0)
    for f in range(0, FACTOR_WIDTH, 2):
        first = dot_nn(stacked, jnp.concatenate([high[f, block], high[f + 1, block]], axis=1))
        second = dot_nn(l_high, jnp.concatenate([low[f, block], low[f + 1, block]], axis=1))
        total[:, 128 * f : 128 * f + 256] += first[:128] + first[128:] + second

    @pl.when(step == pl.num_programs(0) - 1)
    def _():
        for f in range(FACTOR_WIDTH):
            block = total[:, 128 * f : 128 * f + 128].T
            for d, out in enumerate((out_0, out_1, out_2, out_3)):
                out[f] = block[32 * d : 32 * d + 32]


def right_products(place, pair_grad, far_grad, inverse_count, weight, left, left_far):
    block = ROWS * FACTOR_WIDTH
    steps = 64 // ROWS
    half = steps // 2
    grid_spec = pltpu.PrefetchScalarGridSpec(
        num_scalar_prefetch=1,
        grid=(steps,),
        in_specs=[
            pl.BlockSpec((ROWS, 4, 1, 32, 128), lambda t, s: (jnp.minimum(t, half - 1), 0, s[1], 0, 0)),
            pl.BlockSpec((ROWS, 4, 32, 128), lambda t, s: (jnp.maximum(t - half, 0), 0, 0, 0)),
            pl.BlockSpec((ROWS, 128), lambda t, s: (t, 0)),
            pl.BlockSpec((1024, 128), lambda t, s: (0, 0)),
            pl.BlockSpec((block, 128), lambda t, s: (jnp.minimum(t, half - 1), 0)),
            pl.BlockSpec((block, 128), lambda t, s: (jnp.maximum(t - half, 0), 0)),
        ],
        out_specs=[
            pl.BlockSpec((FACTOR_WIDTH, block, 128), lambda t, s: (0, t, 0)),
            pl.BlockSpec((FACTOR_WIDTH, block, 128), lambda t, s: (0, t, 0)),
        ]
        + [whole((FACTOR_WIDTH, 32, 128))] * 4,
        scratch_shapes=[
            pltpu.VMEM((1024, 384), jnp.bfloat16),
            pltpu.VMEM((128, 4096), jnp.float32),
        ],
    )
    return pl.pallas_call(
        right_kernel,
        grid_spec=grid_spec,
        out_shape=[
            pltpu.HBM((FACTOR_WIDTH, 64 * FACTOR_WIDTH, 128), jnp.bfloat16),
            pltpu.HBM((FACTOR_WIDTH, 64 * FACTOR_WIDTH, 128), jnp.bfloat16),
        ]
        + [pltpu.HBM((FACTOR_WIDTH, 32, 128), jnp.float32)] * 4,
        compiler_params=pltpu.CompilerParams(vmem_limit_bytes=48 * 2**20),
        cost_estimate=pl.CostEstimate(flops=COST, bytes_accessed=COST, transcendentals=0),
        name="right_products",
    )(place, pair_grad, far_grad, *[pltpu.with_memory_space_constraint(part, pltpu.HBM) for part in (inverse_count, weight, left)], left_far)


def left_kernel(high, low, right_0, right_1, right_2, right_3, own, far, weights):
    step = pl.program_id(0)

    @pl.when(step == 0)
    def _():
        for f in range(FACTOR_WIDTH):
            for d, right in enumerate((right_0, right_1, right_2, right_3)):
                r_high, r_low = split(right[f])
                row = f * 128 + d * 32
                weights[row : row + 32, 0:128] = r_high
                weights[row : row + 32, 128:256] = r_low

    block = slice(None)
    first = jnp.zeros((ROWS * FACTOR_WIDTH, 256), jnp.float32)
    second = jnp.zeros((ROWS * FACTOR_WIDTH, 128), jnp.float32)
    for f in range(0, FACTOR_WIDTH, 2):
        part = slice(128 * f, 128 * f + 256)
        first += dot_nn(jnp.concatenate([high[f, block], high[f + 1, block]], axis=1), weights[part])
        second += dot_nn(jnp.concatenate([low[f, block], low[f + 1, block]], axis=1), weights[part, 0:128])
    found = first[:, :128] + first[:, 128:] + second
    half = pl.num_programs(0) // 2

    @pl.when(step < half)
    def _():
        far[...] = found

    @pl.when(step >= half)
    def _():
        own[...] = found


def left_products(high, low, rights):
    block = ROWS * FACTOR_WIDTH
    steps = 64 // ROWS
    half = steps // 2
    rows = pl.BlockSpec((FACTOR_WIDTH, block, 128), lambda t: (0, lax.rem(t + half, steps), 0))
    return pl.pallas_call(
        left_kernel,
        grid=(steps,),
        in_specs=[rows, rows] + [whole((FACTOR_WIDTH, 32, 128))] * 4,
        out_specs=[
            pl.BlockSpec((block, 128), lambda t: (jnp.maximum(t - half, 0), 0)),
            pl.BlockSpec((block, 128), lambda t: (jnp.minimum(t, half - 1), 0)),
        ],
        out_shape=[pltpu.HBM((32 * FACTOR_WIDTH, 128), jnp.float32)] * 2,
        scratch_shapes=[pltpu.VMEM((FACTOR_WIDTH * 128, 256), jnp.bfloat16)],
        compiler_params=pltpu.CompilerParams(vmem_limit_bytes=40 * 2**20),
        cost_estimate=pl.CostEstimate(flops=COST, bytes_accessed=COST, transcendentals=0),
        name="left_products",
    )(high, low, pltpu.with_memory_space_constraint(rights[0], pltpu.HBM), *rights[1:])


def swap_core(values):
    return lax.ppermute(values, "core", [(0, 1), (1, 0)])


def fetch_chip(values, distance):
    return lax.ppermute(values, "x", [((i + distance) % 4, i) for i in range(4)])


def send_chip(values, distance):
    return lax.ppermute(values, "x", [(i, (i + distance) % 4) for i in range(4)])


def exchange(send):
    return lax.all_to_all(send, "seq", 0, 0, tiled=True)


def body(
    homolog_features,
    homolog_loss_slope,
    pair_update_gradient,
    alignment_mask,
    asking_matrix,
    key_weight,
    content_matrix,
    sigmoid_filter_matrix,
    final_mixing_matrix,
    first_factor_matrix,
    second_factor_matrix,
    pair_weight,
):
    peers = lax.axis_size("seq")
    share = 64 // peers
    counted = -(-(17 + share) // 8) * 8
    block = RES * 8 // peers
    shared = 24 + block + (0 if share == 2 else share)
    x, core = lax.axis_index("x"), lax.axis_index("core")
    place = jnp.stack([x, core]).astype(jnp.int32)
    mask_core = swap_core(alignment_mask)
    mask_chips = [fetch_chip(alignment_mask, d) for d in (1, 2, 3)]
    weight = pair_weight.reshape(FACTOR_WIDTH, FACTOR_WIDTH, 128).swapaxes(0, 1).reshape(1024, 128)
    value_gate = jnp.concatenate([content_matrix, sigmoid_filter_matrix], axis=1).T
    key_value = jnp.concatenate([key_weight, content_matrix], axis=1)
    factors = jnp.concatenate([first_factor_matrix, second_factor_matrix], axis=1)

    flat, heads, stat = (RES * 64, SEQ), (RES * 8, SEQ), (RES, SEQ)
    x0t, inverse, present, send = call(
        norm_kernel, [flat, stat, stat, (peers, counted, 128)], homolog_features, alignment_mask
    )
    (send,) = call(pair_kernel, [(peers, counted, 128)], send, alignment_mask, mask_core, *mask_chips, free=(2, 3, 4, 5))
    got = exchange(send)
    keys, values, gate, m0t, slope_t = call(
        project_kernel, [heads, heads, flat, flat, flat],
        x0t, homolog_features, homolog_loss_slope, key_weight.T, value_gate, free=(3, 4),
    )
    slope_t, pair_grad = lax.optimization_barrier((slope_t, pair_update_gradient.reshape(32, 4, 2, 32, 128)))
    far_grad = swap_core(lax.dynamic_index_in_dim(pair_grad, 1 - core, 2, keepdims=False))
    got, far_grad, weight, place = lax.optimization_barrier((got, far_grad, weight, place))
    raw, local, counts, query_blocks, send = call(
        score_kernel,
        [heads, (RES, 16), stat, (RES * 8, RES * 8), (peers, shared, 128)],
        got, keys, values, present, asking_matrix, free=(0,),
    )
    got = exchange(send)
    probs, attended, mixed, x1t, inverse_mid, left, right, inverse_count, moments = call(
        attend_kernel,
        [heads, (RES, 64), flat, flat, stat, (RES * 32, SEQ), (FACTOR_WIDTH, RES, SEQ), (64, 128), (block, 128)],
        got, local, raw, m0t, gate, present, final_mixing_matrix.T, factors.T, late=(3, 4), free=(0, 6, 7),
        scratch=[pltpu.VMEM((RES * 32, SEQ), F32)],
    )
    rights = [right] + [fetch_chip(right, d) for d in (1, 2, 3)]
    high, low, right_own, right_1, right_2, right_3 = right_products(
        place, pair_grad, far_grad, inverse_count, weight, left, swap_core(left)
    )
    right_sent = [send_chip(part, d) for d, part in ((2, right_2), (1, right_1), (3, right_3))]
    left_own, left_far = left_products(high, low, rights)
    left_far = [swap_core(part) for part in jnp.split(left_far, 2)]
    mid, out_grad, send = call(
        middle_kernel, [flat, flat, (peers, 16 + block, 128)],
        left_own, *left_far, right_own, *right_sent,
        moments, x1t, inverse_mid, present, slope_t, gate, factors, final_mixing_matrix, free=(1, 2, 4, 5, 6, 13),
        scratch=[pltpu.VMEM((RES * 32, SEQ), F32)],
    )
    got = exchange(send)
    (gate_grad,) = call(gate_back_kernel, [flat], out_grad, mixed, gate, sigmoid_filter_matrix)
    (out,) = call(
        finish_kernel, [(SEQ, RES * 64)],
        got, attended, probs, keys, values, query_blocks, gate_grad, key_value, counts, asking_matrix,
        present, x0t, inverse, mid, late=(6, 11, 13), free=(0, 7),
    )
    return out


def solution(mesh):
    grid = Mesh(mesh.devices.reshape(mesh.devices.shape[0], 4, 2), ("seq", "x", "core"))
    res = ("x", "core")
    in_specs = (
        P("seq", res),
        P("seq", res),
        P(res, None, None),
        P("seq", res),
        P(),
        P(),
        P(),
        P(),
        P(),
        P(),
        P(),
        P(),
    )
    return jax.shard_map(body, mesh=grid, in_specs=in_specs, out_specs=P("seq", res), check_vma=False)
```

```python
import functools

import jax
import jax.numpy as jnp
from jax import lax
from jax.experimental import pallas as pl
from jax.experimental.pallas import tpu as pltpu
from jax.sharding import Mesh
from jax.sharding import PartitionSpec as P

FEATURE_DEPTH = 64
HEAD_COUNT = 8
HEAD_SIZE = 8
FACTOR_WIDTH = 32
RES = 32
SEQ = 128

EPSILON = 1e-05
MASK_FILL = -1000000000.0
PRECISE = lax.Precision.HIGHEST
F32 = jnp.float32


def split(values):
    high = values.astype(jnp.bfloat16)
    low = (values - high.astype(jnp.float32)).astype(jnp.bfloat16)
    return high, low


def dot_nn(a, b):
    return lax.dot_general(a, b, (((1,), (0,)), ((), ())), preferred_element_type=jnp.float32)


def dot_nt(a, b):
    return lax.dot_general(a, b, (((1,), (1,)), ((), ())), preferred_element_type=jnp.float32)


def exact_nn(a, b):
    return lax.dot_general(a, b, (((1,), (0,)), ((), ())), preferred_element_type=F32, precision=PRECISE)


def exact_nt(a, b):
    return lax.dot_general(a, b, (((1,), (1,)), ((), ())), preferred_element_type=F32, precision=PRECISE)


def lhs_parts(weight):
    high, low = split(weight)
    return jnp.concatenate([high, high, low], axis=1)


def project(parts, values):
    high, low = split(values)
    return dot_nn(parts, jnp.concatenate([high, low, high], axis=0))


def row_lane(shape):
    return lax.broadcasted_iota(jnp.int32, shape, 0), lax.broadcasted_iota(jnp.int32, shape, 1)


def sum_lanes_01(ones, values):
    high, rest = values.astype(jnp.bfloat16), values
    rest = rest - high.astype(F32)
    mid = rest.astype(jnp.bfloat16)
    low = (rest - mid.astype(F32)).astype(jnp.bfloat16)
    return dot_nt(ones, high) + dot_nt(ones, mid) + dot_nt(ones, low)


def own_blocks(values):
    rows, _ = row_lane((RES, 128))
    total = jnp.zeros((RES, 128), F32)
    for pair in range(RES // 2):
        total = jnp.where(rows // 2 == pair, values[:, 128 * pair : 128 * pair + 128], total)
    return jnp.where(rows[:, :64] % 2 == 0, total[:, :64], total[:, 64:])


def pack(values):
    return jnp.concatenate([values[:16], values[16:]], axis=1)


def unpack(values):
    return jnp.concatenate([values[:, :64], values[:, 64:]], axis=0)


def over_heads(values):
    return jnp.broadcast_to(values[:, None, :], (RES, 8, values.shape[1])).reshape(RES * 8, values.shape[1])


def head_column(values):
    rows, lanes = row_lane((RES * 8, values.shape[1]))
    return jnp.sum(jnp.where(rows % 8 == lanes, over_heads(values), 0.0), axis=1, keepdims=True)


def head_blocks(values):
    rows, lanes = row_lane((RES * 8, 64))
    picked = jnp.where(rows % 8 == lanes // 8, over_heads(values), 0.0)
    r, c = row_lane((64, RES * 8))
    spread = exact_nn(picked, (r % 8 == c % 8).astype(F32))
    rows, lanes = row_lane((RES * 8, RES * 8))
    return jnp.where(rows // 8 == lanes // 8, spread, 0.0)


def fold_blocks(values):
    rows, lanes = row_lane((RES * 8, RES * 8))
    r, c = row_lane((RES * 8, 128))
    fold = jnp.where((r % 8 == c % 8) & (c < 64), 1.0, 0.0)
    return exact_nn(jnp.where(rows // 8 == lanes // 8, values, 0.0), fold)


def sum_heads(values):
    return jnp.sum(values.reshape(RES, 8, values.shape[1]), axis=1)


def send_all(send, rows, values):
    send[:, rows, :] = jnp.broadcast_to(values[None], (send.shape[0],) + values.shape)


def norm_kernel(m0, mask, x0t, inverse, present, send):
    shown = mask[...].astype(F32).T
    present[...] = shown
    for pair in range(RES // 2):
        block = m0[:, 128 * pair : 128 * pair + 128].T
        for k in range(2):
            part = block[64 * k : 64 * k + 64]
            center = part - jnp.mean(part, axis=0, keepdims=True)
            scale = lax.rsqrt(jnp.mean(center * center, axis=0, keepdims=True) + EPSILON)
            row = 2 * pair + k
            inverse[row : row + 1] = scale
            x0t[64 * row : 64 * row + 64] = center * scale
    ones = shown.astype(jnp.bfloat16)
    sums = own_blocks(sum_lanes_01(ones, x0t[...]))
    counts = dot_nt(jnp.ones((16, SEQ), jnp.bfloat16), ones)
    send[...] = jnp.zeros_like(send)
    send_all(send, slice(0, 16), pack(sums))
    send_all(send, slice(16, 17), jnp.concatenate([counts[0:1], jnp.zeros((1, 96), F32)], axis=1))


def pair_kernel(sent, mask, mask_core, mask_1, mask_2, mask_3, send):
    send[...] = sent[...]
    own = mask[...].astype(F32).T.astype(jnp.bfloat16)
    rows = jnp.concatenate([own, mask_core[...].astype(F32).T.astype(jnp.bfloat16)], axis=0)
    columns = jnp.concatenate(
        [own] + [part[...].astype(F32).T.astype(jnp.bfloat16) for part in (mask_1, mask_2, mask_3)], axis=0
    )
    count = dot_nt(rows, columns)
    share = 64 // send.shape[0]
    for peer in range(send.shape[0]):
        send[peer, 17 : 17 + share, :] = count[share * peer : share * peer + share]


def project_kernel(x0t, m0, slope, key, value_gate, keys, values, gate, m0t, slope_t):
    parts = lhs_parts(value_gate[...])
    for pair in range(RES // 2):
        m0t[128 * pair : 128 * pair + 128] = m0[:, 128 * pair : 128 * pair + 128].T
        slope_t[128 * pair : 128 * pair + 128] = slope[:, 128 * pair : 128 * pair + 128].T
        row = 128 * pair
        both = jnp.concatenate([x0t[row : row + 64], x0t[row + 64 : row + 128]], axis=1)
        found = project(parts, both)
        key_rows = exact_nn(key[...], both)
        gates = jax.nn.sigmoid(found[8:72])
        for k in range(2):
            lanes = slice(SEQ * k, SEQ * k + SEQ)
            head = 8 * (2 * pair + k)
            keys[head : head + 8] = key_rows[:, lanes]
            values[head : head + 8] = found[0:8, lanes]
            gate[row + 64 * k : row + 64 * k + 64] = gates[:, lanes]


def score_kernel(got, keys, values, present, asking, weights, local, counts, query_blocks, send):
    sums = jnp.sum(got[...], axis=0)
    r, c = row_lane((RES, RES))
    count = jnp.sum(jnp.where(r == c, jnp.broadcast_to(sums[16:17, :RES], (RES, RES)), 0.0), axis=1, keepdims=True)
    counts[...] = jnp.broadcast_to(count, (RES, 128))
    queries = exact_nn(unpack(sums[:16]) / count, asking[...]) * HEAD_SIZE ** (-0.5)
    blocks = head_blocks(queries)
    query_blocks[...] = blocks
    scores = exact_nn(blocks, keys[...])
    scores = jnp.where(over_heads(present[...]) > 0, scores, MASK_FILL)
    top = jnp.max(scores, axis=1, keepdims=True)
    raw = jnp.exp(scores - top)
    weights[...] = raw
    total = jnp.sum(raw, axis=1, keepdims=True)
    rows, lanes = row_lane((RES * 8, 64))
    own_head = rows % 8 == lanes // 8
    weighted = sum_heads(jnp.where(own_head, fold_blocks(exact_nt(raw, values[...]))[:, :64], 0.0))
    send_all(send, slice(0, 16), pack(weighted))
    rows, lanes = row_lane((RES * 8, 16))
    stats = jnp.where(lanes == rows % 8, top, jnp.where(lanes == 8 + rows % 8, total, 0.0))
    stats = sum_heads(stats)
    local[...] = stats
    share = 64 // send.shape[0]
    pairs = sums[17 : 17 + share]
    stats = jnp.concatenate([stats[8 * k : 8 * k + 8] for k in range(4)], axis=1)
    if share == 2:
        right = jnp.concatenate([pairs[:, :64], pairs[:, 64:], jnp.zeros((4, 64), F32)], axis=0)
    else:
        right = jnp.zeros((8, 64), F32)
        send_all(send, slice(send.shape[1] - share, send.shape[1]), pairs)
    send_all(send, slice(16, 24), jnp.concatenate([stats, right], axis=1))
    products = raw.reshape(RES, 8, 1, SEQ) * values[...].reshape(RES, 1, 8, SEQ)
    products = products.reshape(RES * 64, SEQ)
    half = RES // 2
    rows, lanes = row_lane((half * 64, 128))
    same = rows // 64 == lanes // 8
    r, c = row_lane((128, 64))
    fold = jnp.where(r % 8 == c % 8, 1.0, 0.0).astype(jnp.bfloat16)
    moments = []
    for k in range(2):
        a_high, a_low = split(products[half * 64 * k : half * 64 * (k + 1)])
        b_high, b_low = split(keys[128 * k : 128 * k + 128])
        found = dot_nt(
            jnp.concatenate([a_high, a_high, a_low], axis=1), jnp.concatenate([b_high, b_low, b_high], axis=1)
        )
        f_high, f_low = split(jnp.where(same, found, 0.0))
        spread = dot_nn(f_high, fold) + dot_nn(f_low, fold)
        spread = jnp.where(rows[:, :64] % 8 == lanes[:, :64] // 8, spread, 0.0)
        moments.append(jnp.sum(spread.reshape(half * 8, 8, 64), axis=1))
    moments = jnp.concatenate(moments, axis=0)
    firsts = fold_blocks(exact_nt(raw, keys[...]))
    rows, lanes = row_lane((RES * 8, 64))
    rest = jnp.where(lanes < 8, firsts[:, :64], jnp.where(lanes == 8, top, jnp.where(lanes == 9, total, 0.0)))
    block = jnp.concatenate([moments, rest], axis=1)
    size = RES * 8 // send.shape[0]
    send[:, 24 : 24 + size, :] = block.reshape(send.shape[0], size, 128)


def attend_kernel(
    got, local, raw, m0t, gate, present, mixing, factors,
    probs, attended, mixed, x1t, inverse_mid, left, right, inverse_count, moments, scratch, arrive,
):
    peers = got.shape[0]
    share = 64 // peers
    for peer in range(peers):
        if share == 2:
            pairs = jnp.concatenate([got[peer, 16:18, 64:], got[peer, 18:20, 64:]], axis=1)
        else:
            pairs = got[peer, got.shape[1] - share :, :]
        inverse_count[share * peer : share * peer + share] = 1.0 / pairs
    weighted = jnp.concatenate([got[:, 0:16, 0:64], got[:, 0:16, 64:128]], axis=1)
    stats = jnp.concatenate([got[:, 16:24, 16 * k : 16 * k + 16] for k in range(4)], axis=1)
    tops = stats[:, :, 0:8]
    top = jnp.max(tops, axis=0)
    factor = jnp.exp(tops - top[None])
    total = jnp.sum(factor * stats[:, :, 8:16], axis=0)
    r, c = row_lane((8, 64))
    expand = jnp.where(r == c // 8, 1.0, 0.0)
    high, low = split(factor.reshape(peers * RES, 8))
    wide = expand.astype(jnp.bfloat16)
    factor = (dot_nn(high, wide) + dot_nn(low, wide)).reshape(peers, RES, 64)
    heads = jnp.sum(factor * weighted, axis=0) / exact_nn(total, expand)
    probs[...] = raw[...] * head_column(jnp.exp(local[:, 0:8] - top) / total)
    attended[...] = heads
    size = RES * 8 // peers
    block = got[:, 24 : 24 + size, :]
    tops = block[:, :, 72:73]
    block = jnp.sum(jnp.exp(tops - jnp.max(tops, axis=0)[None]) * block, axis=0)
    lanes = lax.broadcasted_iota(jnp.int32, block.shape, 1)
    moments[...] = jnp.where(lanes < 72, block / block[:, 73:74], 0.0)
    heads_t = heads.T
    mixing_parts = lhs_parts(mixing[...])
    factor_parts = lhs_parts(factors[...])
    arrive()
    for pair in range(RES // 2):
        shown, used, base = [], [], []
        for k in range(2):
            i = 2 * pair + k
            rows = slice(64 * i, 64 * i + 64)
            use = gate[rows] * heads_t[:, i : i + 1]
            mixed[rows] = use
            used.append(use)
            base.append(m0t[rows])
            shown.append(present[i : i + 1])
        middle = jnp.concatenate(base, axis=1) + project(mixing_parts, jnp.concatenate(used, axis=1))
        center = middle - jnp.mean(middle, axis=0, keepdims=True)
        scale = lax.rsqrt(jnp.mean(center * center, axis=0, keepdims=True) + EPSILON)
        normed = center * scale
        found = project(factor_parts, normed) * jnp.concatenate(shown, axis=1)
        for k in range(2):
            i = 2 * pair + k
            lanes = slice(SEQ * k, SEQ * k + SEQ)
            x1t[64 * i : 64 * i + 64] = normed[:, lanes]
            inverse_mid[i : i + 1] = scale[:, lanes]
            left[32 * i : 32 * i + 32] = found[:32, lanes]
            scratch[32 * i : 32 * i + 32] = found[32:, lanes]
    for f in range(FACTOR_WIDTH):
        right[f] = scratch[pl.ds(f, RES, stride=FACTOR_WIDTH), :]


def middle_kernel(
    left_own, left_far_0, left_far_1, right_own, right_1, right_2, right_3, moments, x1t, inverse_mid, present, slope_t, gate,
    factors_back, mixing_back, mid, out_grad, send, scratch,
):
    for f in range(FACTOR_WIDTH):
        scratch[32 * f : 32 * f + 32] = (right_own[f] + right_1[f]) + (right_2[f] + right_3[f])
    parts = lhs_parts(factors_back[...])
    mixing_parts = lhs_parts(mixing_back[...])
    ones = jnp.ones((16, SEQ), jnp.bfloat16)
    sums = []
    for pair in range(RES // 2):
        grads = []
        for k in range(2):
            i = 2 * pair + k
            rows = slice(32 * i, 32 * i + 32)
            left_far = left_far_0 if i < RES // 2 else left_far_1
            near = slice(32 * (i % 16), 32 * (i % 16) + 32)
            both = jnp.concatenate(
                [left_own[rows] + left_far[near], scratch[pl.ds(i, FACTOR_WIDTH, stride=RES), :]], axis=0
            )
            grads.append(both * present[i : i + 1])
        mid_in = project(parts, jnp.concatenate(grads, axis=1))
        rows = slice(128 * pair, 128 * pair + 128)
        normed = jnp.concatenate([x1t[128 * pair : 128 * pair + 64], x1t[128 * pair + 64 : 128 * pair + 128]], axis=1)
        scale = jnp.concatenate([inverse_mid[2 * pair : 2 * pair + 1], inverse_mid[2 * pair + 1 : 2 * pair + 2]], axis=1)
        back = scale * (
            mid_in
            - jnp.mean(mid_in, axis=0, keepdims=True)
            - normed * jnp.mean(mid_in * normed, axis=0, keepdims=True)
        )
        back = back + jnp.concatenate(
            [slope_t[128 * pair : 128 * pair + 64], slope_t[128 * pair + 64 : 128 * pair + 128]], axis=1
        )
        grad = project(mixing_parts, back)
        gated = []
        for k in range(2):
            lanes = slice(SEQ * k, SEQ * k + SEQ)
            rows = slice(128 * pair + 64 * k, 128 * pair + 64 * k + 64)
            mid[rows] = back[:, lanes]
            out_grad[rows] = grad[:, lanes]
            gated.append(grad[:, lanes] * gate[rows])
        sums.append(sum_lanes_01(ones, jnp.concatenate(gated, axis=0)))
    sums = [jnp.concatenate([part, part], axis=0) for part in sums]
    send_all(send, slice(0, 16), pack(own_blocks(jnp.concatenate(sums, axis=1))))
    send_all(send, slice(16, 16 + moments.shape[0]), moments[...])


def gate_back_kernel(out_grad, mixed, gate, filter_weight, x_grad):
    parts = lhs_parts(filter_weight[...])
    for pair in range(RES // 2):
        both = []
        for k in range(2):
            rows = slice(128 * pair + 64 * k, 128 * pair + 64 * k + 64)
            both.append(out_grad[rows] * mixed[rows] * (1.0 - gate[rows]))
        found = project(parts, jnp.concatenate(both, axis=1))
        for k in range(2):
            x_grad[128 * pair + 64 * k : 128 * pair + 64 * k + 64] = found[:, SEQ * k : SEQ * k + SEQ]


def finish_kernel(
    got, attended, probs, keys, values, query_blocks, partial, key_value, counts, asking, present, x0t, inverse, mid, out, arrive
):
    att_grad = unpack(jnp.sum(got[:, 0:16, :], axis=0))
    moments = got[:, 16:, :].reshape(RES * 8, 128)
    rows, lanes = row_lane((RES * 8, 64))
    own_head = rows % 8 == lanes // 8
    along = jnp.sum(jnp.where(own_head, over_heads(att_grad * attended[...]), 0.0), axis=1, keepdims=True)
    r, c = row_lane((64, 64))
    spread = exact_nn(jnp.where(own_head, over_heads(att_grad), 0.0), (r % 8 == c // 8).astype(F32))
    both = jnp.concatenate([spread * moments[:, :64], -along * moments[:, 64:]], axis=1)
    r, c = row_lane((128, 64))
    query_grad = exact_nn(both, jnp.where((r < 72) & (r % 8 == c % 8), 1.0, 0.0))
    query_grad = sum_heads(jnp.where(own_head, query_grad, 0.0)) * HEAD_SIZE ** (-0.5)
    mean_grad = (exact_nt(query_grad, asking[...]) / counts[:, :64]).T

    blocks = head_blocks(att_grad)
    score_grad = probs[...] * (exact_nn(blocks, values[...]) - along)
    key_grad = exact_nn(query_blocks[...].T, score_grad)
    value_grad = exact_nn(blocks.T, probs[...])
    parts = lhs_parts(key_value[...])
    arrive()
    for pair in range(RES // 2):
        both = []
        for k in range(2):
            rows = slice(16 * pair + 8 * k, 16 * pair + 8 * k + 8)
            both.append(jnp.concatenate([key_grad[rows], value_grad[rows]], axis=0))
        found = project(parts, jnp.concatenate(both, axis=1))
        done = []
        for k in range(2):
            i = 2 * pair + k
            rows = slice(64 * i, 64 * i + 64)
            grad = partial[rows] + found[:, SEQ * k : SEQ * k + SEQ] + mean_grad[:, i : i + 1] * present[i : i + 1]
            normed = x0t[rows]
            back = inverse[i : i + 1] * (
                grad - jnp.mean(grad, axis=0, keepdims=True) - normed * jnp.mean(grad * normed, axis=0, keepdims=True)
            )
            done.append(mid[rows] + back)
        out[:, 128 * pair : 128 * pair + 128] = jnp.concatenate(done, axis=0).T


def whole(shape):
    return pl.BlockSpec(shape, lambda *_: (0,) * len(shape))


def staged(kernel, count, late, *refs):
    operands, rest = refs[: count[0]], refs[count[0] :]
    results, rest = rest[: count[1]], rest[count[1] :]
    total = count[0] + count[1]
    held, sems, scratch = rest[:total], rest[total], rest[total + 1 :]
    copies = [pltpu.make_async_copy(operands[k], held[k], sems.at[k]) for k in range(count[0])]
    for copy in copies:
        copy.start()

    def arrive():
        for k in late:
            copies[k].wait()

    for k in range(count[0]):
        if k not in late:
            copies[k].wait()
    kernel(*held, *scratch, *([arrive] if late else []))
    copies = [
        pltpu.make_async_copy(held[count[0] + k], results[k], sems.at[count[0] + k]) for k in range(count[1])
    ]
    for copy in copies:
        copy.start()
    for copy in copies:
        copy.wait()


def call(kernel, shapes, *operands, scratch=(), late=(), free=(), vmem=40):
    shapes = [jax.ShapeDtypeStruct(shape, F32) for shape in shapes]
    size = sum(4 * array.size for array in shapes) + sum(array.size * array.dtype.itemsize for array in operands)
    arrays = list(operands) + shapes
    return pl.pallas_call(
        functools.partial(staged, kernel, (len(operands), len(shapes)), late),
        in_specs=[
            pl.BlockSpec(memory_space=pl.ANY if k in free else pltpu.HBM) for k in range(len(operands))
        ],
        out_specs=[pl.BlockSpec(memory_space=pltpu.HBM)] * len(shapes),
        out_shape=[pltpu.HBM(array.shape, array.dtype) for array in shapes],
        scratch_shapes=[pltpu.VMEM(array.shape, array.dtype) for array in arrays]
        + [pltpu.SemaphoreType.DMA((len(arrays),))]
        + list(scratch),
        compiler_params=pltpu.CompilerParams(vmem_limit_bytes=vmem * 2**20),
        cost_estimate=pl.CostEstimate(flops=100_000_000, bytes_accessed=int(size), transcendentals=0),
        name=kernel.__name__,
    )(
        *[
            array if k in free else pltpu.with_memory_space_constraint(array, pltpu.HBM)
            for k, array in enumerate(operands)
        ]
    )


ROWS = 8
COST = 1000


def right_kernel(
    place, own_g, far_g, inverse_count, weight, left, left_far, high, low, out_0, out_1, out_2, out_3, weights, total
):
    step = pl.program_id(0)
    x = place[0]

    @pl.when(step == 0)
    def _():
        w_high, w_low = split(weight[...])
        weights[:, 0:128] = w_high
        weights[:, 128:256] = w_low
        weights[:, 256:384] = w_high
        total[...] = jnp.zeros_like(total)

    near = step < pl.num_programs(0) // 2
    inverse_column = inverse_count[...].T
    for pair in range(ROWS // 2):
        blocks = []
        for row in (2 * pair, 2 * pair + 1):
            for d in range(4):
                chip = lax.rem(x + d, 4)
                scale = inverse_column[32 * d : 32 * d + 32, row : row + 1]
                blocks.append(scale * jnp.where(near, own_g[row, chip, 0], far_g[row, chip, 0]))
        g_high, g_low = split(jnp.concatenate(blocks, axis=0))
        grads = dot_nt(weights[...], jnp.concatenate([g_high, g_high, g_low], axis=1))
        grads_high, grads_low = split(grads)
        for k in range(2):
            row = (2 * pair + k) * FACTOR_WIDTH
            rows, lanes = slice(row, row + FACTOR_WIDTH), slice(128 * k, 128 * k + 128)
            high[:, rows, :] = grads_high[:, lanes].reshape(FACTOR_WIDTH, FACTOR_WIDTH, 128)
            low[:, rows, :] = grads_low[:, lanes].reshape(FACTOR_WIDTH, FACTOR_WIDTH, 128)
    l_high, l_low = split(jnp.where(near, left[...], left_far[...]).T)
    block = slice(None)
    stacked = jnp.concatenate([l_high, l_low], axis=0)
    for f in range(0, FACTOR_WIDTH, 2):
        first = dot_nn(stacked, jnp.concatenate([high[f, block], high[f + 1, block]], axis=1))
        second = dot_nn(l_high, jnp.concatenate([low[f, block], low[f + 1, block]], axis=1))
        total[:, 128 * f : 128 * f + 256] += first[:128] + first[128:] + second

    @pl.when(step == pl.num_programs(0) - 1)
    def _():
        for f in range(FACTOR_WIDTH):
            block = total[:, 128 * f : 128 * f + 128].T
            for d, out in enumerate((out_0, out_1, out_2, out_3)):
                out[f] = block[32 * d : 32 * d + 32]


def right_products(place, pair_grad, far_grad, inverse_count, weight, left, left_far):
    block = ROWS * FACTOR_WIDTH
    steps = 64 // ROWS
    half = steps // 2
    grid_spec = pltpu.PrefetchScalarGridSpec(
        num_scalar_prefetch=1,
        grid=(steps,),
        in_specs=[
            pl.BlockSpec((ROWS, 4, 1, 32, 128), lambda t, s: (jnp.minimum(t, half - 1), 0, s[1], 0, 0)),
            pl.BlockSpec((ROWS, 4, 1, 32, 128), lambda t, s: (jnp.maximum(t - half, 0), 0, s[1], 0, 0)),
            pl.BlockSpec((ROWS, 128), lambda t, s: (t, 0)),
            pl.BlockSpec((1024, 128), lambda t, s: (0, 0)),
            pl.BlockSpec((block, 128), lambda t, s: (jnp.minimum(t, half - 1), 0)),
            pl.BlockSpec((block, 128), lambda t, s: (jnp.maximum(t - half, 0), 0)),
        ],
        out_specs=[
            pl.BlockSpec((FACTOR_WIDTH, block, 128), lambda t, s: (0, t, 0)),
            pl.BlockSpec((FACTOR_WIDTH, block, 128), lambda t, s: (0, t, 0)),
        ]
        + [whole((FACTOR_WIDTH, 32, 128))] * 4,
        scratch_shapes=[
            pltpu.VMEM((1024, 384), jnp.bfloat16),
            pltpu.VMEM((128, 4096), jnp.float32),
        ],
    )
    return pl.pallas_call(
        right_kernel,
        grid_spec=grid_spec,
        out_shape=[
            pltpu.HBM((FACTOR_WIDTH, 64 * FACTOR_WIDTH, 128), jnp.bfloat16),
            pltpu.HBM((FACTOR_WIDTH, 64 * FACTOR_WIDTH, 128), jnp.bfloat16),
        ]
        + [pltpu.HBM((FACTOR_WIDTH, 32, 128), jnp.float32)] * 4,
        compiler_params=pltpu.CompilerParams(vmem_limit_bytes=48 * 2**20),
        cost_estimate=pl.CostEstimate(flops=COST, bytes_accessed=COST, transcendentals=0),
        name="right_products",
    )(place, pair_grad, far_grad, *[pltpu.with_memory_space_constraint(part, pltpu.HBM) for part in (inverse_count, weight, left)], left_far)


def left_kernel(high, low, right_0, right_1, right_2, right_3, own, far_0, far_1, weights):
    step = pl.program_id(0)

    @pl.when(step == 0)
    def _():
        for f in range(FACTOR_WIDTH):
            for d, right in enumerate((right_0, right_1, right_2, right_3)):
                r_high, r_low = split(right[f])
                row = f * 128 + d * 32
                weights[row : row + 32, 0:128] = r_high
                weights[row : row + 32, 128:256] = r_low

    block = slice(None)
    first = jnp.zeros((ROWS * FACTOR_WIDTH, 256), jnp.float32)
    second = jnp.zeros((ROWS * FACTOR_WIDTH, 128), jnp.float32)
    for f in range(0, FACTOR_WIDTH, 2):
        part = slice(128 * f, 128 * f + 256)
        first += dot_nn(jnp.concatenate([high[f, block], high[f + 1, block]], axis=1), weights[part])
        second += dot_nn(jnp.concatenate([low[f, block], low[f + 1, block]], axis=1), weights[part, 0:128])
    found = first[:, :128] + first[:, 128:] + second
    half = pl.num_programs(0) // 2

    @pl.when(step < half // 2)
    def _():
        far_0[...] = found

    @pl.when((step >= half // 2) & (step < half))
    def _():
        far_1[...] = found

    @pl.when(step >= half)
    def _():
        own[...] = found


def left_products(high, low, rights):
    block = ROWS * FACTOR_WIDTH
    steps = 64 // ROWS
    half = steps // 2
    rows = pl.BlockSpec((FACTOR_WIDTH, block, 128), lambda t: (0, lax.rem(t + half, steps), 0))
    return pl.pallas_call(
        left_kernel,
        grid=(steps,),
        in_specs=[rows, rows] + [whole((FACTOR_WIDTH, 32, 128))] * 4,
        out_specs=[
            pl.BlockSpec((block, 128), lambda t: (jnp.maximum(t - half, 0), 0)),
            pl.BlockSpec((block, 128), lambda t: (jnp.minimum(t, half // 2 - 1), 0)),
            pl.BlockSpec((block, 128), lambda t: (jnp.clip(t - half // 2, 0, half // 2 - 1), 0)),
        ],
        out_shape=[pltpu.HBM((32 * FACTOR_WIDTH, 128), jnp.float32)]
        + [pltpu.HBM((16 * FACTOR_WIDTH, 128), jnp.float32)] * 2,
        scratch_shapes=[pltpu.VMEM((FACTOR_WIDTH * 128, 256), jnp.bfloat16)],
        compiler_params=pltpu.CompilerParams(vmem_limit_bytes=40 * 2**20),
        cost_estimate=pl.CostEstimate(flops=COST, bytes_accessed=COST, transcendentals=0),
        name="left_products",
    )(high, low, pltpu.with_memory_space_constraint(rights[0], pltpu.HBM), *rights[1:])


def swap_core(values):
    return lax.ppermute(values, "core", [(0, 1), (1, 0)])


def fetch_chip(values, distance):
    return lax.ppermute(values, "x", [((i + distance) % 4, i) for i in range(4)])


def send_chip(values, distance):
    return lax.ppermute(values, "x", [(i, (i + distance) % 4) for i in range(4)])


def exchange(send):
    return lax.all_to_all(send, "seq", 0, 0, tiled=True)


def body(
    homolog_features,
    homolog_loss_slope,
    pair_update_gradient,
    alignment_mask,
    asking_matrix,
    key_weight,
    content_matrix,
    sigmoid_filter_matrix,
    final_mixing_matrix,
    first_factor_matrix,
    second_factor_matrix,
    pair_weight,
):
    peers = lax.axis_size("seq")
    share = 64 // peers
    counted = -(-(17 + share) // 8) * 8
    block = RES * 8 // peers
    shared = 24 + block + (0 if share == 2 else share)
    x, core = lax.axis_index("x"), lax.axis_index("core")
    place = jnp.stack([x, core]).astype(jnp.int32)
    mask_core = swap_core(alignment_mask)
    mask_chips = [fetch_chip(alignment_mask, d) for d in (1, 2, 3)]
    weight = pair_weight.reshape(FACTOR_WIDTH, FACTOR_WIDTH, 128).swapaxes(0, 1).reshape(1024, 128)
    value_gate = jnp.concatenate([content_matrix, sigmoid_filter_matrix], axis=1).T
    key_value = jnp.concatenate([key_weight, content_matrix], axis=1)
    factors = jnp.concatenate([first_factor_matrix, second_factor_matrix], axis=1)

    flat, heads, stat = (RES * 64, SEQ), (RES * 8, SEQ), (RES, SEQ)
    x0t, inverse, present, send = call(
        norm_kernel, [flat, stat, stat, (peers, counted, 128)], homolog_features, alignment_mask
    )
    (send,) = call(pair_kernel, [(peers, counted, 128)], send, alignment_mask, mask_core, *mask_chips, free=(2, 3, 4, 5))
    x0t, send, pair_grad = lax.optimization_barrier((x0t, send, pair_update_gradient))
    far_grad = swap_core(pair_grad).reshape(32, 4, 2, 32, 128)
    pair_grad = pair_grad.reshape(32, 4, 2, 32, 128)
    got = exchange(send)
    keys, values, gate, m0t, slope_t = call(
        project_kernel, [heads, heads, flat, flat, flat],
        x0t, homolog_features, homolog_loss_slope, key_weight.T, value_gate, free=(3, 4),
    )
    got, far_grad, weight, place = lax.optimization_barrier((got, far_grad, weight, place))
    raw, local, counts, query_blocks, send = call(
        score_kernel,
        [heads, (RES, 16), stat, (RES * 8, RES * 8), (peers, shared, 128)],
        got, keys, values, present, asking_matrix, free=(0,),
    )
    got = exchange(send)
    probs, attended, mixed, x1t, inverse_mid, left, right, inverse_count, moments = call(
        attend_kernel,
        [heads, (RES, 64), flat, flat, stat, (RES * 32, SEQ), (FACTOR_WIDTH, RES, SEQ), (64, 128), (block, 128)],
        got, local, raw, m0t, gate, present, final_mixing_matrix.T, factors.T, late=(3, 4), free=(0, 6, 7),
        scratch=[pltpu.VMEM((RES * 32, SEQ), F32)],
    )
    rights = [right] + [fetch_chip(right, d) for d in (1, 2, 3)]
    high, low, right_own, right_1, right_2, right_3 = right_products(
        place, pair_grad, far_grad, inverse_count, weight, left, swap_core(left)
    )
    right_sent = [send_chip(part, d) for d, part in ((2, right_2), (1, right_1), (3, right_3))]
    left_own, *left_far = left_products(high, low, rights)
    left_far = [swap_core(part) for part in left_far]
    mid, out_grad, send = call(
        middle_kernel, [flat, flat, (peers, 16 + block, 128)],
        left_own, *left_far, right_own, *right_sent,
        moments, x1t, inverse_mid, present, slope_t, gate, factors, final_mixing_matrix, free=(1, 2, 4, 5, 6, 13),
        scratch=[pltpu.VMEM((RES * 32, SEQ), F32)],
    )
    got = exchange(send)
    (gate_grad,) = call(gate_back_kernel, [flat], out_grad, mixed, gate, sigmoid_filter_matrix)
    (out,) = call(
        finish_kernel, [(SEQ, RES * 64)],
        got, attended, probs, keys, values, query_blocks, gate_grad, key_value, counts, asking_matrix,
        present, x0t, inverse, mid, late=(6, 11, 13), free=(0, 7),
    )
    return out


def solution(mesh):
    grid = Mesh(mesh.devices.reshape(mesh.devices.shape[0], 4, 2), ("seq", "x", "core"))
    res = ("x", "core")
    in_specs = (
        P("seq", res),
        P("seq", res),
        P(res, None, None),
        P("seq", res),
        P(),
        P(),
        P(),
        P(),
        P(),
        P(),
        P(),
        P(),
    )
    return jax.shard_map(body, mesh=grid, in_specs=in_specs, out_specs=P("seq", res), check_vma=False)
```

```python
import functools

import jax
import jax.numpy as jnp
from jax import lax
from jax.experimental import pallas as pl
from jax.experimental.pallas import tpu as pltpu
from jax.sharding import Mesh
from jax.sharding import PartitionSpec as P

FEATURE_DEPTH = 64
HEAD_COUNT = 8
HEAD_SIZE = 8
FACTOR_WIDTH = 32
RES = 32
SEQ = 128

EPSILON = 1e-05
MASK_FILL = -1000000000.0
PRECISE = lax.Precision.HIGHEST
F32 = jnp.float32


def split(values):
    high = values.astype(jnp.bfloat16)
    low = (values - high.astype(jnp.float32)).astype(jnp.bfloat16)
    return high, low


def dot_nn(a, b):
    return lax.dot_general(a, b, (((1,), (0,)), ((), ())), preferred_element_type=jnp.float32)


def dot_nt(a, b):
    return lax.dot_general(a, b, (((1,), (1,)), ((), ())), preferred_element_type=jnp.float32)


def exact_nn(a, b):
    return lax.dot_general(a, b, (((1,), (0,)), ((), ())), preferred_element_type=F32, precision=PRECISE)


def exact_nt(a, b):
    return lax.dot_general(a, b, (((1,), (1,)), ((), ())), preferred_element_type=F32, precision=PRECISE)


def lhs_parts(weight):
    high, low = split(weight)
    return jnp.concatenate([high, high, low], axis=1)


def project(parts, values):
    high, low = split(values)
    return dot_nn(parts, jnp.concatenate([high, low, high], axis=0))


def row_lane(shape):
    return lax.broadcasted_iota(jnp.int32, shape, 0), lax.broadcasted_iota(jnp.int32, shape, 1)


def sum_lanes_01(ones, values):
    high, rest = values.astype(jnp.bfloat16), values
    rest = rest - high.astype(F32)
    mid = rest.astype(jnp.bfloat16)
    low = (rest - mid.astype(F32)).astype(jnp.bfloat16)
    return dot_nt(ones, high) + dot_nt(ones, mid) + dot_nt(ones, low)


def own_blocks(values):
    rows, _ = row_lane((RES, 128))
    total = jnp.zeros((RES, 128), F32)
    for pair in range(RES // 2):
        total = jnp.where(rows // 2 == pair, values[:, 128 * pair : 128 * pair + 128], total)
    return jnp.where(rows[:, :64] % 2 == 0, total[:, :64], total[:, 64:])


def pack(values):
    return jnp.concatenate([values[:16], values[16:]], axis=1)


def unpack(values):
    return jnp.concatenate([values[:, :64], values[:, 64:]], axis=0)


def over_heads(values):
    return jnp.broadcast_to(values[:, None, :], (RES, 8, values.shape[1])).reshape(RES * 8, values.shape[1])


def head_column(values):
    rows, lanes = row_lane((RES * 8, values.shape[1]))
    return jnp.sum(jnp.where(rows % 8 == lanes, over_heads(values), 0.0), axis=1, keepdims=True)


def head_blocks(values):
    rows, lanes = row_lane((RES * 8, 64))
    picked = jnp.where(rows % 8 == lanes // 8, over_heads(values), 0.0)
    r, c = row_lane((64, RES * 8))
    spread = exact_nn(picked, (r % 8 == c % 8).astype(F32))
    rows, lanes = row_lane((RES * 8, RES * 8))
    return jnp.where(rows // 8 == lanes // 8, spread, 0.0)


def fold_blocks(values):
    rows, lanes = row_lane((RES * 8, RES * 8))
    r, c = row_lane((RES * 8, 128))
    fold = jnp.where((r % 8 == c % 8) & (c < 64), 1.0, 0.0)
    return exact_nn(jnp.where(rows // 8 == lanes // 8, values, 0.0), fold)


def sum_heads(values):
    return jnp.sum(values.reshape(RES, 8, values.shape[1]), axis=1)


def send_all(send, rows, values):
    send[:, rows, :] = jnp.broadcast_to(values[None], (send.shape[0],) + values.shape)


def norm_kernel(m0, mask, x0t, inverse, present, send, arrive, depart):
    shown = mask[...].astype(F32).T
    present[...] = shown
    for pair in range(RES // 2):
        if pair % 4 == 0:
            arrive(pair // 4)
        block = m0[:, 128 * pair : 128 * pair + 128].T
        for k in range(2):
            part = block[64 * k : 64 * k + 64]
            center = part - jnp.mean(part, axis=0, keepdims=True)
            scale = lax.rsqrt(jnp.mean(center * center, axis=0, keepdims=True) + EPSILON)
            row = 2 * pair + k
            inverse[row : row + 1] = scale
            x0t[64 * row : 64 * row + 64] = center * scale
        if pair % 4 == 3:
            depart(pair // 4)
    ones = shown.astype(jnp.bfloat16)
    sums = own_blocks(sum_lanes_01(ones, x0t[...]))
    counts = dot_nt(jnp.ones((16, SEQ), jnp.bfloat16), ones)
    send[...] = jnp.zeros_like(send)
    send_all(send, slice(0, 16), pack(sums))
    send_all(send, slice(16, 17), jnp.concatenate([counts[0:1], jnp.zeros((1, 96), F32)], axis=1))


def pair_kernel(sent, mask, mask_core, mask_1, mask_2, mask_3, send):
    send[...] = sent[...]
    own = mask[...].astype(F32).T.astype(jnp.bfloat16)
    rows = jnp.concatenate([own, mask_core[...].astype(F32).T.astype(jnp.bfloat16)], axis=0)
    columns = jnp.concatenate(
        [own] + [part[...].astype(F32).T.astype(jnp.bfloat16) for part in (mask_1, mask_2, mask_3)], axis=0
    )
    count = dot_nt(rows, columns)
    share = 64 // send.shape[0]
    for peer in range(send.shape[0]):
        send[peer, 17 : 17 + share, :] = count[share * peer : share * peer + share]


def project_kernel(x0t, m0, slope, key, value_gate, keys, values, gate, m0t, slope_t):
    parts = lhs_parts(value_gate[...])
    for pair in range(RES // 2):
        m0t[128 * pair : 128 * pair + 128] = m0[:, 128 * pair : 128 * pair + 128].T
        slope_t[128 * pair : 128 * pair + 128] = slope[:, 128 * pair : 128 * pair + 128].T
        row = 128 * pair
        both = jnp.concatenate([x0t[row : row + 64], x0t[row + 64 : row + 128]], axis=1)
        found = project(parts, both)
        key_rows = exact_nn(key[...], both)
        gates = jax.nn.sigmoid(found[8:72])
        for k in range(2):
            lanes = slice(SEQ * k, SEQ * k + SEQ)
            head = 8 * (2 * pair + k)
            keys[head : head + 8] = key_rows[:, lanes]
            values[head : head + 8] = found[0:8, lanes]
            gate[row + 64 * k : row + 64 * k + 64] = gates[:, lanes]


def score_kernel(got, keys, values, present, asking, weights, local, counts, query_blocks, send):
    sums = jnp.sum(got[...], axis=0)
    r, c = row_lane((RES, RES))
    count = jnp.sum(jnp.where(r == c, jnp.broadcast_to(sums[16:17, :RES], (RES, RES)), 0.0), axis=1, keepdims=True)
    counts[...] = jnp.broadcast_to(count, (RES, 128))
    queries = exact_nn(unpack(sums[:16]) / count, asking[...]) * HEAD_SIZE ** (-0.5)
    blocks = head_blocks(queries)
    query_blocks[...] = blocks
    scores = exact_nn(blocks, keys[...])
    scores = jnp.where(over_heads(present[...]) > 0, scores, MASK_FILL)
    top = jnp.max(scores, axis=1, keepdims=True)
    raw = jnp.exp(scores - top)
    weights[...] = raw
    total = jnp.sum(raw, axis=1, keepdims=True)
    rows, lanes = row_lane((RES * 8, 64))
    own_head = rows % 8 == lanes // 8
    weighted = sum_heads(jnp.where(own_head, fold_blocks(exact_nt(raw, values[...]))[:, :64], 0.0))
    send_all(send, slice(0, 16), pack(weighted))
    rows, lanes = row_lane((RES * 8, 16))
    stats = jnp.where(lanes == rows % 8, top, jnp.where(lanes == 8 + rows % 8, total, 0.0))
    stats = sum_heads(stats)
    local[...] = stats
    share = 64 // send.shape[0]
    pairs = sums[17 : 17 + share]
    stats = jnp.concatenate([stats[8 * k : 8 * k + 8] for k in range(4)], axis=1)
    if share == 2:
        right = jnp.concatenate([pairs[:, :64], pairs[:, 64:], jnp.zeros((4, 64), F32)], axis=0)
    else:
        right = jnp.zeros((8, 64), F32)
        send_all(send, slice(send.shape[1] - share, send.shape[1]), pairs)
    send_all(send, slice(16, 24), jnp.concatenate([stats, right], axis=1))
    products = raw.reshape(RES, 8, 1, SEQ) * values[...].reshape(RES, 1, 8, SEQ)
    products = products.reshape(RES * 64, SEQ)
    half = RES // 2
    rows, lanes = row_lane((half * 64, 128))
    same = rows // 64 == lanes // 8
    r, c = row_lane((128, 64))
    fold = jnp.where(r % 8 == c % 8, 1.0, 0.0).astype(jnp.bfloat16)
    moments = []
    for k in range(2):
        a_high, a_low = split(products[half * 64 * k : half * 64 * (k + 1)])
        b_high, b_low = split(keys[128 * k : 128 * k + 128])
        found = dot_nt(
            jnp.concatenate([a_high, a_high, a_low], axis=1), jnp.concatenate([b_high, b_low, b_high], axis=1)
        )
        f_high, f_low = split(jnp.where(same, found, 0.0))
        spread = dot_nn(f_high, fold) + dot_nn(f_low, fold)
        spread = jnp.where(rows[:, :64] % 8 == lanes[:, :64] // 8, spread, 0.0)
        moments.append(jnp.sum(spread.reshape(half * 8, 8, 64), axis=1))
    moments = jnp.concatenate(moments, axis=0)
    firsts = fold_blocks(exact_nt(raw, keys[...]))
    rows, lanes = row_lane((RES * 8, 64))
    rest = jnp.where(lanes < 8, firsts[:, :64], jnp.where(lanes == 8, top, jnp.where(lanes == 9, total, 0.0)))
    block = jnp.concatenate([moments, rest], axis=1)
    size = RES * 8 // send.shape[0]
    send[:, 24 : 24 + size, :] = block.reshape(send.shape[0], size, 128)


def attend_kernel(
    got, local, raw, m0t, gate, present, mixing, factors,
    probs, attended, mixed, x1t, inverse_mid, left, right, inverse_count, moments, scratch, arrive, depart,
):
    peers = got.shape[0]
    share = 64 // peers
    for peer in range(peers):
        if share == 2:
            pairs = jnp.concatenate([got[peer, 16:18, 64:], got[peer, 18:20, 64:]], axis=1)
        else:
            pairs = got[peer, got.shape[1] - share :, :]
        inverse_count[share * peer : share * peer + share] = 1.0 / pairs
    weighted = jnp.concatenate([got[:, 0:16, 0:64], got[:, 0:16, 64:128]], axis=1)
    stats = jnp.concatenate([got[:, 16:24, 16 * k : 16 * k + 16] for k in range(4)], axis=1)
    tops = stats[:, :, 0:8]
    top = jnp.max(tops, axis=0)
    factor = jnp.exp(tops - top[None])
    total = jnp.sum(factor * stats[:, :, 8:16], axis=0)
    r, c = row_lane((8, 64))
    expand = jnp.where(r == c // 8, 1.0, 0.0)
    high, low = split(factor.reshape(peers * RES, 8))
    wide = expand.astype(jnp.bfloat16)
    factor = (dot_nn(high, wide) + dot_nn(low, wide)).reshape(peers, RES, 64)
    heads = jnp.sum(factor * weighted, axis=0) / exact_nn(total, expand)
    probs[...] = raw[...] * head_column(jnp.exp(local[:, 0:8] - top) / total)
    attended[...] = heads
    size = RES * 8 // peers
    block = got[:, 24 : 24 + size, :]
    tops = block[:, :, 72:73]
    block = jnp.sum(jnp.exp(tops - jnp.max(tops, axis=0)[None]) * block, axis=0)
    lanes = lax.broadcasted_iota(jnp.int32, block.shape, 1)
    moments[...] = jnp.where(lanes < 72, block / block[:, 73:74], 0.0)
    heads_t = heads.T
    mixing_parts = lhs_parts(mixing[...])
    factor_parts = lhs_parts(factors[...])
    for pair in range(RES // 2):
        if pair % 4 == 0:
            arrive(pair // 4)
        shown, used, base = [], [], []
        for k in range(2):
            i = 2 * pair + k
            rows = slice(64 * i, 64 * i + 64)
            use = gate[rows] * heads_t[:, i : i + 1]
            mixed[rows] = use
            used.append(use)
            base.append(m0t[rows])
            shown.append(present[i : i + 1])
        middle = jnp.concatenate(base, axis=1) + project(mixing_parts, jnp.concatenate(used, axis=1))
        center = middle - jnp.mean(middle, axis=0, keepdims=True)
        scale = lax.rsqrt(jnp.mean(center * center, axis=0, keepdims=True) + EPSILON)
        normed = center * scale
        found = project(factor_parts, normed) * jnp.concatenate(shown, axis=1)
        for k in range(2):
            i = 2 * pair + k
            lanes = slice(SEQ * k, SEQ * k + SEQ)
            x1t[64 * i : 64 * i + 64] = normed[:, lanes]
            inverse_mid[i : i + 1] = scale[:, lanes]
            left[32 * i : 32 * i + 32] = found[:32, lanes]
            scratch[32 * i : 32 * i + 32] = found[32:, lanes]
        if pair % 4 == 3:
            depart(pair // 4)
    for f in range(FACTOR_WIDTH):
        right[f] = scratch[pl.ds(f, RES, stride=FACTOR_WIDTH), :]


def middle_kernel(
    left_own, left_far_0, left_far_1, right_own, right_1, right_2, right_3, moments, x1t, inverse_mid, present, slope_t, gate,
    factors_back, mixing_back, mid, out_grad, send, scratch, arrive, depart,
):
    parts = lhs_parts(factors_back[...])
    mixing_parts = lhs_parts(mixing_back[...])
    ones = jnp.ones((16, SEQ), jnp.bfloat16)
    sums = []
    for pair in range(RES // 2):
        if pair % 4 == 0:
            arrive(pair // 4)
            rows = slice(2 * pair, 2 * pair + 8)
            for f in range(FACTOR_WIDTH):
                part = (right_own[f, rows] + right_1[f, rows]) + (right_2[f, rows] + right_3[f, rows])
                scratch[32 * f + 2 * pair : 32 * f + 2 * pair + 8] = part
        grads = []
        for k in range(2):
            i = 2 * pair + k
            rows = slice(32 * i, 32 * i + 32)
            left_far = left_far_0 if i < RES // 2 else left_far_1
            near = slice(32 * (i % 16), 32 * (i % 16) + 32)
            both = jnp.concatenate(
                [left_own[rows] + left_far[near], scratch[pl.ds(i, FACTOR_WIDTH, stride=RES), :]], axis=0
            )
            grads.append(both * present[i : i + 1])
        mid_in = project(parts, jnp.concatenate(grads, axis=1))
        rows = slice(128 * pair, 128 * pair + 128)
        normed = jnp.concatenate([x1t[128 * pair : 128 * pair + 64], x1t[128 * pair + 64 : 128 * pair + 128]], axis=1)
        scale = jnp.concatenate([inverse_mid[2 * pair : 2 * pair + 1], inverse_mid[2 * pair + 1 : 2 * pair + 2]], axis=1)
        back = scale * (
            mid_in
            - jnp.mean(mid_in, axis=0, keepdims=True)
            - normed * jnp.mean(mid_in * normed, axis=0, keepdims=True)
        )
        back = back + jnp.concatenate(
            [slope_t[128 * pair : 128 * pair + 64], slope_t[128 * pair + 64 : 128 * pair + 128]], axis=1
        )
        grad = project(mixing_parts, back)
        gated = []
        for k in range(2):
            lanes = slice(SEQ * k, SEQ * k + SEQ)
            rows = slice(128 * pair + 64 * k, 128 * pair + 64 * k + 64)
            mid[rows] = back[:, lanes]
            out_grad[rows] = grad[:, lanes]
            gated.append(grad[:, lanes] * gate[rows])
        if pair % 4 == 3:
            depart(pair // 4)
        sums.append(sum_lanes_01(ones, jnp.concatenate(gated, axis=0)))
    sums = [jnp.concatenate([part, part], axis=0) for part in sums]
    send_all(send, slice(0, 16), pack(own_blocks(jnp.concatenate(sums, axis=1))))
    send_all(send, slice(16, 16 + moments.shape[0]), moments[...])


def gate_back_kernel(out_grad, mixed, gate, filter_weight, x_grad):
    parts = lhs_parts(filter_weight[...])
    for pair in range(RES // 2):
        both = []
        for k in range(2):
            rows = slice(128 * pair + 64 * k, 128 * pair + 64 * k + 64)
            both.append(out_grad[rows] * mixed[rows] * (1.0 - gate[rows]))
        found = project(parts, jnp.concatenate(both, axis=1))
        for k in range(2):
            x_grad[128 * pair + 64 * k : 128 * pair + 64 * k + 64] = found[:, SEQ * k : SEQ * k + SEQ]


def finish_kernel(
    got, attended, probs, keys, values, query_blocks, partial, key_value, counts, asking, present, x0t, inverse, mid, out, arrive, depart
):
    att_grad = unpack(jnp.sum(got[:, 0:16, :], axis=0))
    moments = got[:, 16:, :].reshape(RES * 8, 128)
    rows, lanes = row_lane((RES * 8, 64))
    own_head = rows % 8 == lanes // 8
    along = jnp.sum(jnp.where(own_head, over_heads(att_grad * attended[...]), 0.0), axis=1, keepdims=True)
    r, c = row_lane((64, 64))
    spread = exact_nn(jnp.where(own_head, over_heads(att_grad), 0.0), (r % 8 == c // 8).astype(F32))
    both = jnp.concatenate([spread * moments[:, :64], -along * moments[:, 64:]], axis=1)
    r, c = row_lane((128, 64))
    query_grad = exact_nn(both, jnp.where((r < 72) & (r % 8 == c % 8), 1.0, 0.0))
    query_grad = sum_heads(jnp.where(own_head, query_grad, 0.0)) * HEAD_SIZE ** (-0.5)
    mean_grad = (exact_nt(query_grad, asking[...]) / counts[:, :64]).T

    blocks = head_blocks(att_grad)
    score_grad = probs[...] * (exact_nn(blocks, values[...]) - along)
    key_grad = exact_nn(query_blocks[...].T, score_grad)
    value_grad = exact_nn(blocks.T, probs[...])
    parts = lhs_parts(key_value[...])
    for pair in range(RES // 2):
        if pair % 4 == 0:
            arrive(pair // 4)
        both = []
        for k in range(2):
            rows = slice(16 * pair + 8 * k, 16 * pair + 8 * k + 8)
            both.append(jnp.concatenate([key_grad[rows], value_grad[rows]], axis=0))
        found = project(parts, jnp.concatenate(both, axis=1))
        done = []
        for k in range(2):
            i = 2 * pair + k
            rows = slice(64 * i, 64 * i + 64)
            grad = partial[rows] + found[:, SEQ * k : SEQ * k + SEQ] + mean_grad[:, i : i + 1] * present[i : i + 1]
            normed = x0t[rows]
            back = inverse[i : i + 1] * (
                grad - jnp.mean(grad, axis=0, keepdims=True) - normed * jnp.mean(grad * normed, axis=0, keepdims=True)
            )
            done.append(mid[rows] + back)
        out[:, 128 * pair : 128 * pair + 128] = jnp.concatenate(done, axis=0).T
        if pair % 4 == 3:
            depart(pair // 4)


def whole(shape):
    return pl.BlockSpec(shape, lambda *_: (0,) * len(shape))


GROUPS = 4


def portion(ref, group):
    axis = 1 if len(ref.shape) == 3 or ref.shape[1] > 128 else 0
    size = ref.shape[axis] // GROUPS
    window = slice(group * size, group * size + size)
    return ref.at[:, window] if axis else ref.at[window]


def staged(kernel, count, late, early, *refs):
    operands, rest = refs[: count[0]], refs[count[0] :]
    results, rest = rest[: count[1]], rest[count[1] :]
    total = count[0] + count[1]
    held, sems, scratch = rest[:total], rest[total], rest[total + 1 :]
    whole_in = [k for k in range(count[0]) if k not in late]
    copies = [pltpu.make_async_copy(operands[k], held[k], sems.at[k, 0]) for k in whole_in]
    groups = [
        [
            pltpu.make_async_copy(portion(operands[k], group), portion(held[k], group), sems.at[k, group])
            for k in late
        ]
        for group in range(GROUPS)
    ]
    for copy in copies + sum(groups, []):
        copy.start()

    def arrive(group):
        for copy in groups[group]:
            copy.wait()

    leaving = []

    def depart(group):
        for k in early:
            at = count[0] + k
            copy = pltpu.make_async_copy(portion(held[at], group), portion(results[k], group), sems.at[at, group])
            copy.start()
            leaving.append(copy)

    for copy in copies:
        copy.wait()
    kernel(*held, *scratch, *([arrive, depart] if late else []))
    for k in range(count[1]):
        if k not in early:
            at = count[0] + k
            copy = pltpu.make_async_copy(held[at], results[k], sems.at[at, 0])
            copy.start()
            leaving.append(copy)
    for copy in leaving:
        copy.wait()


def call(kernel, shapes, *operands, scratch=(), late=(), early=(), free=(), vmem=40):
    shapes = [jax.ShapeDtypeStruct(shape, F32) for shape in shapes]
    size = sum(4 * array.size for array in shapes) + sum(array.size * array.dtype.itemsize for array in operands)
    arrays = list(operands) + shapes
    return pl.pallas_call(
        functools.partial(staged, kernel, (len(operands), len(shapes)), late, early),
        in_specs=[
            pl.BlockSpec(memory_space=pl.ANY if k in free else pltpu.HBM) for k in range(len(operands))
        ],
        out_specs=[pl.BlockSpec(memory_space=pltpu.HBM)] * len(shapes),
        out_shape=[pltpu.HBM(array.shape, array.dtype) for array in shapes],
        scratch_shapes=[pltpu.VMEM(array.shape, array.dtype) for array in arrays]
        + [pltpu.SemaphoreType.DMA((len(arrays), GROUPS))]
        + list(scratch),
        compiler_params=pltpu.CompilerParams(vmem_limit_bytes=vmem * 2**20),
        cost_estimate=pl.CostEstimate(flops=100_000_000, bytes_accessed=int(size), transcendentals=0),
        name=kernel.__name__,
    )(
        *[
            array if k in free else pltpu.with_memory_space_constraint(array, pltpu.HBM)
            for k, array in enumerate(operands)
        ]
    )


ROWS = 8
COST = 1000


def right_kernel(
    place, own_g, far_g, inverse_count, weight, left, left_far, high, low, out_0, out_1, out_2, out_3, weights, total
):
    step = pl.program_id(0)
    x = place[0]

    @pl.when(step == 0)
    def _():
        w_high, w_low = split(weight[...])
        weights[:, 0:128] = w_high
        weights[:, 128:256] = w_low
        weights[:, 256:384] = w_high
        total[...] = jnp.zeros_like(total)

    near = step < pl.num_programs(0) // 2
    for pair in range(ROWS // 2):
        blocks = []
        for row in (2 * pair, 2 * pair + 1):
            for d in range(4):
                chip = lax.rem(x + d, 4)
                blocks.append(jnp.where(near, own_g[row, chip, 0], far_g[row, chip, 0]))
        g_high, g_low = split(jnp.concatenate(blocks, axis=0))
        grads = dot_nt(weights[...], jnp.concatenate([g_high, g_high, g_low], axis=1))
        grads = grads * jnp.concatenate(
            [inverse_count[2 * pair : 2 * pair + 1], inverse_count[2 * pair + 1 : 2 * pair + 2]], axis=1
        )
        grads_high, grads_low = split(grads)
        for k in range(2):
            row = (2 * pair + k) * FACTOR_WIDTH
            rows, lanes = slice(row, row + FACTOR_WIDTH), slice(128 * k, 128 * k + 128)
            high[:, rows, :] = grads_high[:, lanes].reshape(FACTOR_WIDTH, FACTOR_WIDTH, 128)
            low[:, rows, :] = grads_low[:, lanes].reshape(FACTOR_WIDTH, FACTOR_WIDTH, 128)
    l_high, l_low = split(jnp.where(near, left[...], left_far[...]).T)
    block = slice(None)
    stacked = jnp.concatenate([l_high, l_low], axis=0)
    for f in range(0, FACTOR_WIDTH, 2):
        first = dot_nn(stacked, jnp.concatenate([high[f, block], high[f + 1, block]], axis=1))
        second = dot_nn(l_high, jnp.concatenate([low[f, block], low[f + 1, block]], axis=1))
        total[:, 128 * f : 128 * f + 256] += first[:128] + first[128:] + second

    @pl.when(step == pl.num_programs(0) - 1)
    def _():
        for f in range(FACTOR_WIDTH):
            block = total[:, 128 * f : 128 * f + 128].T
            for d, out in enumerate((out_0, out_1, out_2, out_3)):
                out[f] = block[32 * d : 32 * d + 32]


def right_products(place, pair_grad, far_grad, inverse_count, weight, left, left_far):
    block = ROWS * FACTOR_WIDTH
    steps = 64 // ROWS
    half = steps // 2
    grid_spec = pltpu.PrefetchScalarGridSpec(
        num_scalar_prefetch=1,
        grid=(steps,),
        in_specs=[
            pl.BlockSpec((ROWS, 4, 1, 32, 128), lambda t, s: (jnp.minimum(t, half - 1), 0, s[1], 0, 0)),
            pl.BlockSpec((ROWS, 4, 1, 32, 128), lambda t, s: (jnp.maximum(t - half, 0), 0, s[1], 0, 0)),
            pl.BlockSpec((ROWS, 128), lambda t, s: (t, 0)),
            pl.BlockSpec((1024, 128), lambda t, s: (0, 0)),
            pl.BlockSpec((block, 128), lambda t, s: (jnp.minimum(t, half - 1), 0)),
            pl.BlockSpec((block, 128), lambda t, s: (jnp.maximum(t - half, 0), 0)),
        ],
        out_specs=[
            pl.BlockSpec((FACTOR_WIDTH, block, 128), lambda t, s: (0, t, 0)),
            pl.BlockSpec((FACTOR_WIDTH, block, 128), lambda t, s: (0, t, 0)),
        ]
        + [whole((FACTOR_WIDTH, 32, 128))] * 4,
        scratch_shapes=[
            pltpu.VMEM((1024, 384), jnp.bfloat16),
            pltpu.VMEM((128, 4096), jnp.float32),
        ],
    )
    return pl.pallas_call(
        right_kernel,
        grid_spec=grid_spec,
        out_shape=[
            pltpu.HBM((FACTOR_WIDTH, 64 * FACTOR_WIDTH, 128), jnp.bfloat16),
            pltpu.HBM((FACTOR_WIDTH, 64 * FACTOR_WIDTH, 128), jnp.bfloat16),
        ]
        + [pltpu.HBM((FACTOR_WIDTH, 32, 128), jnp.float32)] * 4,
        compiler_params=pltpu.CompilerParams(vmem_limit_bytes=48 * 2**20),
        cost_estimate=pl.CostEstimate(flops=COST, bytes_accessed=COST, transcendentals=0),
        name="right_products",
    )(
        place,
        *[
            pltpu.with_memory_space_constraint(part, pltpu.HBM)
            for part in (pair_grad, far_grad, inverse_count, weight, left)
        ],
        left_far,
    )


def left_kernel(high, low, right_0, right_1, right_2, right_3, own, far_0, far_1, weights):
    step = pl.program_id(0)

    @pl.when(step == 0)
    def _():
        for f in range(FACTOR_WIDTH):
            for d, right in enumerate((right_0, right_1, right_2, right_3)):
                r_high, r_low = split(right[f])
                row = f * 128 + d * 32
                weights[row : row + 32, 0:128] = r_high
                weights[row : row + 32, 128:256] = r_low

    block = slice(None)
    first = jnp.zeros((ROWS * FACTOR_WIDTH, 256), jnp.float32)
    second = jnp.zeros((ROWS * FACTOR_WIDTH, 128), jnp.float32)
    for f in range(0, FACTOR_WIDTH, 2):
        part = slice(128 * f, 128 * f + 256)
        first += dot_nn(jnp.concatenate([high[f, block], high[f + 1, block]], axis=1), weights[part])
        second += dot_nn(jnp.concatenate([low[f, block], low[f + 1, block]], axis=1), weights[part, 0:128])
    found = first[:, :128] + first[:, 128:] + second
    half = pl.num_programs(0) // 2

    @pl.when(step < half // 2)
    def _():
        far_0[...] = found

    @pl.when((step >= half // 2) & (step < half))
    def _():
        far_1[...] = found

    @pl.when(step >= half)
    def _():
        own[...] = found


def left_products(high, low, rights):
    block = ROWS * FACTOR_WIDTH
    steps = 64 // ROWS
    half = steps // 2
    rows = pl.BlockSpec((FACTOR_WIDTH, block, 128), lambda t: (0, lax.rem(t + half, steps), 0))
    return pl.pallas_call(
        left_kernel,
        grid=(steps,),
        in_specs=[rows, rows] + [whole((FACTOR_WIDTH, 32, 128))] * 4,
        out_specs=[
            pl.BlockSpec((block, 128), lambda t: (jnp.maximum(t - half, 0), 0)),
            pl.BlockSpec((block, 128), lambda t: (jnp.minimum(t, half // 2 - 1), 0)),
            pl.BlockSpec((block, 128), lambda t: (jnp.clip(t - half // 2, 0, half // 2 - 1), 0)),
        ],
        out_shape=[pltpu.HBM((32 * FACTOR_WIDTH, 128), jnp.float32)]
        + [pltpu.HBM((16 * FACTOR_WIDTH, 128), jnp.float32)] * 2,
        scratch_shapes=[pltpu.VMEM((FACTOR_WIDTH * 128, 256), jnp.bfloat16)],
        compiler_params=pltpu.CompilerParams(vmem_limit_bytes=40 * 2**20),
        cost_estimate=pl.CostEstimate(flops=COST, bytes_accessed=COST, transcendentals=0),
        name="left_products",
    )(high, low, pltpu.with_memory_space_constraint(rights[0], pltpu.HBM), *rights[1:])


def swap_core(values):
    return lax.ppermute(values, "core", [(0, 1), (1, 0)])


def fetch_chip(values, distance):
    return lax.ppermute(values, "x", [((i + distance) % 4, i) for i in range(4)])


def send_chip(values, distance):
    return lax.ppermute(values, "x", [(i, (i + distance) % 4) for i in range(4)])


def exchange(send):
    return lax.all_to_all(send, "seq", 0, 0, tiled=True)


def body(
    homolog_features,
    homolog_loss_slope,
    pair_update_gradient,
    alignment_mask,
    asking_matrix,
    key_weight,
    content_matrix,
    sigmoid_filter_matrix,
    final_mixing_matrix,
    first_factor_matrix,
    second_factor_matrix,
    pair_weight,
):
    peers = lax.axis_size("seq")
    share = 64 // peers
    counted = -(-(17 + share) // 8) * 8
    block = RES * 8 // peers
    shared = 24 + block + (0 if share == 2 else share)
    x, core = lax.axis_index("x"), lax.axis_index("core")
    place = jnp.stack([x, core]).astype(jnp.int32)
    mask_core = swap_core(alignment_mask)
    mask_chips = [fetch_chip(alignment_mask, d) for d in (1, 2, 3)]
    weight = pair_weight.reshape(FACTOR_WIDTH, FACTOR_WIDTH, 128).swapaxes(0, 1).reshape(1024, 128)
    value_gate = jnp.concatenate([content_matrix, sigmoid_filter_matrix], axis=1).T
    key_value = jnp.concatenate([key_weight, content_matrix], axis=1)
    factors = jnp.concatenate([first_factor_matrix, second_factor_matrix], axis=1)

    flat, heads, stat = (RES * 64, SEQ), (RES * 8, SEQ), (RES, SEQ)
    x0t, inverse, present, send = call(
        norm_kernel, [flat, stat, stat, (peers, counted, 128)], homolog_features, alignment_mask, late=(0,), early=(0,)
    )
    (send,) = call(pair_kernel, [(peers, counted, 128)], send, alignment_mask, mask_core, *mask_chips, free=(2, 3, 4, 5))
    x0t, send, pair_grad = lax.optimization_barrier((x0t, send, pair_update_gradient))
    far_grad = swap_core(pair_grad).reshape(32, 4, 2, 32, 128)
    pair_grad = pair_grad.reshape(32, 4, 2, 32, 128)
    got = exchange(send)
    keys, values, gate, m0t, slope_t = call(
        project_kernel, [heads, heads, flat, flat, flat],
        x0t, homolog_features, homolog_loss_slope, key_weight.T, value_gate, free=(3, 4),
    )
    got, far_grad, weight, place = lax.optimization_barrier((got, far_grad, weight, place))
    raw, local, counts, query_blocks, send = call(
        score_kernel,
        [heads, (RES, 16), stat, (RES * 8, RES * 8), (peers, shared, 128)],
        got, keys, values, present, asking_matrix, free=(0,),
    )
    got = exchange(send)
    probs, attended, mixed, x1t, inverse_mid, left, right, inverse_count, moments = call(
        attend_kernel,
        [heads, (RES, 64), flat, flat, stat, (RES * 32, SEQ), (FACTOR_WIDTH, RES, SEQ), (64, 128), (block, 128)],
        got, local, raw, m0t, gate, present, final_mixing_matrix.T, factors.T, late=(3, 4), early=(2, 3, 5), free=(0, 6, 7),
        scratch=[pltpu.VMEM((RES * 32, SEQ), F32)],
    )
    rights = [right] + [fetch_chip(right, d) for d in (1, 2, 3)]
    high, low, right_own, right_1, right_2, right_3 = right_products(
        place, pair_grad, far_grad, inverse_count, weight, left, swap_core(left)
    )
    right_sent = [send_chip(part, d) for d, part in ((2, right_2), (1, right_1), (3, right_3))]
    left_own, *left_far = left_products(high, low, rights)
    left_far = [swap_core(part) for part in left_far]
    mid, out_grad, send = call(
        middle_kernel, [flat, flat, (peers, 16 + block, 128)],
        left_own, *left_far, right_own, *right_sent,
        moments, x1t, inverse_mid, present, slope_t, gate, factors, final_mixing_matrix, late=(0, 3, 4, 5, 6, 8, 11, 12), early=(0, 1), free=(1, 2, 4, 5, 6, 13),
        scratch=[pltpu.VMEM((RES * 32, SEQ), F32)],
    )
    got = exchange(send)
    (gate_grad,) = call(gate_back_kernel, [flat], out_grad, mixed, gate, sigmoid_filter_matrix)
    (out,) = call(
        finish_kernel, [(SEQ, RES * 64)],
        got, attended, probs, keys, values, query_blocks, gate_grad, key_value, counts, asking_matrix,
        present, x0t, inverse, mid, late=(6, 11, 13), early=(0,), free=(0, 7),
    )
    return out


def solution(mesh):
    grid = Mesh(mesh.devices.reshape(mesh.devices.shape[0], 4, 2), ("seq", "x", "core"))
    res = ("x", "core")
    in_specs = (
        P("seq", res),
        P("seq", res),
        P(res, None, None),
        P("seq", res),
        P(),
        P(),
        P(),
        P(),
        P(),
        P(),
        P(),
        P(),
    )
    return jax.shard_map(body, mesh=grid, in_specs=in_specs, out_specs=P("seq", res), check_vma=False)
```

```python
import functools

import jax
import jax.numpy as jnp
from jax import lax
from jax.experimental import pallas as pl
from jax.experimental.pallas import tpu as pltpu
from jax.sharding import Mesh
from jax.sharding import PartitionSpec as P

FEATURE_DEPTH = 64
HEAD_COUNT = 8
HEAD_SIZE = 8
FACTOR_WIDTH = 32
RES = 32
SIDE = 4
SEQ = 128

EPSILON = 1e-05
MASK_FILL = -1000000000.0
PRECISE = lax.Precision.HIGHEST
F32 = jnp.float32


def split(values):
    high = values.astype(jnp.bfloat16)
    low = (values - high.astype(jnp.float32)).astype(jnp.bfloat16)
    return high, low


def dot_nn(a, b):
    return lax.dot_general(a, b, (((1,), (0,)), ((), ())), preferred_element_type=jnp.float32)


def dot_nt(a, b):
    return lax.dot_general(a, b, (((1,), (1,)), ((), ())), preferred_element_type=jnp.float32)


def exact_nn(a, b):
    return lax.dot_general(a, b, (((1,), (0,)), ((), ())), preferred_element_type=F32, precision=PRECISE)


def exact_nt(a, b):
    return lax.dot_general(a, b, (((1,), (1,)), ((), ())), preferred_element_type=F32, precision=PRECISE)


def near_nn(a, b):
    a_high, a_low = split(a)
    b_high, b_low = split(b)
    return dot_nn(a_high, b_high) + (dot_nn(a_high, b_low) + dot_nn(a_low, b_high))


def near_nt(a, b):
    a_high, a_low = split(a)
    b_high, b_low = split(b)
    return dot_nt(
        jnp.concatenate([a_high, a_high, a_low], axis=1), jnp.concatenate([b_high, b_low, b_high], axis=1)
    )


def pick_nn(values, ones):
    high, low = split(values)
    rest = values - high.astype(F32) - low.astype(F32)
    ones = ones.astype(jnp.bfloat16)
    return dot_nn(high, ones) + (dot_nn(low, ones) + dot_nn(rest.astype(jnp.bfloat16), ones))


def lhs_parts(weight):
    high, low = split(weight)
    return jnp.concatenate([high, high, low], axis=1)


def project(parts, values):
    high, low = split(values)
    return dot_nn(parts, jnp.concatenate([high, low, high], axis=0))


def row_lane(shape):
    return lax.broadcasted_iota(jnp.int32, shape, 0), lax.broadcasted_iota(jnp.int32, shape, 1)


def sum_lanes_01(ones, values):
    high, rest = values.astype(jnp.bfloat16), values
    rest = rest - high.astype(F32)
    mid = rest.astype(jnp.bfloat16)
    low = (rest - mid.astype(F32)).astype(jnp.bfloat16)
    return dot_nt(ones, high) + dot_nt(ones, mid) + dot_nt(ones, low)


def own_blocks(values):
    rows, _ = row_lane((RES, 128))
    total = jnp.zeros((RES, 128), F32)
    for pair in range(RES // 2):
        total = jnp.where(rows // 2 == pair, values[:, 128 * pair : 128 * pair + 128], total)
    return jnp.where(rows[:, :64] % 2 == 0, total[:, :64], total[:, 64:])


def pack(values):
    return jnp.concatenate([values[:16], values[16:]], axis=1)


def unpack(values):
    return jnp.concatenate([values[:, :64], values[:, 64:]], axis=0)


def over_heads(values):
    return jnp.broadcast_to(values[:, None, :], (RES, 8, values.shape[1])).reshape(RES * 8, values.shape[1])


def head_column(values):
    rows, lanes = row_lane((RES * 8, values.shape[1]))
    return jnp.sum(jnp.where(rows % 8 == lanes, over_heads(values), 0.0), axis=1, keepdims=True)


def head_blocks(values):
    rows, lanes = row_lane((RES * 8, 64))
    picked = jnp.where(rows % 8 == lanes // 8, over_heads(values), 0.0)
    r, c = row_lane((64, RES * 8))
    spread = pick_nn(picked, (r % 8 == c % 8).astype(F32))
    rows, lanes = row_lane((RES * 8, RES * 8))
    return jnp.where(rows // 8 == lanes // 8, spread, 0.0)


def fold_blocks(values):
    rows, lanes = row_lane((RES * 8, RES * 8))
    r, c = row_lane((RES * 8, 128))
    fold = jnp.where((r % 8 == c % 8) & (c < 64), 1.0, 0.0)
    return pick_nn(jnp.where(rows // 8 == lanes // 8, values, 0.0), fold)


def sum_heads(values):
    return jnp.sum(values.reshape(RES, 8, values.shape[1]), axis=1)


def send_all(send, rows, values):
    send[:, rows, :] = jnp.broadcast_to(values[None], (send.shape[0],) + values.shape)


def norm_kernel(m0, mask, x0t, inverse, present, send):
    shown = mask[...].astype(F32).T
    present[...] = shown
    for pair in range(RES // 2):
        block = m0[:, 128 * pair : 128 * pair + 128].T
        for k in range(2):
            part = block[64 * k : 64 * k + 64]
            center = part - jnp.mean(part, axis=0, keepdims=True)
            scale = lax.rsqrt(jnp.mean(center * center, axis=0, keepdims=True) + EPSILON)
            row = 2 * pair + k
            inverse[row : row + 1] = scale
            x0t[64 * row : 64 * row + 64] = center * scale
    ones = shown.astype(jnp.bfloat16)
    sums = own_blocks(sum_lanes_01(ones, x0t[...]))
    counts = dot_nt(jnp.ones((16, SEQ), jnp.bfloat16), ones)
    send[...] = jnp.zeros_like(send)
    send_all(send, slice(0, 16), pack(sums))
    send_all(send, slice(16, 17), jnp.concatenate([counts[0:1], jnp.zeros((1, 96), F32)], axis=1))


def pair_kernel(sent, mask, mask_core, mask_1, mask_2, mask_3, send):
    send[...] = sent[...]
    own = mask[...].astype(F32).T.astype(jnp.bfloat16)
    rows = jnp.concatenate([own, mask_core[...].astype(F32).T.astype(jnp.bfloat16)], axis=0)
    columns = jnp.concatenate(
        [own] + [part[...].astype(F32).T.astype(jnp.bfloat16) for part in (mask_1, mask_2, mask_3)], axis=0
    )
    count = dot_nt(rows, columns)
    share = 64 // send.shape[0]
    for peer in range(send.shape[0]):
        send[peer, 17 : 17 + share, :] = count[share * peer : share * peer + share]


def project_kernel(x0t, m0, slope, key, value_gate, keys, values, gate, m0t, slope_t):
    parts = lhs_parts(value_gate[...])
    for pair in range(RES // 2):
        block = slice(128 * pair, 128 * pair + 128)
        m0t[block] = m0[:, block].T
        slope_t[block] = slope[:, block].T
    for first in range(0, RES, SIDE):
        both = jnp.concatenate([x0t[64 * i : 64 * i + 64] for i in range(first, first + SIDE)], axis=1)
        found = project(parts, both)
        key_rows = exact_nn(key[...], both)
        gates = jax.nn.sigmoid(found[8:72])
        for k in range(SIDE):
            i = first + k
            lanes = slice(SEQ * k, SEQ * k + SEQ)
            keys[8 * i : 8 * i + 8] = key_rows[:, lanes]
            values[8 * i : 8 * i + 8] = found[0:8, lanes]
            gate[64 * i : 64 * i + 64] = gates[:, lanes]


def score_kernel(got, keys, values, present, asking, weights, local, counts, query_blocks, send):
    sums = jnp.sum(got[...], axis=0)
    r, c = row_lane((RES, RES))
    count = jnp.sum(jnp.where(r == c, jnp.broadcast_to(sums[16:17, :RES], (RES, RES)), 0.0), axis=1, keepdims=True)
    counts[...] = jnp.broadcast_to(count, (RES, 128))
    queries = exact_nn(unpack(sums[:16]) / count, asking[...]) * HEAD_SIZE ** (-0.5)
    blocks = head_blocks(queries)
    query_blocks[...] = blocks
    scores = exact_nn(blocks, keys[...])
    scores = jnp.where(over_heads(present[...]) > 0, scores, MASK_FILL)
    top = jnp.max(scores, axis=1, keepdims=True)
    raw = jnp.exp(scores - top)
    weights[...] = raw
    total = jnp.sum(raw, axis=1, keepdims=True)
    rows, lanes = row_lane((RES * 8, 64))
    own_head = rows % 8 == lanes // 8
    weighted = sum_heads(jnp.where(own_head, fold_blocks(near_nt(raw, values[...]))[:, :64], 0.0))
    send_all(send, slice(0, 16), pack(weighted))
    rows, lanes = row_lane((RES * 8, 16))
    stats = jnp.where(lanes == rows % 8, top, jnp.where(lanes == 8 + rows % 8, total, 0.0))
    stats = sum_heads(stats)
    local[...] = stats
    share = 64 // send.shape[0]
    pairs = sums[17 : 17 + share]
    stats = jnp.concatenate([stats[8 * k : 8 * k + 8] for k in range(4)], axis=1)
    if share == 2:
        right = jnp.concatenate([pairs[:, :64], pairs[:, 64:], jnp.zeros((4, 64), F32)], axis=0)
    else:
        right = jnp.zeros((8, 64), F32)
        send_all(send, slice(send.shape[1] - share, send.shape[1]), pairs)
    send_all(send, slice(16, 24), jnp.concatenate([stats, right], axis=1))
    products = raw.reshape(RES, 8, 1, SEQ) * values[...].reshape(RES, 1, 8, SEQ)
    products = products.reshape(RES * 64, SEQ)
    half = RES // 2
    rows, lanes = row_lane((half * 64, 128))
    same = rows // 64 == lanes // 8
    r, c = row_lane((128, 64))
    fold = jnp.where(r % 8 == c % 8, 1.0, 0.0).astype(jnp.bfloat16)
    moments = []
    for k in range(2):
        a_high, a_low = split(products[half * 64 * k : half * 64 * (k + 1)])
        b_high, b_low = split(keys[128 * k : 128 * k + 128])
        found = dot_nt(
            jnp.concatenate([a_high, a_high, a_low], axis=1), jnp.concatenate([b_high, b_low, b_high], axis=1)
        )
        f_high, f_low = split(jnp.where(same, found, 0.0))
        spread = dot_nn(f_high, fold) + dot_nn(f_low, fold)
        spread = jnp.where(rows[:, :64] % 8 == lanes[:, :64] // 8, spread, 0.0)
        moments.append(jnp.sum(spread.reshape(half * 8, 8, 64), axis=1))
    moments = jnp.concatenate(moments, axis=0)
    firsts = fold_blocks(near_nt(raw, keys[...]))
    rows, lanes = row_lane((RES * 8, 64))
    rest = jnp.where(lanes < 8, firsts[:, :64], jnp.where(lanes == 8, top, jnp.where(lanes == 9, total, 0.0)))
    block = jnp.concatenate([moments, rest], axis=1)
    size = RES * 8 // send.shape[0]
    send[:, 24 : 24 + size, :] = block.reshape(send.shape[0], size, 128)


def attend_kernel(
    got, local, raw, m0t, gate, present, mixing, factors,
    probs, attended, mixed, x1t, inverse_mid, left, right, inverse_count, moments, scratch, arrive,
):
    peers = got.shape[0]
    share = 64 // peers
    for peer in range(peers):
        if share == 2:
            pairs = jnp.concatenate([got[peer, 16:18, 64:], got[peer, 18:20, 64:]], axis=1)
        else:
            pairs = got[peer, got.shape[1] - share :, :]
        inverse_count[share * peer : share * peer + share] = 1.0 / pairs
    weighted = jnp.concatenate([got[:, 0:16, 0:64], got[:, 0:16, 64:128]], axis=1)
    stats = jnp.concatenate([got[:, 16:24, 16 * k : 16 * k + 16] for k in range(4)], axis=1)
    tops = stats[:, :, 0:8]
    top = jnp.max(tops, axis=0)
    factor = jnp.exp(tops - top[None])
    total = jnp.sum(factor * stats[:, :, 8:16], axis=0)
    r, c = row_lane((8, 64))
    expand = jnp.where(r == c // 8, 1.0, 0.0)
    high, low = split(factor.reshape(peers * RES, 8))
    wide = expand.astype(jnp.bfloat16)
    factor = (dot_nn(high, wide) + dot_nn(low, wide)).reshape(peers, RES, 64)
    heads = jnp.sum(factor * weighted, axis=0) / exact_nn(total, expand)
    probs[...] = raw[...] * head_column(jnp.exp(local[:, 0:8] - top) / total)
    attended[...] = heads
    size = RES * 8 // peers
    block = got[:, 24 : 24 + size, :]
    tops = block[:, :, 72:73]
    block = jnp.sum(jnp.exp(tops - jnp.max(tops, axis=0)[None]) * block, axis=0)
    lanes = lax.broadcasted_iota(jnp.int32, block.shape, 1)
    moments[...] = jnp.where(lanes < 72, block / block[:, 73:74], 0.0)
    heads_t = heads.T
    mixing_parts = lhs_parts(mixing[...])
    factor_parts = lhs_parts(factors[...])
    arrive()
    for first in range(0, RES, SIDE):
        shown, used, base = [], [], []
        for k in range(SIDE):
            i = first + k
            rows = slice(64 * i, 64 * i + 64)
            use = gate[rows] * heads_t[:, i : i + 1]
            mixed[rows] = use
            used.append(use)
            base.append(m0t[rows])
            shown.append(present[i : i + 1])
        middle = jnp.concatenate(base, axis=1) + project(mixing_parts, jnp.concatenate(used, axis=1))
        center = middle - jnp.mean(middle, axis=0, keepdims=True)
        scale = lax.rsqrt(jnp.mean(center * center, axis=0, keepdims=True) + EPSILON)
        normed = center * scale
        found = project(factor_parts, normed) * jnp.concatenate(shown, axis=1)
        for k in range(SIDE):
            i = first + k
            lanes = slice(SEQ * k, SEQ * k + SEQ)
            x1t[64 * i : 64 * i + 64] = normed[:, lanes]
            inverse_mid[i : i + 1] = scale[:, lanes]
            left[32 * i : 32 * i + 32] = found[:32, lanes]
            scratch[32 * i : 32 * i + 32] = found[32:, lanes]
    for f in range(FACTOR_WIDTH):
        right[f] = scratch[pl.ds(f, RES, stride=FACTOR_WIDTH), :]


def middle_kernel(
    left_own, left_far_0, left_far_1, right_own, right_1, right_2, right_3, moments, x1t, inverse_mid, present, slope_t, gate,
    factors_back, mixing_back, mid, out_grad, send, scratch,
):
    for f in range(FACTOR_WIDTH):
        scratch[32 * f : 32 * f + 32] = (right_own[f] + right_1[f]) + (right_2[f] + right_3[f])
    parts = lhs_parts(factors_back[...])
    mixing_parts = lhs_parts(mixing_back[...])
    ones = jnp.ones((16, SEQ), jnp.bfloat16)
    sums = []
    for first in range(0, RES, SIDE):
        grads = []
        for k in range(SIDE):
            i = first + k
            rows = slice(32 * i, 32 * i + 32)
            left_far = left_far_0 if i < RES // 2 else left_far_1
            near = slice(32 * (i % 16), 32 * (i % 16) + 32)
            both = jnp.concatenate(
                [left_own[rows] + left_far[near], scratch[pl.ds(i, FACTOR_WIDTH, stride=RES), :]], axis=0
            )
            grads.append(both * present[i : i + 1])
        mid_in = project(parts, jnp.concatenate(grads, axis=1))
        group = range(first, first + SIDE)
        normed = jnp.concatenate([x1t[64 * i : 64 * i + 64] for i in group], axis=1)
        scale = jnp.concatenate([inverse_mid[i : i + 1] for i in group], axis=1)
        back = scale * (
            mid_in
            - jnp.mean(mid_in, axis=0, keepdims=True)
            - normed * jnp.mean(mid_in * normed, axis=0, keepdims=True)
        )
        back = back + jnp.concatenate([slope_t[64 * i : 64 * i + 64] for i in group], axis=1)
        grad = project(mixing_parts, back)
        gated = []
        for k in range(SIDE):
            lanes = slice(SEQ * k, SEQ * k + SEQ)
            rows = slice(64 * (first + k), 64 * (first + k) + 64)
            mid[rows] = back[:, lanes]
            out_grad[rows] = grad[:, lanes]
            gated.append(grad[:, lanes] * gate[rows])
        high, low = split(jnp.concatenate(gated, axis=0))
        sums.append(dot_nt(ones, high) + dot_nt(ones, low))
    sums = [jnp.concatenate([part, part], axis=0) for part in sums]
    send_all(send, slice(0, 16), pack(own_blocks(jnp.concatenate(sums, axis=1))))
    send_all(send, slice(16, 16 + moments.shape[0]), moments[...])


def gate_back_kernel(out_grad, mixed, gate, filter_weight, x_grad):
    parts = lhs_parts(filter_weight[...])
    for first in range(0, RES, SIDE):
        both = []
        for i in range(first, first + SIDE):
            rows = slice(64 * i, 64 * i + 64)
            both.append(out_grad[rows] * mixed[rows] * (1.0 - gate[rows]))
        found = project(parts, jnp.concatenate(both, axis=1))
        for k in range(SIDE):
            x_grad[64 * (first + k) : 64 * (first + k) + 64] = found[:, SEQ * k : SEQ * k + SEQ]


def finish_kernel(
    got, attended, probs, keys, values, query_blocks, partial, key_value, counts, asking, present, x0t, inverse, mid, out, arrive
):
    att_grad = unpack(jnp.sum(got[:, 0:16, :], axis=0))
    moments = got[:, 16:, :].reshape(RES * 8, 128)
    rows, lanes = row_lane((RES * 8, 64))
    own_head = rows % 8 == lanes // 8
    along = jnp.sum(jnp.where(own_head, over_heads(att_grad * attended[...]), 0.0), axis=1, keepdims=True)
    r, c = row_lane((64, 64))
    spread = pick_nn(jnp.where(own_head, over_heads(att_grad), 0.0), (r % 8 == c // 8).astype(F32))
    both = jnp.concatenate([spread * moments[:, :64], -along * moments[:, 64:]], axis=1)
    r, c = row_lane((128, 64))
    query_grad = exact_nn(both, jnp.where((r < 72) & (r % 8 == c % 8), 1.0, 0.0))
    query_grad = sum_heads(jnp.where(own_head, query_grad, 0.0)) * HEAD_SIZE ** (-0.5)
    mean_grad = (exact_nt(query_grad, asking[...]) / counts[:, :64]).T

    blocks = head_blocks(att_grad)
    score_grad = probs[...] * (near_nn(blocks, values[...]) - along)
    key_grad = near_nn(query_blocks[...].T, score_grad)
    value_grad = near_nn(blocks.T, probs[...])
    parts = lhs_parts(key_value[...])
    arrive()
    for first in range(0, RES, SIDE):
        both = []
        for i in range(first, first + SIDE):
            rows = slice(8 * i, 8 * i + 8)
            both.append(jnp.concatenate([key_grad[rows], value_grad[rows]], axis=0))
        found = project(parts, jnp.concatenate(both, axis=1))
        done = []
        for k in range(SIDE):
            i = first + k
            rows = slice(64 * i, 64 * i + 64)
            grad = partial[rows] + found[:, SEQ * k : SEQ * k + SEQ] + mean_grad[:, i : i + 1] * present[i : i + 1]
            normed = x0t[rows]
            back = inverse[i : i + 1] * (
                grad - jnp.mean(grad, axis=0, keepdims=True) - normed * jnp.mean(grad * normed, axis=0, keepdims=True)
            )
            done.append(mid[rows] + back)
        for k in range(0, SIDE, 2):
            column = 64 * (first + k)
            out[:, column : column + 128] = jnp.concatenate(done[k : k + 2], axis=0).T


def whole(shape):
    return pl.BlockSpec(shape, lambda *_: (0,) * len(shape))


def staged(kernel, count, late, *refs):
    operands, rest = refs[: count[0]], refs[count[0] :]
    results, rest = rest[: count[1]], rest[count[1] :]
    total = count[0] + count[1]
    held, sems, scratch = rest[:total], rest[total], rest[total + 1 :]
    copies = [pltpu.make_async_copy(operands[k], held[k], sems.at[k]) for k in range(count[0])]
    for copy in copies:
        copy.start()

    def arrive():
        for k in late:
            copies[k].wait()

    for k in range(count[0]):
        if k not in late:
            copies[k].wait()
    kernel(*held, *scratch, *([arrive] if late else []))
    copies = [
        pltpu.make_async_copy(held[count[0] + k], results[k], sems.at[count[0] + k]) for k in range(count[1])
    ]
    for copy in copies:
        copy.start()
    for copy in copies:
        copy.wait()


def call(kernel, shapes, *operands, scratch=(), late=(), free=(), vmem=40):
    shapes = [jax.ShapeDtypeStruct(shape, F32) for shape in shapes]
    size = sum(4 * array.size for array in shapes) + sum(array.size * array.dtype.itemsize for array in operands)
    arrays = list(operands) + shapes
    return pl.pallas_call(
        functools.partial(staged, kernel, (len(operands), len(shapes)), late),
        in_specs=[
            pl.BlockSpec(memory_space=pl.ANY if k in free else pltpu.HBM) for k in range(len(operands))
        ],
        out_specs=[pl.BlockSpec(memory_space=pltpu.HBM)] * len(shapes),
        out_shape=[pltpu.HBM(array.shape, array.dtype) for array in shapes],
        scratch_shapes=[pltpu.VMEM(array.shape, array.dtype) for array in arrays]
        + [pltpu.SemaphoreType.DMA((len(arrays),))]
        + list(scratch),
        compiler_params=pltpu.CompilerParams(vmem_limit_bytes=vmem * 2**20),
        cost_estimate=pl.CostEstimate(flops=100_000_000, bytes_accessed=int(size), transcendentals=0),
        name=kernel.__name__,
    )(
        *[
            array if k in free else pltpu.with_memory_space_constraint(array, pltpu.HBM)
            for k, array in enumerate(operands)
        ]
    )


ROWS = 8
COST = 1000


def right_kernel(
    place, own_g, far_g, inverse_count, weight, left, left_far, high, low, out_0, out_1, out_2, out_3, weights, total
):
    step = pl.program_id(0)
    x = place[0]

    @pl.when(step == 0)
    def _():
        w_high, w_low = split(weight[...])
        weights[:, 0:128] = w_high
        weights[:, 128:256] = w_low
        weights[:, 256:384] = w_high
        total[...] = jnp.zeros_like(total)

    near = step < pl.num_programs(0) // 2
    for pair in range(ROWS // 2):
        blocks = []
        for row in (2 * pair, 2 * pair + 1):
            for d in range(4):
                chip = lax.rem(x + d, 4)
                blocks.append(jnp.where(near, own_g[row, chip, 0], far_g[row, chip, 0]))
        g_high, g_low = split(jnp.concatenate(blocks, axis=0))
        grads = dot_nt(weights[...], jnp.concatenate([g_high, g_high, g_low], axis=1))
        grads = grads * jnp.concatenate(
            [inverse_count[2 * pair : 2 * pair + 1], inverse_count[2 * pair + 1 : 2 * pair + 2]], axis=1
        )
        grads_high, grads_low = split(grads)
        for k in range(2):
            row = (2 * pair + k) * FACTOR_WIDTH
            rows, lanes = slice(row, row + FACTOR_WIDTH), slice(128 * k, 128 * k + 128)
            high[:, rows, :] = grads_high[:, lanes].reshape(FACTOR_WIDTH, FACTOR_WIDTH, 128)
            low[:, rows, :] = grads_low[:, lanes].reshape(FACTOR_WIDTH, FACTOR_WIDTH, 128)
    l_high, l_low = split(jnp.where(near, left[...], left_far[...]).T)
    block = slice(None)
    stacked = jnp.concatenate([l_high, l_low], axis=0)
    for f in range(0, FACTOR_WIDTH, 2):
        first = dot_nn(stacked, jnp.concatenate([high[f, block], high[f + 1, block]], axis=1))
        second = dot_nn(l_high, jnp.concatenate([low[f, block], low[f + 1, block]], axis=1))
        total[:, 128 * f : 128 * f + 256] += first[:128] + first[128:] + second

    @pl.when(step == pl.num_programs(0) - 1)
    def _():
        for f in range(FACTOR_WIDTH):
            block = total[:, 128 * f : 128 * f + 128].T
            for d, out in enumerate((out_0, out_1, out_2, out_3)):
                out[f] = block[32 * d : 32 * d + 32]


def right_products(place, pair_grad, far_grad, inverse_count, weight, left, left_far):
    block = ROWS * FACTOR_WIDTH
    steps = 64 // ROWS
    half = steps // 2
    grid_spec = pltpu.PrefetchScalarGridSpec(
        num_scalar_prefetch=1,
        grid=(steps,),
        in_specs=[
            pl.BlockSpec((ROWS, 4, 1, 32, 128), lambda t, s: (jnp.minimum(t, half - 1), 0, s[1], 0, 0)),
            pl.BlockSpec((ROWS, 4, 1, 32, 128), lambda t, s: (jnp.maximum(t - half, 0), 0, s[1], 0, 0)),
            pl.BlockSpec((ROWS, 128), lambda t, s: (t, 0)),
            pl.BlockSpec((1024, 128), lambda t, s: (0, 0)),
            pl.BlockSpec((block, 128), lambda t, s: (jnp.minimum(t, half - 1), 0)),
            pl.BlockSpec((block, 128), lambda t, s: (jnp.maximum(t - half, 0), 0)),
        ],
        out_specs=[
            pl.BlockSpec((FACTOR_WIDTH, block, 128), lambda t, s: (0, t, 0)),
            pl.BlockSpec((FACTOR_WIDTH, block, 128), lambda t, s: (0, t, 0)),
        ]
        + [whole((FACTOR_WIDTH, 32, 128))] * 4,
        scratch_shapes=[
            pltpu.VMEM((1024, 384), jnp.bfloat16),
            pltpu.VMEM((128, 4096), jnp.float32),
        ],
    )
    return pl.pallas_call(
        right_kernel,
        grid_spec=grid_spec,
        out_shape=[
            pltpu.HBM((FACTOR_WIDTH, 64 * FACTOR_WIDTH, 128), jnp.bfloat16),
            pltpu.HBM((FACTOR_WIDTH, 64 * FACTOR_WIDTH, 128), jnp.bfloat16),
        ]
        + [pltpu.HBM((FACTOR_WIDTH, 32, 128), jnp.float32)] * 4,
        compiler_params=pltpu.CompilerParams(vmem_limit_bytes=48 * 2**20),
        cost_estimate=pl.CostEstimate(flops=COST, bytes_accessed=COST, transcendentals=0),
        name="right_products",
    )(
        place,
        *[
            pltpu.with_memory_space_constraint(part, pltpu.HBM)
            for part in (pair_grad, far_grad, inverse_count, weight, left)
        ],
        left_far,
    )


def left_kernel(high, low, right_0, right_1, right_2, right_3, own, far_0, far_1, weights):
    step = pl.program_id(0)

    @pl.when(step == 0)
    def _():
        for f in range(FACTOR_WIDTH):
            for d, right in enumerate((right_0, right_1, right_2, right_3)):
                r_high, r_low = split(right[f])
                row = f * 128 + d * 32
                weights[row : row + 32, 0:128] = r_high
                weights[row : row + 32, 128:256] = r_low

    block = slice(None)
    first = jnp.zeros((ROWS * FACTOR_WIDTH, 256), jnp.float32)
    second = jnp.zeros((ROWS * FACTOR_WIDTH, 128), jnp.float32)
    for f in range(0, FACTOR_WIDTH, 2):
        part = slice(128 * f, 128 * f + 256)
        first += dot_nn(jnp.concatenate([high[f, block], high[f + 1, block]], axis=1), weights[part])
        second += dot_nn(jnp.concatenate([low[f, block], low[f + 1, block]], axis=1), weights[part, 0:128])
    found = first[:, :128] + first[:, 128:] + second
    half = pl.num_programs(0) // 2

    @pl.when(step < half // 2)
    def _():
        far_0[...] = found

    @pl.when((step >= half // 2) & (step < half))
    def _():
        far_1[...] = found

    @pl.when(step >= half)
    def _():
        own[...] = found


def left_products(high, low, rights):
    block = ROWS * FACTOR_WIDTH
    steps = 64 // ROWS
    half = steps // 2
    rows = pl.BlockSpec((FACTOR_WIDTH, block, 128), lambda t: (0, lax.rem(t + half, steps), 0))
    return pl.pallas_call(
        left_kernel,
        grid=(steps,),
        in_specs=[rows, rows] + [whole((FACTOR_WIDTH, 32, 128))] * 4,
        out_specs=[
            pl.BlockSpec((block, 128), lambda t: (jnp.maximum(t - half, 0), 0)),
            pl.BlockSpec((block, 128), lambda t: (jnp.minimum(t, half // 2 - 1), 0)),
            pl.BlockSpec((block, 128), lambda t: (jnp.clip(t - half // 2, 0, half // 2 - 1), 0)),
        ],
        out_shape=[pltpu.HBM((32 * FACTOR_WIDTH, 128), jnp.float32)]
        + [pltpu.HBM((16 * FACTOR_WIDTH, 128), jnp.float32)] * 2,
        scratch_shapes=[pltpu.VMEM((FACTOR_WIDTH * 128, 256), jnp.bfloat16)],
        compiler_params=pltpu.CompilerParams(vmem_limit_bytes=40 * 2**20),
        cost_estimate=pl.CostEstimate(flops=COST, bytes_accessed=COST, transcendentals=0),
        name="left_products",
    )(high, low, pltpu.with_memory_space_constraint(rights[0], pltpu.HBM), *rights[1:])


def swap_core(values):
    return lax.ppermute(values, "core", [(0, 1), (1, 0)])


def fetch_chip(values, distance):
    return lax.ppermute(values, "x", [((i + distance) % 4, i) for i in range(4)])


def send_chip(values, distance):
    return lax.ppermute(values, "x", [(i, (i + distance) % 4) for i in range(4)])


def exchange(send):
    return lax.all_to_all(send, "seq", 0, 0, tiled=True)


def body(
    homolog_features,
    homolog_loss_slope,
    pair_update_gradient,
    alignment_mask,
    asking_matrix,
    key_weight,
    content_matrix,
    sigmoid_filter_matrix,
    final_mixing_matrix,
    first_factor_matrix,
    second_factor_matrix,
    pair_weight,
):
    peers = lax.axis_size("seq")
    share = 64 // peers
    counted = -(-(17 + share) // 8) * 8
    block = RES * 8 // peers
    shared = 24 + block + (0 if share == 2 else share)
    x, core = lax.axis_index("x"), lax.axis_index("core")
    place = jnp.stack([x, core]).astype(jnp.int32)
    mask_core = swap_core(alignment_mask)
    mask_chips = [fetch_chip(alignment_mask, d) for d in (1, 2, 3)]
    weight = pair_weight.reshape(FACTOR_WIDTH, FACTOR_WIDTH, 128).swapaxes(0, 1).reshape(1024, 128)
    value_gate = jnp.concatenate([content_matrix, sigmoid_filter_matrix], axis=1).T
    key_value = jnp.concatenate([key_weight, content_matrix], axis=1)
    factors = jnp.concatenate([first_factor_matrix, second_factor_matrix], axis=1)

    flat, heads, stat = (RES * 64, SEQ), (RES * 8, SEQ), (RES, SEQ)
    x0t, inverse, present, send = call(
        norm_kernel, [flat, stat, stat, (peers, counted, 128)], homolog_features, alignment_mask
    )
    (send,) = call(pair_kernel, [(peers, counted, 128)], send, alignment_mask, mask_core, *mask_chips, free=(2, 3, 4, 5))
    x0t, send, pair_grad = lax.optimization_barrier((x0t, send, pair_update_gradient))
    far_grad = swap_core(pair_grad).reshape(32, 4, 2, 32, 128)
    pair_grad = pair_grad.reshape(32, 4, 2, 32, 128)
    got = exchange(send)
    keys, values, gate, m0t, slope_t = call(
        project_kernel, [heads, heads, flat, flat, flat],
        x0t, homolog_features, homolog_loss_slope, key_weight.T, value_gate, free=(3, 4),
    )
    got, far_grad, weight, place = lax.optimization_barrier((got, far_grad, weight, place))
    raw, local, counts, query_blocks, send = call(
        score_kernel,
        [heads, (RES, 16), stat, (RES * 8, RES * 8), (peers, shared, 128)],
        got, keys, values, present, asking_matrix, free=(0,),
    )
    got = exchange(send)
    probs, attended, mixed, x1t, inverse_mid, left, right, inverse_count, moments = call(
        attend_kernel,
        [heads, (RES, 64), flat, flat, stat, (RES * 32, SEQ), (FACTOR_WIDTH, RES, SEQ), (64, 128), (block, 128)],
        got, local, raw, m0t, gate, present, final_mixing_matrix.T, factors.T, late=(3, 4), free=(0, 6, 7),
        scratch=[pltpu.VMEM((RES * 32, SEQ), F32)],
    )
    rights = [right] + [fetch_chip(right, d) for d in (1, 2, 3)]
    high, low, right_own, right_1, right_2, right_3 = right_products(
        place, pair_grad, far_grad, inverse_count, weight, left, swap_core(left)
    )
    right_sent = [send_chip(part, d) for d, part in ((2, right_2), (1, right_1), (3, right_3))]
    left_own, *left_far = left_products(high, low, rights)
    left_far = [swap_core(part) for part in left_far]
    mid, out_grad, send = call(
        middle_kernel, [flat, flat, (peers, 16 + block, 128)],
        left_own, *left_far, right_own, *right_sent,
        moments, x1t, inverse_mid, present, slope_t, gate, factors, final_mixing_matrix, free=(1, 2, 4, 5, 6, 13),
        scratch=[pltpu.VMEM((RES * 32, SEQ), F32)],
    )
    got = exchange(send)
    (gate_grad,) = call(gate_back_kernel, [flat], out_grad, mixed, gate, sigmoid_filter_matrix)
    (out,) = call(
        finish_kernel, [(SEQ, RES * 64)],
        got, attended, probs, keys, values, query_blocks, gate_grad, key_value, counts, asking_matrix,
        present, x0t, inverse, mid, late=(6, 11, 13), free=(0, 7),
    )
    return out


def solution(mesh):
    grid = Mesh(mesh.devices.reshape(mesh.devices.shape[0], 4, 2), ("seq", "x", "core"))
    res = ("x", "core")
    in_specs = (
        P("seq", res),
        P("seq", res),
        P(res, None, None),
        P("seq", res),
        P(),
        P(),
        P(),
        P(),
        P(),
        P(),
        P(),
        P(),
    )
    return jax.shard_map(body, mesh=grid, in_specs=in_specs, out_specs=P("seq", res), check_vma=False)
```

```python
import functools

import jax
import jax.numpy as jnp
from jax import lax
from jax.experimental import pallas as pl
from jax.experimental.pallas import tpu as pltpu
from jax.sharding import Mesh
from jax.sharding import PartitionSpec as P

FEATURE_DEPTH = 64
HEAD_COUNT = 8
HEAD_SIZE = 8
FACTOR_WIDTH = 32
RES = 32
SIDE = 4
SEQ = 128

EPSILON = 1e-05
MASK_FILL = -1000000000.0
PRECISE = lax.Precision.HIGHEST
F32 = jnp.float32


def split(values):
    high = values.astype(jnp.bfloat16)
    low = (values - high.astype(jnp.float32)).astype(jnp.bfloat16)
    return high, low


def dot_nn(a, b):
    return lax.dot_general(a, b, (((1,), (0,)), ((), ())), preferred_element_type=jnp.float32)


def dot_nt(a, b):
    return lax.dot_general(a, b, (((1,), (1,)), ((), ())), preferred_element_type=jnp.float32)


def exact_nn(a, b):
    return lax.dot_general(a, b, (((1,), (0,)), ((), ())), preferred_element_type=F32, precision=PRECISE)


def exact_nt(a, b):
    return lax.dot_general(a, b, (((1,), (1,)), ((), ())), preferred_element_type=F32, precision=PRECISE)


def near_nn(a, b):
    a_high, a_low = split(a)
    b_high, b_low = split(b)
    return dot_nn(a_high, b_high) + (dot_nn(a_high, b_low) + dot_nn(a_low, b_high))


def near_nt(a, b):
    a_high, a_low = split(a)
    b_high, b_low = split(b)
    return dot_nt(
        jnp.concatenate([a_high, a_high, a_low], axis=1), jnp.concatenate([b_high, b_low, b_high], axis=1)
    )


def pick_nn(values, ones):
    high, low = split(values)
    rest = values - high.astype(F32) - low.astype(F32)
    ones = ones.astype(jnp.bfloat16)
    return dot_nn(high, ones) + (dot_nn(low, ones) + dot_nn(rest.astype(jnp.bfloat16), ones))


def lhs_parts(weight):
    high, low = split(weight)
    return jnp.concatenate([high, high, low], axis=1)


def project(parts, values):
    high, low = split(values)
    return dot_nn(parts, jnp.concatenate([high, low, high], axis=0))


def row_lane(shape):
    return lax.broadcasted_iota(jnp.int32, shape, 0), lax.broadcasted_iota(jnp.int32, shape, 1)


def sum_lanes_01(ones, values):
    high, rest = values.astype(jnp.bfloat16), values
    rest = rest - high.astype(F32)
    mid = rest.astype(jnp.bfloat16)
    low = (rest - mid.astype(F32)).astype(jnp.bfloat16)
    return dot_nt(ones, high) + dot_nt(ones, mid) + dot_nt(ones, low)


def own_blocks(values):
    rows, _ = row_lane((RES, 128))
    total = jnp.zeros((RES, 128), F32)
    for pair in range(RES // 2):
        total = jnp.where(rows // 2 == pair, values[:, 128 * pair : 128 * pair + 128], total)
    return jnp.where(rows[:, :64] % 2 == 0, total[:, :64], total[:, 64:])


def pack(values):
    return jnp.concatenate([values[:16], values[16:]], axis=1)


def unpack(values):
    return jnp.concatenate([values[:, :64], values[:, 64:]], axis=0)


def over_heads(values):
    return jnp.broadcast_to(values[:, None, :], (RES, 8, values.shape[1])).reshape(RES * 8, values.shape[1])


def head_column(values):
    rows, lanes = row_lane((RES * 8, values.shape[1]))
    return jnp.sum(jnp.where(rows % 8 == lanes, over_heads(values), 0.0), axis=1, keepdims=True)


def head_blocks(values):
    rows, lanes = row_lane((RES * 8, 64))
    picked = jnp.where(rows % 8 == lanes // 8, over_heads(values), 0.0)
    r, c = row_lane((64, RES * 8))
    spread = pick_nn(picked, (r % 8 == c % 8).astype(F32))
    rows, lanes = row_lane((RES * 8, RES * 8))
    return jnp.where(rows // 8 == lanes // 8, spread, 0.0)


def fold_blocks(values):
    rows, lanes = row_lane((RES * 8, RES * 8))
    r, c = row_lane((RES * 8, 128))
    fold = jnp.where((r % 8 == c % 8) & (c < 64), 1.0, 0.0)
    return pick_nn(jnp.where(rows // 8 == lanes // 8, values, 0.0), fold)


def sum_heads(values):
    return jnp.sum(values.reshape(RES, 8, values.shape[1]), axis=1)


def send_all(send, rows, values):
    send[:, rows, :] = jnp.broadcast_to(values[None], (send.shape[0],) + values.shape)


def norm_kernel(m0, mask, x0t, inverse, present, send):
    shown = mask[...].astype(F32)
    present[...] = shown
    for pair in range(RES // 2):
        block = m0[:, 128 * pair : 128 * pair + 128].T
        for k in range(2):
            part = block[64 * k : 64 * k + 64]
            center = part - jnp.mean(part, axis=0, keepdims=True)
            scale = lax.rsqrt(jnp.mean(center * center, axis=0, keepdims=True) + EPSILON)
            row = 2 * pair + k
            inverse[row : row + 1] = scale
            x0t[64 * row : 64 * row + 64] = center * scale
    ones = shown.astype(jnp.bfloat16)
    sums = own_blocks(sum_lanes_01(ones, x0t[...]))
    counts = dot_nt(jnp.ones((16, SEQ), jnp.bfloat16), ones)
    send[...] = jnp.zeros_like(send)
    send_all(send, slice(0, 16), pack(sums))
    send_all(send, slice(16, 17), jnp.concatenate([counts[0:1], jnp.zeros((1, 96), F32)], axis=1))


def pair_kernel(sent, mask, mask_core, mask_1, mask_2, mask_3, send):
    send[...] = sent[...]
    own = mask[...].astype(F32).astype(jnp.bfloat16)
    rows = jnp.concatenate([own, mask_core[...].astype(F32).astype(jnp.bfloat16)], axis=0)
    columns = jnp.concatenate(
        [own] + [part[...].astype(F32).astype(jnp.bfloat16) for part in (mask_1, mask_2, mask_3)], axis=0
    )
    count = dot_nt(rows, columns)
    share = 64 // send.shape[0]
    for peer in range(send.shape[0]):
        send[peer, 17 : 17 + share, :] = count[share * peer : share * peer + share]


def project_kernel(x0t, m0, slope, key, value_gate, keys, values, gate, m0t, slope_t):
    parts = lhs_parts(value_gate[...])
    for pair in range(RES // 2):
        block = slice(128 * pair, 128 * pair + 128)
        m0t[block] = m0[:, block].T
        slope_t[block] = slope[:, block].T
    for first in range(0, RES, SIDE):
        both = jnp.concatenate([x0t[64 * i : 64 * i + 64] for i in range(first, first + SIDE)], axis=1)
        found = project(parts, both)
        key_rows = exact_nn(key[...], both)
        gates = jax.nn.sigmoid(found[8:72])
        for k in range(SIDE):
            i = first + k
            lanes = slice(SEQ * k, SEQ * k + SEQ)
            keys[8 * i : 8 * i + 8] = key_rows[:, lanes]
            values[8 * i : 8 * i + 8] = found[0:8, lanes]
            gate[64 * i : 64 * i + 64] = gates[:, lanes]


def score_kernel(got, keys, values, present, asking, weights, local, counts, query_blocks, send):
    sums = jnp.sum(got[...], axis=0)
    r, c = row_lane((RES, RES))
    count = jnp.sum(jnp.where(r == c, jnp.broadcast_to(sums[16:17, :RES], (RES, RES)), 0.0), axis=1, keepdims=True)
    counts[...] = jnp.broadcast_to(count, (RES, 128))
    queries = exact_nn(unpack(sums[:16]) / count, asking[...]) * HEAD_SIZE ** (-0.5)
    blocks = head_blocks(queries)
    query_blocks[...] = blocks
    scores = exact_nn(blocks, keys[...])
    scores = jnp.where(over_heads(present[...]) > 0, scores, MASK_FILL)
    top = jnp.max(scores, axis=1, keepdims=True)
    raw = jnp.exp(scores - top)
    weights[...] = raw
    total = jnp.sum(raw, axis=1, keepdims=True)
    rows, lanes = row_lane((RES * 8, 64))
    own_head = rows % 8 == lanes // 8
    weighted = sum_heads(jnp.where(own_head, fold_blocks(near_nt(raw, values[...]))[:, :64], 0.0))
    send_all(send, slice(0, 16), pack(weighted))
    rows, lanes = row_lane((RES * 8, 16))
    stats = jnp.where(lanes == rows % 8, top, jnp.where(lanes == 8 + rows % 8, total, 0.0))
    stats = sum_heads(stats)
    local[...] = stats
    share = 64 // send.shape[0]
    pairs = sums[17 : 17 + share]
    stats = jnp.concatenate([stats[8 * k : 8 * k + 8] for k in range(4)], axis=1)
    if share == 2:
        right = jnp.concatenate([pairs[:, :64], pairs[:, 64:], jnp.zeros((4, 64), F32)], axis=0)
    else:
        right = jnp.zeros((8, 64), F32)
        send_all(send, slice(send.shape[1] - share, send.shape[1]), pairs)
    send_all(send, slice(16, 24), jnp.concatenate([stats, right], axis=1))
    products = raw.reshape(RES, 8, 1, SEQ) * values[...].reshape(RES, 1, 8, SEQ)
    products = products.reshape(RES * 64, SEQ)
    half = RES // 2
    rows, lanes = row_lane((half * 64, 128))
    same = rows // 64 == lanes // 8
    r, c = row_lane((128, 64))
    fold = jnp.where(r % 8 == c % 8, 1.0, 0.0).astype(jnp.bfloat16)
    moments = []
    for k in range(2):
        a_high, a_low = split(products[half * 64 * k : half * 64 * (k + 1)])
        b_high, b_low = split(keys[128 * k : 128 * k + 128])
        found = dot_nt(
            jnp.concatenate([a_high, a_high, a_low], axis=1), jnp.concatenate([b_high, b_low, b_high], axis=1)
        )
        f_high, f_low = split(jnp.where(same, found, 0.0))
        spread = dot_nn(f_high, fold) + dot_nn(f_low, fold)
        spread = jnp.where(rows[:, :64] % 8 == lanes[:, :64] // 8, spread, 0.0)
        moments.append(jnp.sum(spread.reshape(half * 8, 8, 64), axis=1))
    moments = jnp.concatenate(moments, axis=0)
    firsts = fold_blocks(near_nt(raw, keys[...]))
    rows, lanes = row_lane((RES * 8, 64))
    rest = jnp.where(lanes < 8, firsts[:, :64], jnp.where(lanes == 8, top, jnp.where(lanes == 9, total, 0.0)))
    block = jnp.concatenate([moments, rest], axis=1)
    size = RES * 8 // send.shape[0]
    send[:, 24 : 24 + size, :] = block.reshape(send.shape[0], size, 128)


def attend_kernel(
    got, local, raw, m0t, gate, present, mixing, factors,
    probs, attended, x1t, inverse_mid, left, right, inverse_count, moments, scratch, arrive,
):
    peers = got.shape[0]
    share = 64 // peers
    for peer in range(peers):
        if share == 2:
            pairs = jnp.concatenate([got[peer, 16:18, 64:], got[peer, 18:20, 64:]], axis=1)
        else:
            pairs = got[peer, got.shape[1] - share :, :]
        inverse_count[share * peer : share * peer + share] = 1.0 / pairs
    weighted = jnp.concatenate([got[:, 0:16, 0:64], got[:, 0:16, 64:128]], axis=1)
    stats = jnp.concatenate([got[:, 16:24, 16 * k : 16 * k + 16] for k in range(4)], axis=1)
    tops = stats[:, :, 0:8]
    top = jnp.max(tops, axis=0)
    factor = jnp.exp(tops - top[None])
    total = jnp.sum(factor * stats[:, :, 8:16], axis=0)
    r, c = row_lane((8, 64))
    expand = jnp.where(r == c // 8, 1.0, 0.0)
    high, low = split(factor.reshape(peers * RES, 8))
    wide = expand.astype(jnp.bfloat16)
    factor = (dot_nn(high, wide) + dot_nn(low, wide)).reshape(peers, RES, 64)
    heads = jnp.sum(factor * weighted, axis=0) / exact_nn(total, expand)
    probs[...] = raw[...] * head_column(jnp.exp(local[:, 0:8] - top) / total)
    attended[...] = heads
    size = RES * 8 // peers
    block = got[:, 24 : 24 + size, :]
    tops = block[:, :, 72:73]
    block = jnp.sum(jnp.exp(tops - jnp.max(tops, axis=0)[None]) * block, axis=0)
    lanes = lax.broadcasted_iota(jnp.int32, block.shape, 1)
    moments[...] = jnp.where(lanes < 72, block / block[:, 73:74], 0.0)
    heads_t = heads.T
    mixing_parts = lhs_parts(mixing[...])
    factor_parts = lhs_parts(factors[...])
    arrive()
    for first in range(0, RES, 2):
        shown, used, base = [], [], []
        for k in range(2):
            i = first + k
            rows = slice(64 * i, 64 * i + 64)
            use = gate[rows] * heads_t[:, i : i + 1]
            used.append(use)
            base.append(m0t[rows])
            shown.append(present[i : i + 1])
        middle = jnp.concatenate(base, axis=1) + project(mixing_parts, jnp.concatenate(used, axis=1))
        center = middle - jnp.mean(middle, axis=0, keepdims=True)
        scale = lax.rsqrt(jnp.mean(center * center, axis=0, keepdims=True) + EPSILON)
        normed = center * scale
        found = project(factor_parts, normed) * jnp.concatenate(shown, axis=1)
        for k in range(2):
            i = first + k
            lanes = slice(SEQ * k, SEQ * k + SEQ)
            x1t[64 * i : 64 * i + 64] = normed[:, lanes]
            inverse_mid[i : i + 1] = scale[:, lanes]
            left[32 * i : 32 * i + 32] = found[:32, lanes]
            scratch[32 * i : 32 * i + 32] = found[32:, lanes]
    for f in range(FACTOR_WIDTH):
        right[f] = scratch[pl.ds(f, RES, stride=FACTOR_WIDTH), :]


def middle_kernel(
    left_own, left_far_0, left_far_1, right_own, right_1, right_2, right_3, moments, x1t, inverse_mid, present, slope_t, gate,
    factors_back, mixing_back, mid, send, scratch,
):
    for f in range(FACTOR_WIDTH):
        scratch[32 * f : 32 * f + 32] = (right_own[f] + right_1[f]) + (right_2[f] + right_3[f])
    parts = lhs_parts(factors_back[...])
    mixing_parts = lhs_parts(mixing_back[...])
    ones = jnp.ones((16, SEQ), jnp.bfloat16)
    sums = []
    for first in range(0, RES, SIDE):
        grads = []
        for k in range(SIDE):
            i = first + k
            rows = slice(32 * i, 32 * i + 32)
            left_far = left_far_0 if i < RES // 2 else left_far_1
            near = slice(32 * (i % 16), 32 * (i % 16) + 32)
            both = jnp.concatenate(
                [left_own[rows] + left_far[near], scratch[pl.ds(i, FACTOR_WIDTH, stride=RES), :]], axis=0
            )
            grads.append(both * present[i : i + 1])
        mid_in = project(parts, jnp.concatenate(grads, axis=1))
        group = range(first, first + SIDE)
        normed = jnp.concatenate([x1t[64 * i : 64 * i + 64] for i in group], axis=1)
        scale = jnp.concatenate([inverse_mid[i : i + 1] for i in group], axis=1)
        back = scale * (
            mid_in
            - jnp.mean(mid_in, axis=0, keepdims=True)
            - normed * jnp.mean(mid_in * normed, axis=0, keepdims=True)
        )
        back = back + jnp.concatenate([slope_t[64 * i : 64 * i + 64] for i in group], axis=1)
        grad = project(mixing_parts, back)
        gated = []
        for k in range(SIDE):
            lanes = slice(SEQ * k, SEQ * k + SEQ)
            rows = slice(64 * (first + k), 64 * (first + k) + 64)
            mid[rows] = back[:, lanes]
            gated.append(grad[:, lanes] * gate[rows])
        high, low = split(jnp.concatenate(gated, axis=0))
        sums.append(dot_nt(ones, high) + dot_nt(ones, low))
    sums = [jnp.concatenate([part, part], axis=0) for part in sums]
    send_all(send, slice(0, 16), pack(own_blocks(jnp.concatenate(sums, axis=1))))
    send_all(send, slice(16, 16 + moments.shape[0]), moments[...])


def gate_back_kernel(mid, attended, gate, mixing_back, filter_weight, x0t, inverse, base):
    parts = lhs_parts(filter_weight[...])
    mixing_parts = lhs_parts(mixing_back[...])
    heads_t = attended[...].T
    for first in range(0, RES, SIDE):
        group = range(first, first + SIDE)
        above = jnp.concatenate([mid[64 * i : 64 * i + 64] for i in group], axis=1)
        gates = jnp.concatenate([gate[64 * i : 64 * i + 64] for i in group], axis=1)
        used = jnp.concatenate([gate[64 * i : 64 * i + 64] * heads_t[:, i : i + 1] for i in group], axis=1)
        grad = project(parts, project(mixing_parts, above) * used * (1.0 - gates))
        normed = jnp.concatenate([x0t[64 * i : 64 * i + 64] for i in group], axis=1)
        scale = jnp.concatenate([inverse[i : i + 1] for i in group], axis=1)
        total = above + scale * (
            grad - jnp.mean(grad, axis=0, keepdims=True) - normed * jnp.mean(grad * normed, axis=0, keepdims=True)
        )
        for k in range(SIDE):
            base[64 * (first + k) : 64 * (first + k) + 64] = total[:, SEQ * k : SEQ * k + SEQ]


def finish_kernel(
    got, attended, probs, keys, values, query_blocks, base, key_value, counts, asking, present, x0t, inverse, out, arrive
):
    att_grad = unpack(jnp.sum(got[:, 0:16, :], axis=0))
    moments = got[:, 16:, :].reshape(RES * 8, 128)
    rows, lanes = row_lane((RES * 8, 64))
    own_head = rows % 8 == lanes // 8
    along = jnp.sum(jnp.where(own_head, over_heads(att_grad * attended[...]), 0.0), axis=1, keepdims=True)
    r, c = row_lane((64, 64))
    spread = pick_nn(jnp.where(own_head, over_heads(att_grad), 0.0), (r % 8 == c // 8).astype(F32))
    both = jnp.concatenate([spread * moments[:, :64], -along * moments[:, 64:]], axis=1)
    r, c = row_lane((128, 64))
    query_grad = exact_nn(both, jnp.where((r < 72) & (r % 8 == c % 8), 1.0, 0.0))
    query_grad = sum_heads(jnp.where(own_head, query_grad, 0.0)) * HEAD_SIZE ** (-0.5)
    mean_grad = (exact_nt(query_grad, asking[...]) / counts[:, :64]).T

    blocks = head_blocks(att_grad)
    score_grad = probs[...] * (near_nn(blocks, values[...]) - along)
    key_grad = near_nn(query_blocks[...].T, score_grad)
    value_grad = near_nn(blocks.T, probs[...])
    parts = lhs_parts(key_value[...])
    arrive()
    for first in range(0, RES, SIDE):
        both = []
        for i in range(first, first + SIDE):
            rows = slice(8 * i, 8 * i + 8)
            both.append(jnp.concatenate([key_grad[rows], value_grad[rows]], axis=0))
        found = project(parts, jnp.concatenate(both, axis=1))
        done = []
        for k in range(SIDE):
            i = first + k
            rows = slice(64 * i, 64 * i + 64)
            grad = found[:, SEQ * k : SEQ * k + SEQ] + mean_grad[:, i : i + 1] * present[i : i + 1]
            normed = x0t[rows]
            back = inverse[i : i + 1] * (
                grad - jnp.mean(grad, axis=0, keepdims=True) - normed * jnp.mean(grad * normed, axis=0, keepdims=True)
            )
            done.append(base[rows] + back)
        for k in range(0, SIDE, 2):
            column = 64 * (first + k)
            out[:, column : column + 128] = jnp.concatenate(done[k : k + 2], axis=0).T


def whole(shape):
    return pl.BlockSpec(shape, lambda *_: (0,) * len(shape))


def staged(kernel, count, late, *refs):
    operands, rest = refs[: count[0]], refs[count[0] :]
    results, rest = rest[: count[1]], rest[count[1] :]
    total = count[0] + count[1]
    held, sems, scratch = rest[:total], rest[total], rest[total + 1 :]
    copies = [pltpu.make_async_copy(operands[k], held[k], sems.at[k]) for k in range(count[0])]
    for copy in copies:
        copy.start()

    def arrive():
        for k in late:
            copies[k].wait()

    for k in range(count[0]):
        if k not in late:
            copies[k].wait()
    kernel(*held, *scratch, *([arrive] if late else []))
    copies = [
        pltpu.make_async_copy(held[count[0] + k], results[k], sems.at[count[0] + k]) for k in range(count[1])
    ]
    for copy in copies:
        copy.start()
    for copy in copies:
        copy.wait()


def call(kernel, shapes, *operands, scratch=(), late=(), free=(), vmem=40):
    shapes = [jax.ShapeDtypeStruct(shape, F32) for shape in shapes]
    size = sum(4 * array.size for array in shapes) + sum(array.size * array.dtype.itemsize for array in operands)
    arrays = list(operands) + shapes
    return pl.pallas_call(
        functools.partial(staged, kernel, (len(operands), len(shapes)), late),
        in_specs=[
            pl.BlockSpec(memory_space=pl.ANY if k in free else pltpu.HBM) for k in range(len(operands))
        ],
        out_specs=[pl.BlockSpec(memory_space=pltpu.HBM)] * len(shapes),
        out_shape=[pltpu.HBM(array.shape, array.dtype) for array in shapes],
        scratch_shapes=[pltpu.VMEM(array.shape, array.dtype) for array in arrays]
        + [pltpu.SemaphoreType.DMA((len(arrays),))]
        + list(scratch),
        compiler_params=pltpu.CompilerParams(vmem_limit_bytes=vmem * 2**20),
        cost_estimate=pl.CostEstimate(flops=100_000_000, bytes_accessed=int(size), transcendentals=0),
        name=kernel.__name__,
    )(
        *[
            array if k in free else pltpu.with_memory_space_constraint(array, pltpu.HBM)
            for k, array in enumerate(operands)
        ]
    )


ROWS = 8
COST = 1000


def right_kernel(
    place, own_g, far_g, inverse_count, weight, left, left_far, high, low, out_0, out_1, out_2, out_3, weights, total
):
    step = pl.program_id(0)
    x = place[0]

    @pl.when(step == 0)
    def _():
        w_high, w_low = split(weight[...])
        weights[:, 0:128] = w_high
        weights[:, 128:256] = w_low
        weights[:, 256:384] = w_high
        total[...] = jnp.zeros_like(total)

    near = step < pl.num_programs(0) // 2
    for pair in range(ROWS // 2):
        blocks = []
        for row in (2 * pair, 2 * pair + 1):
            for d in range(4):
                chip = lax.rem(x + d, 4)
                blocks.append(jnp.where(near, own_g[row, chip, 0], far_g[row, chip, 0]))
        g_high, g_low = split(jnp.concatenate(blocks, axis=0))
        grads = dot_nt(weights[...], jnp.concatenate([g_high, g_high, g_low], axis=1))
        grads = grads * jnp.concatenate(
            [inverse_count[2 * pair : 2 * pair + 1], inverse_count[2 * pair + 1 : 2 * pair + 2]], axis=1
        )
        grads_high, grads_low = split(grads)
        for k in range(2):
            row = (2 * pair + k) * FACTOR_WIDTH
            rows, lanes = slice(row, row + FACTOR_WIDTH), slice(128 * k, 128 * k + 128)
            high[:, rows, :] = grads_high[:, lanes].reshape(FACTOR_WIDTH, FACTOR_WIDTH, 128)
            low[:, rows, :] = grads_low[:, lanes].reshape(FACTOR_WIDTH, FACTOR_WIDTH, 128)
    l_high, l_low = split(jnp.where(near, left[...], left_far[...]).T)
    block = slice(None)
    stacked = jnp.concatenate([l_high, l_low], axis=0)
    for f in range(0, FACTOR_WIDTH, 2):
        first = dot_nn(stacked, jnp.concatenate([high[f, block], high[f + 1, block]], axis=1))
        second = dot_nn(l_high, jnp.concatenate([low[f, block], low[f + 1, block]], axis=1))
        total[:, 128 * f : 128 * f + 256] += first[:128] + first[128:] + second

    @pl.when(step == pl.num_programs(0) - 1)
    def _():
        for f in range(FACTOR_WIDTH):
            block = total[:, 128 * f : 128 * f + 128].T
            for d, out in enumerate((out_0, out_1, out_2, out_3)):
                out[f] = block[32 * d : 32 * d + 32]


def right_products(place, pair_grad, far_grad, inverse_count, weight, left, left_far):
    block = ROWS * FACTOR_WIDTH
    steps = 64 // ROWS
    half = steps // 2
    grid_spec = pltpu.PrefetchScalarGridSpec(
        num_scalar_prefetch=1,
        grid=(steps,),
        in_specs=[
            pl.BlockSpec((ROWS, 4, 1, 32, 128), lambda t, s: (jnp.minimum(t, half - 1), 0, s[1], 0, 0)),
            pl.BlockSpec((ROWS, 4, 1, 32, 128), lambda t, s: (jnp.maximum(t - half, 0), 0, s[1], 0, 0)),
            pl.BlockSpec((ROWS, 128), lambda t, s: (t, 0)),
            pl.BlockSpec((1024, 128), lambda t, s: (0, 0)),
            pl.BlockSpec((block, 128), lambda t, s: (jnp.minimum(t, half - 1), 0)),
            pl.BlockSpec((block, 128), lambda t, s: (jnp.maximum(t - half, 0), 0)),
        ],
        out_specs=[
            pl.BlockSpec((FACTOR_WIDTH, block, 128), lambda t, s: (0, t, 0)),
            pl.BlockSpec((FACTOR_WIDTH, block, 128), lambda t, s: (0, t, 0)),
        ]
        + [whole((FACTOR_WIDTH, 32, 128))] * 4,
        scratch_shapes=[
            pltpu.VMEM((1024, 384), jnp.bfloat16),
            pltpu.VMEM((128, 4096), jnp.float32),
        ],
    )
    return pl.pallas_call(
        right_kernel,
        grid_spec=grid_spec,
        out_shape=[
            pltpu.HBM((FACTOR_WIDTH, 64 * FACTOR_WIDTH, 128), jnp.bfloat16),
            pltpu.HBM((FACTOR_WIDTH, 64 * FACTOR_WIDTH, 128), jnp.bfloat16),
        ]
        + [pltpu.HBM((FACTOR_WIDTH, 32, 128), jnp.float32)] * 4,
        compiler_params=pltpu.CompilerParams(vmem_limit_bytes=48 * 2**20),
        cost_estimate=pl.CostEstimate(flops=COST, bytes_accessed=COST, transcendentals=0),
        name="right_products",
    )(
        place,
        *[
            pltpu.with_memory_space_constraint(part, pltpu.HBM)
            for part in (pair_grad, far_grad, inverse_count, weight, left)
        ],
        left_far,
    )


def left_kernel(high, low, right_0, right_1, right_2, right_3, own, far_0, far_1, weights):
    step = pl.program_id(0)

    @pl.when(step == 0)
    def _():
        for f in range(FACTOR_WIDTH):
            for d, right in enumerate((right_0, right_1, right_2, right_3)):
                r_high, r_low = split(right[f])
                row = f * 128 + d * 32
                weights[row : row + 32, 0:128] = r_high
                weights[row : row + 32, 128:256] = r_low

    block = slice(None)
    first = jnp.zeros((ROWS * FACTOR_WIDTH, 256), jnp.float32)
    second = jnp.zeros((ROWS * FACTOR_WIDTH, 128), jnp.float32)
    for f in range(0, FACTOR_WIDTH, 2):
        part = slice(128 * f, 128 * f + 256)
        first += dot_nn(jnp.concatenate([high[f, block], high[f + 1, block]], axis=1), weights[part])
        second += dot_nn(jnp.concatenate([low[f, block], low[f + 1, block]], axis=1), weights[part, 0:128])
    found = first[:, :128] + first[:, 128:] + second
    half = pl.num_programs(0) // 2

    @pl.when(step < half // 2)
    def _():
        far_0[...] = found

    @pl.when((step >= half // 2) & (step < half))
    def _():
        far_1[...] = found

    @pl.when(step >= half)
    def _():
        own[...] = found


def left_products(high, low, rights):
    block = ROWS * FACTOR_WIDTH
    steps = 64 // ROWS
    half = steps // 2
    rows = pl.BlockSpec((FACTOR_WIDTH, block, 128), lambda t: (0, lax.rem(t + half, steps), 0))
    return pl.pallas_call(
        left_kernel,
        grid=(steps,),
        in_specs=[rows, rows] + [whole((FACTOR_WIDTH, 32, 128))] * 4,
        out_specs=[
            pl.BlockSpec((block, 128), lambda t: (jnp.maximum(t - half, 0), 0)),
            pl.BlockSpec((block, 128), lambda t: (jnp.minimum(t, half // 2 - 1), 0)),
            pl.BlockSpec((block, 128), lambda t: (jnp.clip(t - half // 2, 0, half // 2 - 1), 0)),
        ],
        out_shape=[pltpu.HBM((32 * FACTOR_WIDTH, 128), jnp.float32)]
        + [pltpu.HBM((16 * FACTOR_WIDTH, 128), jnp.float32)] * 2,
        scratch_shapes=[pltpu.VMEM((FACTOR_WIDTH * 128, 256), jnp.bfloat16)],
        compiler_params=pltpu.CompilerParams(vmem_limit_bytes=40 * 2**20),
        cost_estimate=pl.CostEstimate(flops=COST, bytes_accessed=COST, transcendentals=0),
        name="left_products",
    )(high, low, pltpu.with_memory_space_constraint(rights[0], pltpu.HBM), *rights[1:])


def swap_core(values):
    return lax.ppermute(values, "core", [(0, 1), (1, 0)])


def fetch_chip(values, distance):
    return lax.ppermute(values, "x", [((i + distance) % 4, i) for i in range(4)])


def send_chip(values, distance):
    return lax.ppermute(values, "x", [(i, (i + distance) % 4) for i in range(4)])


def exchange(send):
    return lax.all_to_all(send, "seq", 0, 0, tiled=True)


def body(
    homolog_features,
    homolog_loss_slope,
    pair_update_gradient,
    alignment_mask,
    asking_matrix,
    key_weight,
    content_matrix,
    sigmoid_filter_matrix,
    final_mixing_matrix,
    first_factor_matrix,
    second_factor_matrix,
    pair_weight,
):
    peers = lax.axis_size("seq")
    share = 64 // peers
    counted = -(-(17 + share) // 8) * 8
    block = RES * 8 // peers
    shared = 24 + block + (0 if share == 2 else share)
    x, core = lax.axis_index("x"), lax.axis_index("core")
    place = jnp.stack([x, core]).astype(jnp.int32)
    mask = alignment_mask.T
    mask_core = swap_core(mask)
    mask_chips = [fetch_chip(mask, d) for d in (1, 2, 3)]
    weight = pair_weight.reshape(FACTOR_WIDTH, FACTOR_WIDTH, 128).swapaxes(0, 1).reshape(1024, 128)
    value_gate = jnp.concatenate([content_matrix, sigmoid_filter_matrix], axis=1).T
    key_value = jnp.concatenate([key_weight, content_matrix], axis=1)
    factors = jnp.concatenate([first_factor_matrix, second_factor_matrix], axis=1)

    flat, heads, stat = (RES * 64, SEQ), (RES * 8, SEQ), (RES, SEQ)
    x0t, inverse, present, send = call(
        norm_kernel, [flat, stat, stat, (peers, counted, 128)], homolog_features, mask
    )
    (send,) = call(pair_kernel, [(peers, counted, 128)], send, mask, mask_core, *mask_chips, free=(2, 3, 4, 5))
    x0t, send, pair_grad = lax.optimization_barrier((x0t, send, pair_update_gradient))
    far_grad = swap_core(pair_grad).reshape(32, 4, 2, 32, 128)
    pair_grad = pair_grad.reshape(32, 4, 2, 32, 128)
    got = exchange(send)
    keys, values, gate, m0t, slope_t = call(
        project_kernel, [heads, heads, flat, flat, flat],
        x0t, homolog_features, homolog_loss_slope, key_weight.T, value_gate, free=(3, 4),
    )
    got, far_grad, weight, place = lax.optimization_barrier((got, far_grad, weight, place))
    raw, local, counts, query_blocks, send = call(
        score_kernel,
        [heads, (RES, 16), stat, (RES * 8, RES * 8), (peers, shared, 128)],
        got, keys, values, present, asking_matrix, free=(0,),
    )
    got = exchange(send)
    probs, attended, x1t, inverse_mid, left, right, inverse_count, moments = call(
        attend_kernel,
        [heads, (RES, 64), flat, stat, (RES * 32, SEQ), (FACTOR_WIDTH, RES, SEQ), (64, 128), (block, 128)],
        got, local, raw, m0t, gate, present, final_mixing_matrix.T, factors.T, late=(3, 4), free=(0, 6, 7),
        scratch=[pltpu.VMEM((RES * 32, SEQ), F32)],
    )
    rights = [right] + [fetch_chip(right, d) for d in (1, 2, 3)]
    high, low, right_own, right_1, right_2, right_3 = right_products(
        place, pair_grad, far_grad, inverse_count, weight, left, swap_core(left)
    )
    right_sent = [send_chip(part, d) for d, part in ((2, right_2), (1, right_1), (3, right_3))]
    left_own, *left_far = left_products(high, low, rights)
    left_far = [swap_core(part) for part in left_far]
    mid, send = call(
        middle_kernel, [flat, (peers, 16 + block, 128)],
        left_own, *left_far, right_own, *right_sent,
        moments, x1t, inverse_mid, present, slope_t, gate, factors, final_mixing_matrix, free=(1, 2, 4, 5, 6, 13),
        scratch=[pltpu.VMEM((RES * 32, SEQ), F32)],
    )
    got = exchange(send)
    (base,) = call(
        gate_back_kernel, [flat], mid, attended, gate, final_mixing_matrix, sigmoid_filter_matrix, x0t, inverse
    )
    (out,) = call(
        finish_kernel, [(SEQ, RES * 64)],
        got, attended, probs, keys, values, query_blocks, base, key_value, counts, asking_matrix,
        present, x0t, inverse, late=(6, 11), free=(0, 7),
    )
    return out


def solution(mesh):
    grid = Mesh(mesh.devices.reshape(mesh.devices.shape[0], 4, 2), ("seq", "x", "core"))
    res = ("x", "core")
    in_specs = (
        P("seq", res),
        P("seq", res),
        P(res, None, None),
        P("seq", res),
        P(),
        P(),
        P(),
        P(),
        P(),
        P(),
        P(),
        P(),
    )
    return jax.shard_map(body, mesh=grid, in_specs=in_specs, out_specs=P("seq", res), check_vma=False)
```

```python
import functools

import jax
import jax.numpy as jnp
from jax import lax
from jax.experimental import pallas as pl
from jax.experimental.pallas import tpu as pltpu
from jax.sharding import Mesh
from jax.sharding import PartitionSpec as P

FEATURE_DEPTH = 64
HEAD_COUNT = 8
HEAD_SIZE = 8
FACTOR_WIDTH = 32
RES = 32
SIDE = 4
SEQ = 128

EPSILON = 1e-05
MASK_FILL = -1000000000.0
PRECISE = lax.Precision.HIGHEST
F32 = jnp.float32


def split(values):
    high = values.astype(jnp.bfloat16)
    low = (values - high.astype(jnp.float32)).astype(jnp.bfloat16)
    return high, low


def dot_nn(a, b):
    return lax.dot_general(a, b, (((1,), (0,)), ((), ())), preferred_element_type=jnp.float32)


def dot_nt(a, b):
    return lax.dot_general(a, b, (((1,), (1,)), ((), ())), preferred_element_type=jnp.float32)


def exact_nn(a, b):
    return lax.dot_general(a, b, (((1,), (0,)), ((), ())), preferred_element_type=F32, precision=PRECISE)


def exact_nt(a, b):
    return lax.dot_general(a, b, (((1,), (1,)), ((), ())), preferred_element_type=F32, precision=PRECISE)


def near_nn(a, b):
    a_high, a_low = split(a)
    b_high, b_low = split(b)
    return dot_nn(a_high, b_high) + (dot_nn(a_high, b_low) + dot_nn(a_low, b_high))


def near_nt(a, b):
    a_high, a_low = split(a)
    b_high, b_low = split(b)
    return dot_nt(
        jnp.concatenate([a_high, a_high, a_low], axis=1), jnp.concatenate([b_high, b_low, b_high], axis=1)
    )


def pick_nn(values, ones):
    high, low = split(values)
    rest = values - high.astype(F32) - low.astype(F32)
    ones = ones.astype(jnp.bfloat16)
    return dot_nn(high, ones) + (dot_nn(low, ones) + dot_nn(rest.astype(jnp.bfloat16), ones))


def lhs_parts(weight):
    high, low = split(weight)
    return jnp.concatenate([high, high, low], axis=1)


def project(parts, values):
    high, low = split(values)
    return dot_nn(parts, jnp.concatenate([high, low, high], axis=0))


def row_lane(shape):
    return lax.broadcasted_iota(jnp.int32, shape, 0), lax.broadcasted_iota(jnp.int32, shape, 1)


def sum_lanes_01(ones, values):
    high, rest = values.astype(jnp.bfloat16), values
    rest = rest - high.astype(F32)
    mid = rest.astype(jnp.bfloat16)
    low = (rest - mid.astype(F32)).astype(jnp.bfloat16)
    return dot_nt(ones, high) + dot_nt(ones, mid) + dot_nt(ones, low)


def own_blocks(values):
    rows, _ = row_lane((RES, 128))
    total = jnp.zeros((RES, 128), F32)
    for pair in range(RES // 2):
        total = jnp.where(rows // 2 == pair, values[:, 128 * pair : 128 * pair + 128], total)
    return jnp.where(rows[:, :64] % 2 == 0, total[:, :64], total[:, 64:])


def pack(values):
    return jnp.concatenate([values[:16], values[16:]], axis=1)


def unpack(values):
    return jnp.concatenate([values[:, :64], values[:, 64:]], axis=0)


def over_heads(values):
    return jnp.broadcast_to(values[:, None, :], (RES, 8, values.shape[1])).reshape(RES * 8, values.shape[1])


def head_column(values):
    rows, lanes = row_lane((RES * 8, values.shape[1]))
    return jnp.sum(jnp.where(rows % 8 == lanes, over_heads(values), 0.0), axis=1, keepdims=True)


def head_blocks(values):
    rows, lanes = row_lane((RES * 8, 64))
    picked = jnp.where(rows % 8 == lanes // 8, over_heads(values), 0.0)
    r, c = row_lane((64, RES * 8))
    spread = pick_nn(picked, (r % 8 == c % 8).astype(F32))
    rows, lanes = row_lane((RES * 8, RES * 8))
    return jnp.where(rows // 8 == lanes // 8, spread, 0.0)


def fold_blocks(values):
    rows, lanes = row_lane((RES * 8, RES * 8))
    r, c = row_lane((RES * 8, 128))
    fold = jnp.where((r % 8 == c % 8) & (c < 64), 1.0, 0.0)
    return pick_nn(jnp.where(rows // 8 == lanes // 8, values, 0.0), fold)


def sum_heads(values):
    return jnp.sum(values.reshape(RES, 8, values.shape[1]), axis=1)


def send_all(send, rows, values):
    send[:, rows, :] = jnp.broadcast_to(values[None], (send.shape[0],) + values.shape)


def norm_kernel(m0, mask, x0t, inverse, present, send):
    shown = mask[...].astype(F32)
    present[...] = shown
    for pair in range(RES // 2):
        block = m0[:, 128 * pair : 128 * pair + 128].T
        for k in range(2):
            part = block[64 * k : 64 * k + 64]
            center = part - jnp.mean(part, axis=0, keepdims=True)
            scale = lax.rsqrt(jnp.mean(center * center, axis=0, keepdims=True) + EPSILON)
            row = 2 * pair + k
            inverse[row : row + 1] = scale
            x0t[64 * row : 64 * row + 64] = center * scale
    ones = shown.astype(jnp.bfloat16)
    sums = own_blocks(sum_lanes_01(ones, x0t[...]))
    counts = dot_nt(jnp.ones((16, SEQ), jnp.bfloat16), ones)
    send[...] = jnp.zeros_like(send)
    send_all(send, slice(0, 16), pack(sums))
    send_all(send, slice(16, 17), jnp.concatenate([counts[0:1], jnp.zeros((1, 96), F32)], axis=1))


def pair_kernel(sent, mask, mask_core, mask_1, mask_2, mask_3, send):
    send[...] = sent[...]
    own = mask[...].astype(F32).astype(jnp.bfloat16)
    rows = jnp.concatenate([own, mask_core[...].astype(F32).astype(jnp.bfloat16)], axis=0)
    columns = jnp.concatenate(
        [own] + [part[...].astype(F32).astype(jnp.bfloat16) for part in (mask_1, mask_2, mask_3)], axis=0
    )
    count = dot_nt(rows, columns)
    share = 64 // send.shape[0]
    for peer in range(send.shape[0]):
        send[peer, 17 : 17 + share, :] = count[share * peer : share * peer + share]


def project_kernel(x0t, m0, slope, key, value_gate, keys, values, gate, m0t, slope_t):
    parts = lhs_parts(value_gate[...])
    for pair in range(RES // 2):
        block = slice(128 * pair, 128 * pair + 128)
        m0t[block] = m0[:, block].T
        slope_t[block] = slope[:, block].T
    for first in range(0, RES, SIDE):
        both = jnp.concatenate([x0t[64 * i : 64 * i + 64] for i in range(first, first + SIDE)], axis=1)
        found = project(parts, both)
        key_rows = exact_nn(key[...], both)
        gates = jax.nn.sigmoid(found[8:72])
        for k in range(SIDE):
            i = first + k
            lanes = slice(SEQ * k, SEQ * k + SEQ)
            keys[8 * i : 8 * i + 8] = key_rows[:, lanes]
            values[8 * i : 8 * i + 8] = found[0:8, lanes]
            gate[64 * i : 64 * i + 64] = gates[:, lanes]


def score_kernel(got, keys, values, present, asking, weights, local, counts, query_blocks, send):
    sums = jnp.sum(got[...], axis=0)
    r, c = row_lane((RES, RES))
    count = jnp.sum(jnp.where(r == c, jnp.broadcast_to(sums[16:17, :RES], (RES, RES)), 0.0), axis=1, keepdims=True)
    counts[...] = jnp.broadcast_to(count, (RES, 128))
    queries = exact_nn(unpack(sums[:16]) / count, asking[...]) * HEAD_SIZE ** (-0.5)
    blocks = head_blocks(queries)
    query_blocks[...] = blocks
    scores = exact_nn(blocks, keys[...])
    scores = jnp.where(over_heads(present[...]) > 0, scores, MASK_FILL)
    top = jnp.max(scores, axis=1, keepdims=True)
    raw = jnp.exp(scores - top)
    weights[...] = raw
    total = jnp.sum(raw, axis=1, keepdims=True)
    rows, lanes = row_lane((RES * 8, 64))
    own_head = rows % 8 == lanes // 8
    weighted = sum_heads(jnp.where(own_head, fold_blocks(near_nt(raw, values[...]))[:, :64], 0.0))
    send_all(send, slice(0, 16), pack(weighted))
    rows, lanes = row_lane((RES * 8, 16))
    stats = jnp.where(lanes == rows % 8, top, jnp.where(lanes == 8 + rows % 8, total, 0.0))
    stats = sum_heads(stats)
    local[...] = stats
    share = 64 // send.shape[0]
    pairs = sums[17 : 17 + share]
    stats = jnp.concatenate([stats[8 * k : 8 * k + 8] for k in range(4)], axis=1)
    if share == 2:
        right = jnp.concatenate([pairs[:, :64], pairs[:, 64:], jnp.zeros((4, 64), F32)], axis=0)
    else:
        right = jnp.zeros((8, 64), F32)
        send_all(send, slice(send.shape[1] - share, send.shape[1]), pairs)
    send_all(send, slice(16, 24), jnp.concatenate([stats, right], axis=1))
    products = raw.reshape(RES, 8, 1, SEQ) * values[...].reshape(RES, 1, 8, SEQ)
    products = products.reshape(RES * 64, SEQ)
    half = RES // 2
    rows, lanes = row_lane((half * 64, 128))
    same = rows // 64 == lanes // 8
    r, c = row_lane((128, 64))
    fold = jnp.where(r % 8 == c % 8, 1.0, 0.0).astype(jnp.bfloat16)
    moments = []
    for k in range(2):
        a_high, a_low = split(products[half * 64 * k : half * 64 * (k + 1)])
        b_high, b_low = split(keys[128 * k : 128 * k + 128])
        found = dot_nt(
            jnp.concatenate([a_high, a_high, a_low], axis=1), jnp.concatenate([b_high, b_low, b_high], axis=1)
        )
        f_high, f_low = split(jnp.where(same, found, 0.0))
        spread = dot_nn(f_high, fold) + dot_nn(f_low, fold)
        spread = jnp.where(rows[:, :64] % 8 == lanes[:, :64] // 8, spread, 0.0)
        moments.append(jnp.sum(spread.reshape(half * 8, 8, 64), axis=1))
    moments = jnp.concatenate(moments, axis=0)
    firsts = fold_blocks(near_nt(raw, keys[...]))
    rows, lanes = row_lane((RES * 8, 64))
    rest = jnp.where(lanes < 8, firsts[:, :64], jnp.where(lanes == 8, top, jnp.where(lanes == 9, total, 0.0)))
    block = jnp.concatenate([moments, rest], axis=1)
    size = RES * 8 // send.shape[0]
    send[:, 24 : 24 + size, :] = block.reshape(send.shape[0], size, 128)


def attend_kernel(
    got, local, raw, m0t, gate, present, mixing, factors,
    probs, attended, x1t, inverse_mid, left, right, inverse_count, moments, scratch, arrive,
):
    peers = got.shape[0]
    share = 64 // peers
    for peer in range(peers):
        if share == 2:
            pairs = jnp.concatenate([got[peer, 16:18, 64:], got[peer, 18:20, 64:]], axis=1)
        else:
            pairs = got[peer, got.shape[1] - share :, :]
        inverse_count[share * peer : share * peer + share] = 1.0 / pairs
    weighted = jnp.concatenate([got[:, 0:16, 0:64], got[:, 0:16, 64:128]], axis=1)
    stats = jnp.concatenate([got[:, 16:24, 16 * k : 16 * k + 16] for k in range(4)], axis=1)
    tops = stats[:, :, 0:8]
    top = jnp.max(tops, axis=0)
    factor = jnp.exp(tops - top[None])
    total = jnp.sum(factor * stats[:, :, 8:16], axis=0)
    r, c = row_lane((8, 64))
    expand = jnp.where(r == c // 8, 1.0, 0.0)
    high, low = split(factor.reshape(peers * RES, 8))
    wide = expand.astype(jnp.bfloat16)
    factor = (dot_nn(high, wide) + dot_nn(low, wide)).reshape(peers, RES, 64)
    heads = jnp.sum(factor * weighted, axis=0) / exact_nn(total, expand)
    probs[...] = raw[...] * head_column(jnp.exp(local[:, 0:8] - top) / total)
    attended[...] = heads
    size = RES * 8 // peers
    block = got[:, 24 : 24 + size, :]
    tops = block[:, :, 72:73]
    block = jnp.sum(jnp.exp(tops - jnp.max(tops, axis=0)[None]) * block, axis=0)
    lanes = lax.broadcasted_iota(jnp.int32, block.shape, 1)
    moments[...] = jnp.where(lanes < 72, block / block[:, 73:74], 0.0)
    heads_t = heads.T
    mixing_parts = lhs_parts(mixing[...])
    factor_parts = lhs_parts(factors[...])
    arrive()
    for first in range(0, RES, 2):
        shown, used, base = [], [], []
        for k in range(2):
            i = first + k
            rows = slice(64 * i, 64 * i + 64)
            use = gate[rows] * heads_t[:, i : i + 1]
            used.append(use)
            base.append(m0t[rows])
            shown.append(present[i : i + 1])
        middle = jnp.concatenate(base, axis=1) + project(mixing_parts, jnp.concatenate(used, axis=1))
        center = middle - jnp.mean(middle, axis=0, keepdims=True)
        scale = lax.rsqrt(jnp.mean(center * center, axis=0, keepdims=True) + EPSILON)
        normed = center * scale
        found = project(factor_parts, normed) * jnp.concatenate(shown, axis=1)
        for k in range(2):
            i = first + k
            lanes = slice(SEQ * k, SEQ * k + SEQ)
            x1t[64 * i : 64 * i + 64] = normed[:, lanes]
            inverse_mid[i : i + 1] = scale[:, lanes]
            left[32 * i : 32 * i + 32] = found[:32, lanes]
            scratch[32 * i : 32 * i + 32] = found[32:, lanes]
    for f in range(FACTOR_WIDTH):
        right[f] = scratch[pl.ds(f, RES, stride=FACTOR_WIDTH), :]


def middle_kernel(
    left_own, left_far_0, left_far_1, right_own, right_1, right_2, right_3, moments, x1t, inverse_mid, present, slope_t, gate,
    factors_back, mixing_back, mid, send, scratch,
):
    for f in range(FACTOR_WIDTH):
        scratch[32 * f : 32 * f + 32] = (right_own[f] + right_1[f]) + (right_2[f] + right_3[f])
    parts = lhs_parts(factors_back[...])
    mixing_parts = lhs_parts(mixing_back[...])
    ones = jnp.ones((16, SEQ), jnp.bfloat16)
    sums = []
    for first in range(0, RES, SIDE):
        grads = []
        for k in range(SIDE):
            i = first + k
            rows = slice(32 * i, 32 * i + 32)
            left_far = left_far_0 if i < RES // 2 else left_far_1
            near = slice(32 * (i % 16), 32 * (i % 16) + 32)
            both = jnp.concatenate(
                [left_own[rows] + left_far[near], scratch[pl.ds(i, FACTOR_WIDTH, stride=RES), :]], axis=0
            )
            grads.append(both * present[i : i + 1])
        mid_in = project(parts, jnp.concatenate(grads, axis=1))
        group = range(first, first + SIDE)
        normed = jnp.concatenate([x1t[64 * i : 64 * i + 64] for i in group], axis=1)
        scale = jnp.concatenate([inverse_mid[i : i + 1] for i in group], axis=1)
        back = scale * (
            mid_in
            - jnp.mean(mid_in, axis=0, keepdims=True)
            - normed * jnp.mean(mid_in * normed, axis=0, keepdims=True)
        )
        back = back + jnp.concatenate([slope_t[64 * i : 64 * i + 64] for i in group], axis=1)
        grad = project(mixing_parts, back)
        gated = []
        for k in range(SIDE):
            lanes = slice(SEQ * k, SEQ * k + SEQ)
            rows = slice(64 * (first + k), 64 * (first + k) + 64)
            mid[rows] = back[:, lanes]
            gated.append(grad[:, lanes] * gate[rows])
        high, low = split(jnp.concatenate(gated, axis=0))
        sums.append(dot_nt(ones, high) + dot_nt(ones, low))
    sums = [jnp.concatenate([part, part], axis=0) for part in sums]
    send_all(send, slice(0, 16), pack(own_blocks(jnp.concatenate(sums, axis=1))))
    send_all(send, slice(16, 16 + moments.shape[0]), moments[...])


def gate_back_kernel(mid, attended, gate, mixing_back, filter_weight, x0t, inverse, query_blocks, base, query_turned):
    parts = lhs_parts(filter_weight[...])
    mixing_parts = lhs_parts(mixing_back[...])
    heads_t = attended[...].T
    query_turned[...] = query_blocks[...].T
    for first in range(0, RES, SIDE):
        group = range(first, first + SIDE)
        above = jnp.concatenate([mid[64 * i : 64 * i + 64] for i in group], axis=1)
        gates = jnp.concatenate([gate[64 * i : 64 * i + 64] for i in group], axis=1)
        used = jnp.concatenate([gate[64 * i : 64 * i + 64] * heads_t[:, i : i + 1] for i in group], axis=1)
        grad = project(parts, project(mixing_parts, above) * used * (1.0 - gates))
        normed = jnp.concatenate([x0t[64 * i : 64 * i + 64] for i in group], axis=1)
        scale = jnp.concatenate([inverse[i : i + 1] for i in group], axis=1)
        total = above + scale * (
            grad - jnp.mean(grad, axis=0, keepdims=True) - normed * jnp.mean(grad * normed, axis=0, keepdims=True)
        )
        for k in range(SIDE):
            base[64 * (first + k) : 64 * (first + k) + 64] = total[:, SEQ * k : SEQ * k + SEQ]


def finish_kernel(
    got, attended, probs, values, query_turned, base, key_value, counts, asking, present, x0t, inverse, out, arrive
):
    att_grad = unpack(jnp.sum(got[:, 0:16, :], axis=0))
    moments = got[:, 16:, :].reshape(RES * 8, 128)
    rows, lanes = row_lane((RES * 8, 64))
    own_head = rows % 8 == lanes // 8
    along = jnp.sum(jnp.where(own_head, over_heads(att_grad * attended[...]), 0.0), axis=1, keepdims=True)
    r, c = row_lane((64, 64))
    spread = pick_nn(jnp.where(own_head, over_heads(att_grad), 0.0), (r % 8 == c // 8).astype(F32))
    both = jnp.concatenate([spread * moments[:, :64], -along * moments[:, 64:]], axis=1)
    r, c = row_lane((128, 64))
    query_grad = exact_nn(both, jnp.where((r < 72) & (r % 8 == c % 8), 1.0, 0.0))
    query_grad = sum_heads(jnp.where(own_head, query_grad, 0.0)) * HEAD_SIZE ** (-0.5)
    mean_grad = (exact_nt(query_grad, asking[...]) / counts[:, :64]).T

    blocks = head_blocks(att_grad)
    score_grad = probs[...] * (near_nn(blocks, values[...]) - along)
    key_grad = near_nn(query_turned[...], score_grad)
    value_grad = near_nn(blocks.T, probs[...])
    parts = lhs_parts(key_value[...])
    arrive()
    for first in range(0, RES, SIDE):
        both = []
        for i in range(first, first + SIDE):
            rows = slice(8 * i, 8 * i + 8)
            both.append(jnp.concatenate([key_grad[rows], value_grad[rows]], axis=0))
        found = project(parts, jnp.concatenate(both, axis=1))
        done = []
        for k in range(SIDE):
            i = first + k
            rows = slice(64 * i, 64 * i + 64)
            grad = found[:, SEQ * k : SEQ * k + SEQ] + mean_grad[:, i : i + 1] * present[i : i + 1]
            normed = x0t[rows]
            back = inverse[i : i + 1] * (
                grad - jnp.mean(grad, axis=0, keepdims=True) - normed * jnp.mean(grad * normed, axis=0, keepdims=True)
            )
            done.append(base[rows] + back)
        for k in range(0, SIDE, 2):
            column = 64 * (first + k)
            out[:, column : column + 128] = jnp.concatenate(done[k : k + 2], axis=0).T


def whole(shape):
    return pl.BlockSpec(shape, lambda *_: (0,) * len(shape))


def staged(kernel, count, late, *refs):
    operands, rest = refs[: count[0]], refs[count[0] :]
    results, rest = rest[: count[1]], rest[count[1] :]
    total = count[0] + count[1]
    held, sems, scratch = rest[:total], rest[total], rest[total + 1 :]
    copies = [pltpu.make_async_copy(operands[k], held[k], sems.at[k]) for k in range(count[0])]
    for copy in copies:
        copy.start()

    def arrive():
        for k in late:
            copies[k].wait()

    for k in range(count[0]):
        if k not in late:
            copies[k].wait()
    kernel(*held, *scratch, *([arrive] if late else []))
    copies = [
        pltpu.make_async_copy(held[count[0] + k], results[k], sems.at[count[0] + k]) for k in range(count[1])
    ]
    for copy in copies:
        copy.start()
    for copy in copies:
        copy.wait()


def call(kernel, shapes, *operands, scratch=(), late=(), free=(), vmem=40):
    shapes = [jax.ShapeDtypeStruct(shape, F32) for shape in shapes]
    size = sum(4 * array.size for array in shapes) + sum(array.size * array.dtype.itemsize for array in operands)
    arrays = list(operands) + shapes
    return pl.pallas_call(
        functools.partial(staged, kernel, (len(operands), len(shapes)), late),
        in_specs=[
            pl.BlockSpec(memory_space=pl.ANY if k in free else pltpu.HBM) for k in range(len(operands))
        ],
        out_specs=[pl.BlockSpec(memory_space=pltpu.HBM)] * len(shapes),
        out_shape=[pltpu.HBM(array.shape, array.dtype) for array in shapes],
        scratch_shapes=[pltpu.VMEM(array.shape, array.dtype) for array in arrays]
        + [pltpu.SemaphoreType.DMA((len(arrays),))]
        + list(scratch),
        compiler_params=pltpu.CompilerParams(vmem_limit_bytes=vmem * 2**20),
        cost_estimate=pl.CostEstimate(flops=100_000_000, bytes_accessed=int(size), transcendentals=0),
        name=kernel.__name__,
    )(
        *[
            array if k in free else pltpu.with_memory_space_constraint(array, pltpu.HBM)
            for k, array in enumerate(operands)
        ]
    )


ROWS = 8
COST = 1000


def right_kernel(
    place, own_g, far_g, inverse_count, weight, left, left_far, high, low, out_0, out_1, out_2, out_3, weights, total
):
    step = pl.program_id(0)
    x = place[0]

    @pl.when(step == 0)
    def _():
        w_high, w_low = split(weight[...])
        weights[:, 0:128] = w_high
        weights[:, 128:256] = w_low
        weights[:, 256:384] = w_high
        total[...] = jnp.zeros_like(total)

    near = step < pl.num_programs(0) // 2
    for pair in range(ROWS // 2):
        blocks = []
        for row in (2 * pair, 2 * pair + 1):
            for d in range(4):
                chip = lax.rem(x + d, 4)
                blocks.append(jnp.where(near, own_g[row, chip, 0], far_g[row, chip, 0]))
        g_high, g_low = split(jnp.concatenate(blocks, axis=0))
        grads = dot_nt(weights[...], jnp.concatenate([g_high, g_high, g_low], axis=1))
        grads = grads * jnp.concatenate(
            [inverse_count[2 * pair : 2 * pair + 1], inverse_count[2 * pair + 1 : 2 * pair + 2]], axis=1
        )
        grads_high, grads_low = split(grads)
        for k in range(2):
            row = (2 * pair + k) * FACTOR_WIDTH
            rows, lanes = slice(row, row + FACTOR_WIDTH), slice(128 * k, 128 * k + 128)
            high[:, rows, :] = grads_high[:, lanes].reshape(FACTOR_WIDTH, FACTOR_WIDTH, 128)
            low[:, rows, :] = grads_low[:, lanes].reshape(FACTOR_WIDTH, FACTOR_WIDTH, 128)
    l_high, l_low = split(jnp.where(near, left[...], left_far[...]).T)
    block = slice(None)
    stacked = jnp.concatenate([l_high, l_low], axis=0)
    for f in range(0, FACTOR_WIDTH, 2):
        first = dot_nn(stacked, jnp.concatenate([high[f, block], high[f + 1, block]], axis=1))
        second = dot_nn(l_high, jnp.concatenate([low[f, block], low[f + 1, block]], axis=1))
        total[:, 128 * f : 128 * f + 256] += first[:128] + first[128:] + second

    @pl.when(step == pl.num_programs(0) - 1)
    def _():
        for f in range(FACTOR_WIDTH):
            block = total[:, 128 * f : 128 * f + 128].T
            for d, out in enumerate((out_0, out_1, out_2, out_3)):
                out[f] = block[32 * d : 32 * d + 32]


def right_products(place, pair_grad, far_grad, inverse_count, weight, left, left_far):
    block = ROWS * FACTOR_WIDTH
    steps = 64 // ROWS
    half = steps // 2
    grid_spec = pltpu.PrefetchScalarGridSpec(
        num_scalar_prefetch=1,
        grid=(steps,),
        in_specs=[
            pl.BlockSpec((ROWS, 4, 1, 32, 128), lambda t, s: (jnp.minimum(t, half - 1), 0, s[1], 0, 0)),
            pl.BlockSpec((ROWS, 4, 1, 32, 128), lambda t, s: (jnp.maximum(t - half, 0), 0, s[1], 0, 0)),
            pl.BlockSpec((ROWS, 128), lambda t, s: (t, 0)),
            pl.BlockSpec((1024, 128), lambda t, s: (0, 0)),
            pl.BlockSpec((block, 128), lambda t, s: (jnp.minimum(t, half - 1), 0)),
            pl.BlockSpec((block, 128), lambda t, s: (jnp.maximum(t - half, 0), 0)),
        ],
        out_specs=[
            pl.BlockSpec((FACTOR_WIDTH, block, 128), lambda t, s: (0, t, 0)),
            pl.BlockSpec((FACTOR_WIDTH, block, 128), lambda t, s: (0, t, 0)),
        ]
        + [whole((FACTOR_WIDTH, 32, 128))] * 4,
        scratch_shapes=[
            pltpu.VMEM((1024, 384), jnp.bfloat16),
            pltpu.VMEM((128, 4096), jnp.float32),
        ],
    )
    return pl.pallas_call(
        right_kernel,
        grid_spec=grid_spec,
        out_shape=[
            pltpu.HBM((FACTOR_WIDTH, 64 * FACTOR_WIDTH, 128), jnp.bfloat16),
            pltpu.HBM((FACTOR_WIDTH, 64 * FACTOR_WIDTH, 128), jnp.bfloat16),
        ]
        + [pltpu.HBM((FACTOR_WIDTH, 32, 128), jnp.float32)] * 4,
        compiler_params=pltpu.CompilerParams(vmem_limit_bytes=48 * 2**20),
        cost_estimate=pl.CostEstimate(flops=COST, bytes_accessed=COST, transcendentals=0),
        name="right_products",
    )(
        place,
        *[
            pltpu.with_memory_space_constraint(part, pltpu.HBM)
            for part in (pair_grad, far_grad, inverse_count, weight, left)
        ],
        left_far,
    )


def left_kernel(high, low, right_0, right_1, right_2, right_3, own, far_0, far_1, weights):
    step = pl.program_id(0)

    @pl.when(step == 0)
    def _():
        for f in range(FACTOR_WIDTH):
            for d, right in enumerate((right_0, right_1, right_2, right_3)):
                r_high, r_low = split(right[f])
                row = f * 128 + d * 32
                weights[row : row + 32, 0:128] = r_high
                weights[row : row + 32, 128:256] = r_low

    block = slice(None)
    first = jnp.zeros((ROWS * FACTOR_WIDTH, 256), jnp.float32)
    second = jnp.zeros((ROWS * FACTOR_WIDTH, 128), jnp.float32)
    for f in range(0, FACTOR_WIDTH, 2):
        part = slice(128 * f, 128 * f + 256)
        first += dot_nn(jnp.concatenate([high[f, block], high[f + 1, block]], axis=1), weights[part])
        second += dot_nn(jnp.concatenate([low[f, block], low[f + 1, block]], axis=1), weights[part, 0:128])
    found = first[:, :128] + first[:, 128:] + second
    half = pl.num_programs(0) // 2

    @pl.when(step < half // 2)
    def _():
        far_0[...] = found

    @pl.when((step >= half // 2) & (step < half))
    def _():
        far_1[...] = found

    @pl.when(step >= half)
    def _():
        own[...] = found


def left_products(high, low, rights):
    block = ROWS * FACTOR_WIDTH
    steps = 64 // ROWS
    half = steps // 2
    rows = pl.BlockSpec((FACTOR_WIDTH, block, 128), lambda t: (0, lax.rem(t + half, steps), 0))
    return pl.pallas_call(
        left_kernel,
        grid=(steps,),
        in_specs=[rows, rows] + [whole((FACTOR_WIDTH, 32, 128))] * 4,
        out_specs=[
            pl.BlockSpec((block, 128), lambda t: (jnp.maximum(t - half, 0), 0)),
            pl.BlockSpec((block, 128), lambda t: (jnp.minimum(t, half // 2 - 1), 0)),
            pl.BlockSpec((block, 128), lambda t: (jnp.clip(t - half // 2, 0, half // 2 - 1), 0)),
        ],
        out_shape=[pltpu.HBM((32 * FACTOR_WIDTH, 128), jnp.float32)]
        + [pltpu.HBM((16 * FACTOR_WIDTH, 128), jnp.float32)] * 2,
        scratch_shapes=[pltpu.VMEM((FACTOR_WIDTH * 128, 256), jnp.bfloat16)],
        compiler_params=pltpu.CompilerParams(vmem_limit_bytes=40 * 2**20),
        cost_estimate=pl.CostEstimate(flops=COST, bytes_accessed=COST, transcendentals=0),
        name="left_products",
    )(high, low, pltpu.with_memory_space_constraint(rights[0], pltpu.HBM), *rights[1:])


def swap_core(values):
    return lax.ppermute(values, "core", [(0, 1), (1, 0)])


def fetch_chip(values, distance):
    return lax.ppermute(values, "x", [((i + distance) % 4, i) for i in range(4)])


def send_chip(values, distance):
    return lax.ppermute(values, "x", [(i, (i + distance) % 4) for i in range(4)])


def exchange(send):
    return lax.all_to_all(send, "seq", 0, 0, tiled=True)


def body(
    homolog_features,
    homolog_loss_slope,
    pair_update_gradient,
    alignment_mask,
    asking_matrix,
    key_weight,
    content_matrix,
    sigmoid_filter_matrix,
    final_mixing_matrix,
    first_factor_matrix,
    second_factor_matrix,
    pair_weight,
):
    peers = lax.axis_size("seq")
    share = 64 // peers
    counted = -(-(17 + share) // 8) * 8
    block = RES * 8 // peers
    shared = 24 + block + (0 if share == 2 else share)
    x, core = lax.axis_index("x"), lax.axis_index("core")
    place = jnp.stack([x, core]).astype(jnp.int32)
    mask = alignment_mask.T
    mask_core = swap_core(mask)
    mask_chips = [fetch_chip(mask, d) for d in (1, 2, 3)]
    weight = pair_weight.reshape(FACTOR_WIDTH, FACTOR_WIDTH, 128).swapaxes(0, 1).reshape(1024, 128)
    value_gate = jnp.concatenate([content_matrix, sigmoid_filter_matrix], axis=1).T
    key_value = jnp.concatenate([key_weight, content_matrix], axis=1)
    factors = jnp.concatenate([first_factor_matrix, second_factor_matrix], axis=1)

    flat, heads, stat = (RES * 64, SEQ), (RES * 8, SEQ), (RES, SEQ)
    x0t, inverse, present, send = call(
        norm_kernel, [flat, stat, stat, (peers, counted, 128)], homolog_features, mask
    )
    (send,) = call(pair_kernel, [(peers, counted, 128)], send, mask, mask_core, *mask_chips, free=(2, 3, 4, 5))
    x0t, send, pair_grad = lax.optimization_barrier((x0t, send, pair_update_gradient))
    far_grad = swap_core(pair_grad).reshape(32, 4, 2, 32, 128)
    pair_grad = pair_grad.reshape(32, 4, 2, 32, 128)
    got = exchange(send)
    keys, values, gate, m0t, slope_t = call(
        project_kernel, [heads, heads, flat, flat, flat],
        x0t, homolog_features, homolog_loss_slope, key_weight.T, value_gate, free=(3, 4),
    )
    got, far_grad, weight, place = lax.optimization_barrier((got, far_grad, weight, place))
    raw, local, counts, query_blocks, send = call(
        score_kernel,
        [heads, (RES, 16), stat, (RES * 8, RES * 8), (peers, shared, 128)],
        got, keys, values, present, asking_matrix, free=(0,),
    )
    got = exchange(send)
    probs, attended, x1t, inverse_mid, left, right, inverse_count, moments = call(
        attend_kernel,
        [heads, (RES, 64), flat, stat, (RES * 32, SEQ), (FACTOR_WIDTH, RES, SEQ), (64, 128), (block, 128)],
        got, local, raw, m0t, gate, present, final_mixing_matrix.T, factors.T, late=(3, 4), free=(0, 6, 7),
        scratch=[pltpu.VMEM((RES * 32, SEQ), F32)],
    )
    rights = [right] + [fetch_chip(right, d) for d in (1, 2, 3)]
    high, low, right_own, right_1, right_2, right_3 = right_products(
        place, pair_grad, far_grad, inverse_count, weight, left, swap_core(left)
    )
    right_sent = [send_chip(part, d) for d, part in ((2, right_2), (1, right_1), (3, right_3))]
    left_own, *left_far = left_products(high, low, rights)
    left_far = [swap_core(part) for part in left_far]
    mid, send = call(
        middle_kernel, [flat, (peers, 16 + block, 128)],
        left_own, *left_far, right_own, *right_sent,
        moments, x1t, inverse_mid, present, slope_t, gate, factors, final_mixing_matrix, free=(1, 2, 4, 5, 6, 13),
        scratch=[pltpu.VMEM((RES * 32, SEQ), F32)],
    )
    got = exchange(send)
    base, query_turned = call(
        gate_back_kernel, [flat, (RES * 8, RES * 8)],
        mid, attended, gate, final_mixing_matrix, sigmoid_filter_matrix, x0t, inverse, query_blocks,
    )
    (out,) = call(
        finish_kernel, [(SEQ, RES * 64)],
        got, attended, probs, values, query_turned, base, key_value, counts, asking_matrix,
        present, x0t, inverse, late=(5, 10), free=(0, 6),
    )
    return out


def solution(mesh):
    grid = Mesh(mesh.devices.reshape(mesh.devices.shape[0], 4, 2), ("seq", "x", "core"))
    res = ("x", "core")
    in_specs = (
        P("seq", res),
        P("seq", res),
        P(res, None, None),
        P("seq", res),
        P(),
        P(),
        P(),
        P(),
        P(),
        P(),
        P(),
        P(),
    )
    return jax.shard_map(body, mesh=grid, in_specs=in_specs, out_specs=P("seq", res), check_vma=False)
```
